32 devices in a mesh: fsdp: 16 (over z, y, core), blk: 2 (over x).
Axes of the slice: x: 2, y: 2, z: 4, core: 2. Of those that a mesh axis runs over, the one named last changes fastest.
Arguments:
- x_resp: bfloat16 [16, 256, 5120], P('fsdp', 'blk'), may hold values from -6 to 6
- queries: bfloat16 [16, 256, 4096], P('fsdp', 'blk'), may hold values from -12 to 12
- prompt_cache: bfloat16 [16, 1024, 1024], P('fsdp', 'blk'), may hold values from -6 to 6
- kv_weight: bfloat16 [5120, 1024], P('fsdp'), may hold values from -0.078125 to 0.078125
- key_gain: float32 [128], replicated, may hold values from 0.1 to 1.9
- prompt_lengths: int32 [16], P('fsdp'), may hold values from 512 to 1024, as said below
- block_table: int32 [16, 4, 2], P('fsdp', 'blk'), may hold values from 0 to 1
- resp_lengths: int32 [16, 4], P('fsdp', 'blk'), may hold values from 16 to 64, as said below
Outputs:
- context: bfloat16 [16, 256, 4096], P('fsdp', 'blk')
The draws below stay inside these ranges and needn't reach their ends.
Inputs may be any that keep to these rules, and one draw needn't show every extreme that they name: `prompt_lengths`: the first group's prompt has 1024 tokens. `resp_lengths`: the first response of every group has 64 tokens.
All inputs are finite; a program needn't handle non-finite values.
Results may differ from the reference program's by a relative error of at most 0.0039.
Values may be sent and summed in bfloat16 or wider, within the bound.
No kernel may reach another device: no remote copies, remote signals or barrier semaphores. Data moves between devices by JAX's collectives and lax.ppermute only.
A program may use at most 192 MiB of HBM per device.

```python
import jax
import jax.numpy as jnp
from jax import lax

D = 5120
HQ = 32
KVH = 4
HD = 128
BLOCK = 512
RLEN = 64
GROUPS = 16
RESPONSES = 4
RESP_TOK = 256
NBLK = 2
PROMPT = 1024


def draw_queries(key, part):
    key = jax.random.fold_in(key, 11)
    shape = (GROUPS, RESP_TOK, HQ * HD)
    values = jnp.clip(2.5 * jax.random.normal(key, shape, jnp.float32), -12.0, 12.0)
    return values.astype(jnp.bfloat16)


def draw_prompt_cache(key, part):
    key = jax.random.fold_in(key, 12)
    shape = (GROUPS, PROMPT, 2 * KVH * HD)
    values = jnp.clip(jax.random.normal(key, shape, jnp.float32), -6.0, 6.0)
    return values.astype(jnp.bfloat16)


def draw_prompt_lengths(key, part):
    key = jax.random.fold_in(key, 21)
    drawn = jax.random.randint(key, (GROUPS,), PROMPT // 2, PROMPT + 1).astype(jnp.int32)
    return drawn.at[0].set(PROMPT)


def draw_block_table(key, part):
    key = jax.random.fold_in(key, 22)
    first_key, second_key = jax.random.split(key)
    rates = jax.random.randint(first_key, (GROUPS, RESPONSES, 1), 1, NBLK)
    picks = jax.random.randint(second_key, (GROUPS, RESPONSES, NBLK), 0, NBLK)
    table = (picks < rates).astype(jnp.int32)
    return table.at[:, :, 0].set(1)


def draw_resp_lengths(key, part):
    key = jax.random.fold_in(key, 23)
    drawn = jax.random.randint(key, (GROUPS, RESPONSES), RLEN // 4, RLEN + 1).astype(jnp.int32)
    return drawn.at[:, 0].set(RLEN)


def block_scale(key, dims, pieces, least, high):
    gain, own = 1.0, jax.random.fold_in(key, 6)
    for dim, blocks in pieces:
        steps = jnp.exp(jax.random.uniform(jax.random.fold_in(own, dim), (blocks,), jnp.float32, least / len(pieces), high / len(pieces)))
        gain = gain * jnp.repeat(steps, dims[dim] // blocks).reshape([-1 if axis == dim else 1 for axis in range(len(dims))])
    return gain


def bell_draw(own_key, dims, scale, reach, shards=(), dtype=jnp.bfloat16):
    entries = scale * jax.random.normal(own_key, dims, jnp.float32)
    if shards:
        entries = entries * block_scale(own_key, dims, shards, -0.22, 0.18)
    return jnp.clip(entries, -reach, reach).astype(dtype)


def setup_inputs(seed: int = 0) -> dict:
    seeds = jax.random.split(jax.random.key(seed), 9)
    x_resp = bell_draw(seeds[0], (GROUPS, RESP_TOK, D), 1.0, 6.0, ((0, 16), (1, 2)))
    queries = draw_queries(jax.random.fold_in(seeds[8], 71), 0)
    prompt_cache = draw_prompt_cache(jax.random.fold_in(seeds[8], 71), 0)
    kv_weight = bell_draw(seeds[3], (D, 2 * KVH * HD), D ** -0.5, 0.078125, ((0, 16),))
    key_gain = jnp.clip(1.0 + 0.18 * jax.random.normal(seeds[4], (HD,), jnp.float32), 0.1, 1.9)
    prompt_lengths = draw_prompt_lengths(jax.random.fold_in(seeds[8], 71), 0)
    block_table = draw_block_table(jax.random.fold_in(seeds[8], 71), 0)
    resp_lengths = draw_resp_lengths(jax.random.fold_in(seeds[8], 71), 0)
    return dict(x_resp=x_resp, queries=queries, prompt_cache=prompt_cache, kv_weight=kv_weight, key_gain=key_gain, prompt_lengths=prompt_lengths, block_table=block_table, resp_lengths=resp_lengths)


def one_group(group_args, kv_weight, key_gain):
    group_x, group_queries, group_cache, prompt_len, group_table, group_lengths = group_args
    projected = jnp.dot(group_x, kv_weight, preferred_element_type=jnp.float32)
    keys_raw = projected[:, :KVH * HD].reshape(RESP_TOK, KVH, HD)
    scaled = keys_raw * lax.rsqrt(lax.optimization_barrier(jnp.mean(keys_raw * keys_raw, axis=-1, keepdims=True)) + 1e-06)
    own_keys = (scaled * key_gain).astype(jnp.bfloat16)
    own_values = projected[:, KVH * HD:].reshape(RESP_TOK, KVH, HD).astype(jnp.bfloat16)
    prompt_keys = group_cache[:, :KVH * HD].reshape(PROMPT, KVH, HD)
    prompt_values = group_cache[:, KVH * HD:].reshape(PROMPT, KVH, HD)
    places = jnp.arange(PROMPT)
    block_of = places // BLOCK
    slots = jnp.arange(RLEN)

    def one_response(index):
        query = lax.dynamic_slice_in_dim(group_queries, index * RLEN, RLEN, 0).reshape(RLEN, KVH, HQ // KVH, HD)
        keys_here = lax.dynamic_slice_in_dim(own_keys, index * RLEN, RLEN, 0)
        values_here = lax.dynamic_slice_in_dim(own_values, index * RLEN, RLEN, 0)
        listed = jnp.take(group_table[index], block_of)
        prompt_mask = (listed == 1) & (places < prompt_len)
        live_len = group_lengths[index]
        own_mask = (slots[None, :] <= slots[:, None]) & (slots[None, :] < live_len)
        full_mask = jnp.concatenate([jnp.broadcast_to(prompt_mask[None, :], (RLEN, PROMPT)), own_mask], axis=1)
        all_keys = jnp.concatenate([prompt_keys, keys_here], axis=0).astype(jnp.float32)
        all_values = jnp.concatenate([prompt_values, values_here], axis=0).astype(jnp.float32)
        scores = jnp.einsum('tkgd,skd->kgts', query.astype(jnp.float32), all_keys) * HD ** (-0.5)
        scores = jnp.where(full_mask[None, None], scores, -jnp.inf)
        largest = lax.optimization_barrier(jnp.max(scores, axis=-1, keepdims=True))
        weights = jnp.exp(scores - largest)
        denominator = lax.optimization_barrier(jnp.sum(weights, axis=-1))
        rounded = weights.astype(jnp.bfloat16).astype(jnp.float32)
        summed = jnp.einsum('kgts,skd->tkgd', rounded, all_values)
        result = summed / jnp.transpose(denominator, (2, 0, 1))[..., None]
        live = (slots < live_len).astype(jnp.float32)
        return (result.reshape(RLEN, HQ * HD) * live[:, None]).astype(jnp.bfloat16)
    outputs = lax.map(one_response, jnp.arange(RESPONSES).astype(jnp.int32))
    return outputs.reshape(RESP_TOK, HQ * HD)

def reference(x_resp, queries, prompt_cache, kv_weight, key_gain, prompt_lengths, block_table, resp_lengths):

    def per_group(group_args):
        return one_group(group_args, kv_weight, key_gain)
    return lax.map(per_group, (x_resp, queries, prompt_cache, prompt_lengths, block_table, resp_lengths))
```

```python
import functools

import jax
import jax.numpy as jnp
from jax import lax
from jax.experimental import pallas as pl
from jax.experimental.pallas import tpu as pltpu
from jax.sharding import Mesh
from jax.sharding import PartitionSpec as P

HQ = 32
KVH = 4
HD = 128
SHARED = HQ // KVH
BLOCK = 512
RESP_DEV = 2
RLEN = 64
ROWS = RESP_DEV * RLEN
GROUP = SHARED * HD
SCALE = HD ** (-0.5) * 1.4426950408889634
HIDDEN = -1e30
NT = (((1,), (1,)), ((), ()))


def prompt_kernel(first, info, q_ref, k_ref, v_ref, *refs):
    if first:
        acc_ref, ml_ref = refs
    else:
        old_acc, old_ml, acc_ref, ml_ref = refs
    count = k_ref.shape[0]
    place = info[0] + lax.broadcasted_iota(jnp.int32, (1, count), 1)
    inside = place < info[1]
    biases = []
    for r in range(RESP_DEV):
        seen = inside & (jnp.full((1, count), info[2 + r]) == 1)
        biases.append(jnp.broadcast_to(jnp.where(seen, 0.0, HIDDEN), (RLEN, count)))
    bias = jnp.concatenate(biases, axis=0)
    keys = k_ref[...]
    values = v_ref[...]
    lane = lax.broadcasted_iota(jnp.int32, (ROWS, HD), 1)
    ml = jnp.zeros((ROWS, HD), jnp.float32)
    for g in range(SHARED):
        cols = slice(g * HD, (g + 1) * HD)
        scores = lax.dot_general(q_ref[:, cols], keys, NT, preferred_element_type=jnp.float32)
        scores = scores * SCALE + bias
        largest = jnp.max(scores, axis=1, keepdims=True)
        if not first:
            before = old_ml[0, :, g : g + 1]
            largest = jnp.maximum(largest, before)
            faded = jnp.exp2(before - largest)
        weights = jnp.exp2(scores - largest)
        total = jnp.sum(weights, axis=1, keepdims=True)
        acc = jnp.dot(weights.astype(jnp.bfloat16), values, preferred_element_type=jnp.float32)
        if not first:
            total = total + faded * old_ml[0, :, SHARED + g : SHARED + g + 1]
            acc = acc + faded * old_acc[:, cols]
        acc_ref[:, cols] = acc
        ml = jnp.where(lane == g, largest, ml)
        ml = jnp.where(lane == SHARED + g, total, ml)
    ml_ref[0] = ml


def prompt_attention(info, query, cache, state):
    count = cache.shape[0]
    first = state is None
    wide = pl.BlockSpec((ROWS, GROUP), lambda k, s: (0, k))
    small = pl.BlockSpec((1, ROWS, HD), lambda k, s: (k, 0, 0))
    specs = [
        wide,
        pl.BlockSpec((count, HD), lambda k, s: (0, k)),
        pl.BlockSpec((count, HD), lambda k, s: (0, KVH + k)),
    ]
    operands = [query, cache, cache]
    if not first:
        specs += [wide, small]
        operands += list(state)
    return pl.pallas_call(
        functools.partial(prompt_kernel, first),
        grid_spec=pltpu.PrefetchScalarGridSpec(
            num_scalar_prefetch=1, grid=(KVH,), in_specs=specs, out_specs=[wide, small]
        ),
        out_shape=[
            jax.ShapeDtypeStruct((ROWS, HQ * HD), jnp.float32),
            jax.ShapeDtypeStruct((KVH, ROWS, HD), jnp.float32),
        ],
        compiler_params=pltpu.CompilerParams(vmem_limit_bytes=32 * 2**20),
        cost_estimate=pl.CostEstimate(
            flops=8 * ROWS * HQ * count * HD, bytes_accessed=6 * 2**20, transcendentals=ROWS * HQ * count
        ),
        name="prompt_attention",
    )(info, *operands)


def project_kernel(where, x_ref, other_ref, same_ref, cross_ref, mine_ref, theirs_ref, both):
    rows = same_ref.shape[0]
    core = where[1]
    both[pl.ds(pl.multiple_of(core * rows, 16), rows), :] = same_ref[...]
    both[pl.ds(pl.multiple_of((1 - core) * rows, 16), rows), :] = cross_ref[...]
    left = jnp.concatenate([x_ref[...], other_ref[...]], axis=0)
    product = jnp.dot(left, both[...], preferred_element_type=jnp.float32)
    start = pl.program_id(0) == 0

    @pl.when(start)
    def _():
        mine_ref[...] = product[:ROWS]
        theirs_ref[...] = product[ROWS:]

    @pl.when(jnp.logical_not(start))
    def _():
        mine_ref[...] += product[:ROWS]
        theirs_ref[...] += product[ROWS:]


def project(where, x, other, same, cross, steps):
    rows = same.shape[0] // steps
    columns = same.shape[1]
    out = pl.BlockSpec((ROWS, columns), lambda z, w: (0, 0))
    weight = pl.BlockSpec((rows, columns), lambda z, w: (z, 0))
    return pl.pallas_call(
        project_kernel,
        grid_spec=pltpu.PrefetchScalarGridSpec(
            num_scalar_prefetch=1,
            grid=(steps,),
            in_specs=[
                pl.BlockSpec((None, ROWS, 2 * rows), lambda z, w: (z, 0, 0)),
                pl.BlockSpec((None, ROWS, 2 * rows), lambda z, w: (z, 0, 0)),
                weight,
                weight,
            ],
            out_specs=[out, out],
            scratch_shapes=[pltpu.VMEM((2 * rows, columns), jnp.bfloat16)],
        ),
        out_shape=[jax.ShapeDtypeStruct((ROWS, columns), jnp.float32)] * 2,
        compiler_params=pltpu.CompilerParams(vmem_limit_bytes=32 * 2**20),
        cost_estimate=pl.CostEstimate(
            flops=8 * ROWS * rows * steps * columns, bytes_accessed=8 * 2**20, transcendentals=0
        ),
        name="project",
    )(where, x, other, same, cross)


def final_kernel(lengths, gain_ref, q_ref, ka_ref, kb_ref, va_ref, vb_ref, acc_ref, ml_ref, out_ref):
    raw = ka_ref[...] + kb_ref[...]
    mean = jnp.mean(raw * raw, axis=1, keepdims=True)
    keys = (raw * lax.rsqrt(mean + 1e-06) * gain_ref[...]).astype(jnp.bfloat16)
    values = (va_ref[...] + vb_ref[...]).astype(jnp.bfloat16)
    row = lax.broadcasted_iota(jnp.int32, (ROWS, ROWS), 0)
    col = lax.broadcasted_iota(jnp.int32, (ROWS, ROWS), 1)
    length = jnp.where(row < RLEN, lengths[0], lengths[1])
    base = jnp.where(row < RLEN, 0, RLEN)
    seen = (col >= base) & (col <= row) & (col - base < length)
    live = (row - base < length).astype(jnp.float32)
    for g in range(SHARED):
        cols = slice(g * HD, (g + 1) * HD)
        scores = lax.dot_general(q_ref[:, cols], keys, NT, preferred_element_type=jnp.float32)
        scores = jnp.where(seen, scores * SCALE, HIDDEN)
        before = ml_ref[0, :, g : g + 1]
        largest = jnp.maximum(jnp.max(scores, axis=1, keepdims=True), before)
        faded = jnp.exp2(before - largest)
        weights = jnp.exp2(scores - largest)
        total = jnp.sum(weights, axis=1, keepdims=True) + faded * ml_ref[0, :, SHARED + g : SHARED + g + 1]
        acc = jnp.dot(weights.astype(jnp.bfloat16), values, preferred_element_type=jnp.float32)
        acc = acc + faded * acc_ref[:, cols]
        out_ref[:, cols] = (acc / total * live).astype(jnp.bfloat16)


def final_attention(lengths, gain, query, mine, theirs, acc, ml):
    wide = pl.BlockSpec((ROWS, GROUP), lambda k, s: (0, k))
    key = pl.BlockSpec((ROWS, HD), lambda k, s: (0, k))
    value = pl.BlockSpec((ROWS, HD), lambda k, s: (0, KVH + k))
    return pl.pallas_call(
        final_kernel,
        grid_spec=pltpu.PrefetchScalarGridSpec(
            num_scalar_prefetch=1,
            grid=(KVH,),
            in_specs=[
                pl.BlockSpec((1, HD), lambda k, s: (0, 0)),
                wide,
                key,
                key,
                value,
                value,
                wide,
                pl.BlockSpec((1, ROWS, HD), lambda k, s: (k, 0, 0)),
            ],
            out_specs=wide,
        ),
        out_shape=jax.ShapeDtypeStruct((ROWS, HQ * HD), jnp.bfloat16),
        compiler_params=pltpu.CompilerParams(vmem_limit_bytes=32 * 2**20),
        cost_estimate=pl.CostEstimate(
            flops=8 * ROWS * HQ * ROWS * HD, bytes_accessed=6 * 2**20, transcendentals=ROWS * HQ * ROWS
        ),
        name="final_attention",
    )(lengths, gain, query, mine, theirs, mine, theirs, acc, ml)


def swap(array, axis):
    return lax.ppermute(array, axis, [(0, 1), (1, 0)])


def per_device(
    x_resp, queries, prompt_cache, kv_weight, key_gain, prompt_lengths, block_table, resp_lengths
):
    x, query, cache = x_resp[0], queries[0], prompt_cache[0]
    steps = lax.axis_size("z")
    y, core = lax.axis_index("y"), lax.axis_index("core")
    holder, cycle = lax.axis_index("blk"), lax.axis_size("blk")
    part = x.shape[1] // (2 * steps)

    same = lax.all_gather(kv_weight, "z", axis=0, tiled=True)
    halves = jnp.transpose(x.reshape(ROWS, steps, 2, part), (2, 1, 0, 3))
    other = swap(lax.dynamic_index_in_dim(halves, 1 - y, axis=0, keepdims=False), "y")
    x = lax.dynamic_index_in_dim(halves, y, axis=0, keepdims=False)

    state = None
    for stride in range(cycle):
        owner = lax.rem(holder + cycle - stride, cycle)
        first_place = owner * cache.shape[0]
        listed = lax.dynamic_index_in_dim(block_table[0], first_place // BLOCK, axis=1, keepdims=False)
        info = jnp.concatenate([first_place[None], prompt_lengths, listed]).astype(jnp.int32)
        if stride + 1 < cycle:
            following = lax.ppermute(cache, "blk", [(i, (i + 1) % cycle) for i in range(cycle)])
        state = prompt_attention(info, query, cache, state)
        cache = following

    same, other, x, state = lax.optimization_barrier((same, other, x, state))
    cross = swap(same, "core")
    where = jnp.stack([y, core]).astype(jnp.int32)
    mine, theirs = project(where, x, other, same, cross, steps)
    theirs = swap(theirs, "y")
    return final_attention(resp_lengths[0], key_gain[None], query, mine, theirs, *state)[None]


def solution(mesh):
    groups, blocks = mesh.devices.shape
    split = Mesh(mesh.devices.reshape(groups // 4, 2, 2, blocks), ("z", "y", "core", "blk"))
    fsdp = ("z", "y", "core")
    return jax.shard_map(
        per_device,
        mesh=split,
        in_specs=(
            P(fsdp, "blk", None),
            P(fsdp, "blk", None),
            P(fsdp, "blk", None),
            P(fsdp, None),
            P(),
            P(fsdp),
            P(fsdp, "blk", None),
            P(fsdp, "blk"),
        ),
        out_specs=P(fsdp, "blk", None),
        check_vma=False,
    )
```

```python
import functools

import jax
import jax.numpy as jnp
from jax import lax
from jax.experimental import pallas as pl
from jax.experimental.pallas import tpu as pltpu
from jax.sharding import Mesh
from jax.sharding import PartitionSpec as P

HQ = 32
KVH = 4
HD = 128
SHARED = HQ // KVH
BLOCK = 512
RESP_DEV = 2
RLEN = 64
ROWS = RESP_DEV * RLEN
PAIR = 2 * ROWS
GROUP = SHARED * HD
SCALE = HD ** (-0.5) * 1.4426950408889634
HIDDEN = -1e30
NT = (((1,), (1,)), ((), ()))


def pair_scores(keys, q_ref, g):
    heads = [q_ref[:, i * HD : (i + 1) * HD] for i in (g, g + 1)]
    scores = lax.dot_general(keys, jnp.concatenate(heads, axis=0), NT, preferred_element_type=jnp.float32)
    return scores * SCALE


def prompt_kernel(first, info, q_ref, k_ref, v_ref, *refs):
    if first:
        acc_ref, ml_ref = refs
    else:
        old_acc, old_ml, acc_ref, ml_ref = refs
    count = k_ref.shape[0]
    place = info[0] + lax.broadcasted_iota(jnp.int32, (count, PAIR), 0)
    lane = lax.broadcasted_iota(jnp.int32, (count, PAIR), 1)
    listed = jnp.where(lane % ROWS < RLEN, info[2], info[3])
    bias = jnp.where((place < info[1]) & (listed == 1), 0.0, HIDDEN)
    keys = k_ref[...]
    values = v_ref[...].T
    for g in range(0, SHARED, 2):
        cols = slice(g * HD, (g + 2) * HD)
        scores = pair_scores(keys, q_ref, g) + bias
        largest = jnp.max(scores, axis=0, keepdims=True)
        if not first:
            before = old_ml[0:1, cols]
            largest = jnp.maximum(largest, before)
            faded = jnp.exp2(before - largest)
        weights = jnp.exp2(scores - largest)
        total = jnp.sum(weights, axis=0, keepdims=True)
        acc = jnp.dot(values, weights.astype(jnp.bfloat16), preferred_element_type=jnp.float32)
        if not first:
            total = total + faded * old_ml[1:2, cols]
            acc = acc + faded * old_acc[:, cols]
        acc_ref[:, cols] = acc
        ml_ref[0:1, cols] = largest
        ml_ref[1:2, cols] = total


def prompt_attention(info, query, cache, state):
    count = cache.shape[0]
    first = state is None
    wide = pl.BlockSpec((ROWS, GROUP), lambda k, s: (0, k))
    turned = pl.BlockSpec((HD, SHARED * ROWS), lambda k, s: (0, k))
    small = pl.BlockSpec((8, SHARED * ROWS), lambda k, s: (0, k))
    specs = [
        wide,
        pl.BlockSpec((count, HD), lambda k, s: (0, k)),
        pl.BlockSpec((count, HD), lambda k, s: (0, KVH + k)),
    ]
    operands = [query, cache, cache]
    if not first:
        specs += [turned, small]
        operands += list(state)
    return pl.pallas_call(
        functools.partial(prompt_kernel, first),
        grid_spec=pltpu.PrefetchScalarGridSpec(
            num_scalar_prefetch=1, grid=(KVH,), in_specs=specs, out_specs=[turned, small]
        ),
        out_shape=[
            jax.ShapeDtypeStruct((HD, HQ * ROWS), jnp.float32),
            jax.ShapeDtypeStruct((8, HQ * ROWS), jnp.float32),
        ],
        compiler_params=pltpu.CompilerParams(vmem_limit_bytes=32 * 2**20),
        cost_estimate=pl.CostEstimate(
            flops=8 * ROWS * HQ * count * HD, bytes_accessed=6 * 2**20, transcendentals=ROWS * HQ * count
        ),
        name="prompt_attention",
    )(info, *operands)


def project_kernel(where, x_ref, other_ref, same_ref, cross_ref, mine_ref, theirs_ref, both):
    rows = same_ref.shape[0]
    core = where[1]
    both[pl.ds(pl.multiple_of(core * rows, 16), rows), :] = same_ref[...]
    both[pl.ds(pl.multiple_of((1 - core) * rows, 16), rows), :] = cross_ref[...]
    left = jnp.concatenate([x_ref[...], other_ref[...]], axis=0)
    product = jnp.dot(left, both[...], preferred_element_type=jnp.float32)
    start = pl.program_id(0) == 0

    @pl.when(start)
    def _():
        mine_ref[...] = product[:ROWS]
        theirs_ref[...] = product[ROWS:]

    @pl.when(jnp.logical_not(start))
    def _():
        mine_ref[...] += product[:ROWS]
        theirs_ref[...] += product[ROWS:]


def project(where, x, other, same, cross, steps):
    rows = same.shape[0] // steps
    columns = same.shape[1]
    out = pl.BlockSpec((ROWS, columns), lambda z, w: (0, 0))
    weight = pl.BlockSpec((rows, columns), lambda z, w: (z, 0))
    return pl.pallas_call(
        project_kernel,
        grid_spec=pltpu.PrefetchScalarGridSpec(
            num_scalar_prefetch=1,
            grid=(steps,),
            in_specs=[
                pl.BlockSpec((None, ROWS, 2 * rows), lambda z, w: (z, 0, 0)),
                pl.BlockSpec((None, ROWS, 2 * rows), lambda z, w: (z, 0, 0)),
                weight,
                weight,
            ],
            out_specs=[out, out],
            scratch_shapes=[pltpu.VMEM((2 * rows, columns), jnp.bfloat16)],
        ),
        out_shape=[jax.ShapeDtypeStruct((ROWS, columns), jnp.float32)] * 2,
        compiler_params=pltpu.CompilerParams(vmem_limit_bytes=32 * 2**20),
        cost_estimate=pl.CostEstimate(
            flops=8 * ROWS * rows * steps * columns, bytes_accessed=8 * 2**20, transcendentals=0
        ),
        name="project",
    )(where, x, other, same, cross)


def final_kernel(lengths, gain_ref, q_ref, ka_ref, kb_ref, va_ref, vb_ref, acc_ref, ml_ref, out_ref):
    raw = ka_ref[...] + kb_ref[...]
    mean = jnp.mean(raw * raw, axis=1, keepdims=True)
    keys = (raw * lax.rsqrt(mean + 1e-06) * gain_ref[...]).astype(jnp.bfloat16)
    values = (va_ref[...] + vb_ref[...]).T.astype(jnp.bfloat16)
    slot = lax.broadcasted_iota(jnp.int32, (ROWS, PAIR), 0)
    row = lax.broadcasted_iota(jnp.int32, (ROWS, PAIR), 1) % ROWS
    length = jnp.where(row < RLEN, lengths[0], lengths[1])
    base = jnp.where(row < RLEN, 0, RLEN)
    seen = (slot >= base) & (slot <= row) & (slot - base < length)
    live = jnp.where(row - base < length, 1.0, 0.0)[0:1]
    for g in range(0, SHARED, 2):
        cols = slice(g * HD, (g + 2) * HD)
        scores = jnp.where(seen, pair_scores(keys, q_ref, g), HIDDEN)
        before = ml_ref[0:1, cols]
        largest = jnp.maximum(jnp.max(scores, axis=0, keepdims=True), before)
        faded = jnp.exp2(before - largest)
        weights = jnp.exp2(scores - largest)
        total = jnp.sum(weights, axis=0, keepdims=True) + faded * ml_ref[1:2, cols]
        acc = jnp.dot(values, weights.astype(jnp.bfloat16), preferred_element_type=jnp.float32)
        acc = (acc + faded * acc_ref[:, cols]) * (live / total)
        out_ref[:, g * HD : (g + 1) * HD] = acc[:, :ROWS].T.astype(jnp.bfloat16)
        out_ref[:, (g + 1) * HD : (g + 2) * HD] = acc[:, ROWS:].T.astype(jnp.bfloat16)


def final_attention(lengths, gain, query, mine, theirs, acc, ml):
    wide = pl.BlockSpec((ROWS, GROUP), lambda k, s: (0, k))
    key = pl.BlockSpec((ROWS, HD), lambda k, s: (0, k))
    value = pl.BlockSpec((ROWS, HD), lambda k, s: (0, KVH + k))
    return pl.pallas_call(
        final_kernel,
        grid_spec=pltpu.PrefetchScalarGridSpec(
            num_scalar_prefetch=1,
            grid=(KVH,),
            in_specs=[
                pl.BlockSpec((1, HD), lambda k, s: (0, 0)),
                wide,
                key,
                key,
                value,
                value,
                pl.BlockSpec((HD, SHARED * ROWS), lambda k, s: (0, k)),
                pl.BlockSpec((8, SHARED * ROWS), lambda k, s: (0, k)),
            ],
            out_specs=wide,
        ),
        out_shape=jax.ShapeDtypeStruct((ROWS, HQ * HD), jnp.bfloat16),
        compiler_params=pltpu.CompilerParams(vmem_limit_bytes=32 * 2**20),
        cost_estimate=pl.CostEstimate(
            flops=8 * ROWS * HQ * ROWS * HD, bytes_accessed=6 * 2**20, transcendentals=ROWS * HQ * ROWS
        ),
        name="final_attention",
    )(lengths, gain, query, mine, theirs, mine, theirs, acc, ml)


def swap(array, axis):
    return lax.ppermute(array, axis, [(0, 1), (1, 0)])


def per_device(
    x_resp, queries, prompt_cache, kv_weight, key_gain, prompt_lengths, block_table, resp_lengths
):
    x, query, cache = x_resp[0], queries[0], prompt_cache[0]
    steps = lax.axis_size("z")
    y, core = lax.axis_index("y"), lax.axis_index("core")
    holder, cycle = lax.axis_index("blk"), lax.axis_size("blk")
    part = x.shape[1] // (2 * steps)

    same = lax.all_gather(kv_weight, "z", axis=0, tiled=True)
    halves = jnp.transpose(x.reshape(ROWS, steps, 2, part), (2, 1, 0, 3))
    other = swap(lax.dynamic_index_in_dim(halves, 1 - y, axis=0, keepdims=False), "y")
    x = lax.dynamic_index_in_dim(halves, y, axis=0, keepdims=False)

    state = None
    for stride in range(cycle):
        owner = lax.rem(holder + cycle - stride, cycle)
        first_place = owner * cache.shape[0]
        listed = lax.dynamic_index_in_dim(block_table[0], first_place // BLOCK, axis=1, keepdims=False)
        info = jnp.concatenate([first_place[None], prompt_lengths, listed]).astype(jnp.int32)
        if stride + 1 < cycle:
            following = lax.ppermute(cache, "blk", [(i, (i + 1) % cycle) for i in range(cycle)])
        state = prompt_attention(info, query, cache, state)
        cache = following

    same, other, x, state = lax.optimization_barrier((same, other, x, state))
    cross = swap(same, "core")
    where = jnp.stack([y, core]).astype(jnp.int32)
    mine, theirs = project(where, x, other, same, cross, steps)
    theirs = swap(theirs, "y")
    return final_attention(resp_lengths[0], key_gain[None], query, mine, theirs, *state)[None]


def solution(mesh):
    groups, blocks = mesh.devices.shape
    split = Mesh(mesh.devices.reshape(groups // 4, 2, 2, blocks), ("z", "y", "core", "blk"))
    fsdp = ("z", "y", "core")
    return jax.shard_map(
        per_device,
        mesh=split,
        in_specs=(
            P(fsdp, "blk", None),
            P(fsdp, "blk", None),
            P(fsdp, "blk", None),
            P(fsdp, None),
            P(),
            P(fsdp),
            P(fsdp, "blk", None),
            P(fsdp, "blk"),
        ),
        out_specs=P(fsdp, "blk", None),
        check_vma=False,
    )
```

```python
import functools

import jax
import jax.numpy as jnp
from jax import lax
from jax.experimental import pallas as pl
from jax.experimental.pallas import tpu as pltpu
from jax.sharding import Mesh
from jax.sharding import PartitionSpec as P

HQ = 32
KVH = 4
HD = 128
SHARED = HQ // KVH
BLOCK = 512
RESP_DEV = 2
RLEN = 64
ROWS = RESP_DEV * RLEN
PAIR = 2 * ROWS
GROUP = SHARED * HD
SCALE = HD ** (-0.5) * 1.4426950408889634
HIDDEN = -1e30
NT = (((1,), (1,)), ((), ()))
HINT = pl.CostEstimate(flops=1024, bytes_accessed=1024, transcendentals=0)


def pair_scores(keys, q_ref, g):
    heads = [q_ref[:, i * HD : (i + 1) * HD] for i in (g, g + 1)]
    scores = lax.dot_general(keys, jnp.concatenate(heads, axis=0), NT, preferred_element_type=jnp.float32)
    return scores * SCALE


def prompt_kernel(first, info, q_ref, k_ref, v_ref, *refs):
    if first:
        acc_ref, ml_ref = refs
    else:
        old_acc, old_ml, acc_ref, ml_ref = refs
    count = k_ref.shape[0]
    place = info[0] + lax.broadcasted_iota(jnp.int32, (count, PAIR), 0)
    lane = lax.broadcasted_iota(jnp.int32, (count, PAIR), 1)
    listed = jnp.where(lane % ROWS < RLEN, info[2], info[3])
    bias = jnp.where((place < info[1]) & (listed == 1), 0.0, HIDDEN)
    keys = k_ref[...]
    values = v_ref[...].T
    for g in range(0, SHARED, 2):
        cols = slice(g * HD, (g + 2) * HD)
        scores = pair_scores(keys, q_ref, g) + bias
        largest = jnp.max(scores, axis=0, keepdims=True)
        if not first:
            before = old_ml[0:1, cols]
            largest = jnp.maximum(largest, before)
            faded = jnp.exp2(before - largest)
        weights = jnp.exp2(scores - largest)
        total = jnp.sum(weights, axis=0, keepdims=True)
        acc = jnp.dot(values, weights.astype(jnp.bfloat16), preferred_element_type=jnp.float32)
        if not first:
            total = total + faded * old_ml[1:2, cols]
            acc = acc + faded * old_acc[:, cols]
        acc_ref[:, cols] = acc
        ml_ref[0:1, cols] = largest
        ml_ref[1:2, cols] = total


def prompt_attention(info, query, cache, state, head, heads):
    count = cache.shape[0]
    first = state is None
    wide = pl.BlockSpec((ROWS, GROUP), lambda k, s: (0, head + k))
    turned = pl.BlockSpec((HD, SHARED * ROWS), lambda k, s: (0, k))
    small = pl.BlockSpec((8, SHARED * ROWS), lambda k, s: (0, k))
    specs = [
        wide,
        pl.BlockSpec((count, HD), lambda k, s: (0, head + k)),
        pl.BlockSpec((count, HD), lambda k, s: (0, KVH + head + k)),
    ]
    operands = [query, cache, cache]
    if not first:
        specs += [turned, small]
        operands += list(state)
    return pl.pallas_call(
        functools.partial(prompt_kernel, first),
        grid_spec=pltpu.PrefetchScalarGridSpec(
            num_scalar_prefetch=1, grid=(heads,), in_specs=specs, out_specs=[turned, small]
        ),
        out_shape=[
            jax.ShapeDtypeStruct((HD, heads * SHARED * ROWS), jnp.float32),
            jax.ShapeDtypeStruct((8, heads * SHARED * ROWS), jnp.float32),
        ],
        compiler_params=pltpu.CompilerParams(vmem_limit_bytes=32 * 2**20),
        cost_estimate=HINT,
        name="prompt_attention",
    )(info, *operands)


def pack_rows_kernel(where, keep_ref, send_ref, keep_out, send_out):
    keep_out[...] = keep_ref[...]
    send_out[...] = send_ref[...]


def pack_rows(where, x, y, steps):
    part = x.shape[1] // (2 * steps)
    if part % 128:
        halves = jnp.transpose(x.reshape(ROWS, steps, 2, part), (2, 1, 0, 3))
        return [lax.dynamic_index_in_dim(halves, i, axis=0, keepdims=False) for i in (y, 1 - y)]
    out = pl.BlockSpec((None, ROWS, part), lambda z, w: (z, 0, 0))
    return pl.pallas_call(
        pack_rows_kernel,
        grid_spec=pltpu.PrefetchScalarGridSpec(
            num_scalar_prefetch=1,
            grid=(steps,),
            in_specs=[
                pl.BlockSpec((ROWS, part), lambda z, w: (0, 2 * z + w[1])),
                pl.BlockSpec((ROWS, part), lambda z, w: (0, 2 * z + 1 - w[1])),
            ],
            out_specs=[out, out],
        ),
        out_shape=[jax.ShapeDtypeStruct((steps, ROWS, part), x.dtype)] * 2,
        cost_estimate=HINT,
        name="pack_rows",
    )(where, x, x)


def pack_weight_kernel(chunks, where, own_ref, got_ref, *outs):
    rows = own_ref.shape[0]
    helped, direct = row_split(2 * rows)
    core, plane = where[2], where[3]
    own_place = pl.ds(pl.multiple_of(core * rows, 16), rows)
    got_place = pl.ds(pl.multiple_of((1 - core) * rows, 16), rows)
    direct_place = pl.ds(pl.multiple_of(plane * helped, 16), direct)
    for i, (head, heads) in enumerate(chunks):
        columns = slice(head * HD, (head + heads) * HD)
        whole, far = outs[2 * i], outs[2 * i + 1]
        whole[own_place, :] = own_ref[:, columns]
        whole[got_place, :] = got_ref[:, columns]
        far[...] = whole[direct_place, :]


def row_split(rows):
    helped = rows * 2 // 5
    return helped, rows - helped


def pack_weight(where, own, got, chunks):
    rows = own.shape[0]
    shapes = []
    for _, heads in chunks:
        shapes.append(jax.ShapeDtypeStruct((2 * rows, heads * HD), own.dtype))
        shapes.append(jax.ShapeDtypeStruct((row_split(2 * rows)[1], heads * HD), own.dtype))
    outs = pl.pallas_call(
        functools.partial(pack_weight_kernel, chunks),
        grid_spec=pltpu.PrefetchScalarGridSpec(
            num_scalar_prefetch=1,
            grid=(1,),
            in_specs=[pl.BlockSpec((rows, KVH * HD), lambda i, w: (0, 0))] * 2,
            out_specs=[pl.BlockSpec(shape.shape, lambda i, w: (0, 0)) for shape in shapes],
        ),
        out_shape=shapes,
        cost_estimate=HINT,
        name="pack_weight",
    )(where, own, got)
    return outs[0::2], outs[1::2]


def project_kernel(steps, where, *refs):
    groups, refs = refs[:4], refs[4:]
    near, direct, forwarded, outs, whole = refs[:2], refs[2:steps], refs[steps], refs[steps + 1 : -1], refs[-1]
    plane = where[3]
    total = None
    for j in range(steps):
        if j < 2:
            weight = near[j][...]
        else:
            count, extra = direct[j - 2].shape[0], forwarded.shape[1]
            whole[j - 2, pl.ds(pl.multiple_of(plane * extra, 16), count), :] = direct[j - 2][...]
            whole[j - 2, pl.ds(pl.multiple_of((1 - plane) * count, 16), extra), :] = forwarded[j - 2]
            weight = whole[j - 2]
        place = where[0] ^ j
        left = jnp.concatenate([group[place] for group in groups], axis=0)
        product = jnp.dot(left, weight, preferred_element_type=jnp.float32)
        total = product if total is None else total + product
    for i, out in enumerate(outs):
        out[...] = total[i * ROWS : (i + 1) * ROWS]


def project(where, groups, near, direct, forwarded):
    steps = 2 + len(direct)
    rows, columns = near[0].shape
    operands = [*groups, *near, *direct, forwarded]
    out = jax.ShapeDtypeStruct((ROWS, columns), jnp.float32)

    def full(array):
        return pl.BlockSpec(array.shape, lambda i, w: (0,) * len(array.shape))

    return pl.pallas_call(
        functools.partial(project_kernel, steps),
        grid_spec=pltpu.PrefetchScalarGridSpec(
            num_scalar_prefetch=1,
            grid=(1,),
            in_specs=[full(array) for array in operands],
            out_specs=[full(out)] * 4,
            scratch_shapes=[pltpu.VMEM((steps - 2, rows, columns), jnp.bfloat16)],
        ),
        out_shape=[out] * 4,
        compiler_params=pltpu.CompilerParams(vmem_limit_bytes=32 * 2**20),
        cost_estimate=HINT,
        name="project",
    )(where, *operands)


def final_kernel(info, gain_ref, q_ref, here_a, here_b, there_a, there_b, acc_ref, ml_ref, *refs):
    out_ref = refs[-1]
    here = here_a[...] + here_b[...]
    there = there_a[...] + there_b[...]
    first_core = jnp.full(here.shape, info[2]) == 0
    raw = jnp.where(first_core, here, there)
    mean = jnp.mean(raw * raw, axis=1, keepdims=True)
    keys = (raw * lax.rsqrt(mean + 1e-06) * gain_ref[...]).astype(jnp.bfloat16)
    values = jnp.where(first_core, there, here).T.astype(jnp.bfloat16)
    slot = lax.broadcasted_iota(jnp.int32, (ROWS, PAIR), 0)
    row = lax.broadcasted_iota(jnp.int32, (ROWS, PAIR), 1) % ROWS
    length = jnp.where(row < RLEN, info[0], info[1])
    base = jnp.where(row < RLEN, 0, RLEN)
    seen = (slot >= base) & (slot <= row) & (slot - base < length)
    live = jnp.where(row - base < length, 1.0, 0.0)[0:1]
    for g in range(0, SHARED, 2):
        cols = slice(g * HD, (g + 2) * HD)
        scores = jnp.where(seen, pair_scores(keys, q_ref, g), HIDDEN)
        before = ml_ref[0:1, cols]
        largest = jnp.maximum(jnp.max(scores, axis=0, keepdims=True), before)
        faded = jnp.exp2(before - largest)
        weights = jnp.exp2(scores - largest)
        total = jnp.sum(weights, axis=0, keepdims=True) + faded * ml_ref[1:2, cols]
        acc = jnp.dot(values, weights.astype(jnp.bfloat16), preferred_element_type=jnp.float32)
        acc = (acc + faded * acc_ref[:, cols]) * (live / total)
        out_ref[:, g * HD : (g + 1) * HD] = acc[:, :ROWS].T.astype(jnp.bfloat16)
        out_ref[:, (g + 1) * HD : (g + 2) * HD] = acc[:, ROWS:].T.astype(jnp.bfloat16)


def final_attention(info, gain, query, sums, state, offset, chunk, result):
    head, heads = chunk
    wide = pl.BlockSpec((ROWS, GROUP), lambda k, s: (0, head + k))
    part = pl.BlockSpec((ROWS, HD), lambda k, s: (0, k))
    operands = [gain, query, *sums, *state]
    specs = [
        pl.BlockSpec((1, HD), lambda k, s: (0, 0)),
        wide,
        part,
        part,
        part,
        part,
        pl.BlockSpec((HD, SHARED * ROWS), lambda k, s: (0, offset + k)),
        pl.BlockSpec((8, SHARED * ROWS), lambda k, s: (0, offset + k)),
    ]
    aliases = {}
    if result is not None:
        operands.append(result)
        specs.append(pl.BlockSpec(memory_space=pl.ANY))
        aliases = {len(operands): 0}
    return pl.pallas_call(
        final_kernel,
        grid_spec=pltpu.PrefetchScalarGridSpec(
            num_scalar_prefetch=1, grid=(heads,), in_specs=specs, out_specs=wide
        ),
        out_shape=jax.ShapeDtypeStruct((ROWS, HQ * HD), jnp.bfloat16),
        input_output_aliases=aliases,
        compiler_params=pltpu.CompilerParams(vmem_limit_bytes=32 * 2**20),
        cost_estimate=HINT,
        name="final_attention",
    )(info, *operands)


def xor_swap(array, axis, by):
    return lax.ppermute(array, axis, [(i, i ^ by) for i in range(lax.axis_size(axis))])


CHUNKS = ((0, 2), (2, 1), (3, 1))
HALVES = ((0, 2), (2, 2))


def per_device(
    x_resp, queries, prompt_cache, kv_weight, key_gain, prompt_lengths, block_table, resp_lengths
):
    x, query = x_resp[0], queries[0]
    steps = lax.axis_size("z")
    z, y, core = lax.axis_index("z"), lax.axis_index("y"), lax.axis_index("core")
    holder, cycle = lax.axis_index("blk"), lax.axis_size("blk")
    plane = holder % 2
    where = jnp.stack([z, y, core, plane]).astype(jnp.int32)

    caches = [prompt_cache[0]]
    for _ in range(cycle - 1):
        caches.append(lax.ppermute(caches[-1], "blk", [(i, (i + 1) % cycle) for i in range(cycle)]))

    half = KVH * HD
    own = lax.dynamic_slice_in_dim(kv_weight, core * half, half, axis=1)
    got = xor_swap(lax.dynamic_slice_in_dim(kv_weight, (1 - core) * half, half, axis=1), "core", 1)
    whole, far = pack_weight(where, own, got, CHUNKS)
    helped, direct = row_split(2 * kv_weight.shape[0])

    def send(chunk, whole, far):
        pieces = [xor_swap(far, "z", j) for j in range(steps - 1, 1, -1)][::-1]
        return xor_swap(whole, "z", 1), pieces

    def forward(pieces):
        parts = [lax.dynamic_slice_in_dim(p, plane * (direct - helped), helped, axis=0) for p in pieces]
        return xor_swap(jnp.stack(parts), "blk", 1)

    sent = [send(0, whole[0], far[0])]
    query, _ = lax.optimization_barrier((query, whole[0]))
    keep, other = pack_rows(where, x, y, steps)
    other = xor_swap(other, "y", 1)
    groups = [keep, other, xor_swap(keep, "core", 1), xor_swap(other, "core", 1)]

    infos = []
    for stride in range(cycle):
        owner = lax.rem(holder + cycle - stride, cycle)
        place = owner * prompt_cache.shape[1]
        listed = lax.dynamic_index_in_dim(block_table[0], place // BLOCK, axis=1, keepdims=False)
        infos.append(jnp.concatenate([place[None], prompt_lengths, listed]).astype(jnp.int32))

    states = [prompt_attention(infos[0], query, caches[0], None, *heads) for heads in HALVES]

    def rest(i):
        for stride in range(1, cycle):
            states[i] = prompt_attention(infos[stride], query, caches[stride], states[i], *HALVES[i])

    sent[0], ahead, states = lax.optimization_barrier((sent[0], (whole[1], far[1]), states))
    forwarded = [forward(sent[0][1])]
    sent.append(send(1, *ahead))
    rest(0)
    sent[1], ahead, states[0] = lax.optimization_barrier((sent[1], (whole[2], far[2]), states[0]))
    forwarded.append(forward(sent[1][1]))
    sent.append(send(2, *ahead))
    rest(1)
    sent[2], states[1] = lax.optimization_barrier((sent[2], states[1]))
    forwarded.append(forward(sent[2][1]))

    info = jnp.concatenate([resp_lengths[0], core[None]]).astype(jnp.int32)
    result = None
    for i, chunk in enumerate(CHUNKS):
        near, pieces = sent[i]
        sums = project(where, groups, [whole[i], near], pieces, forwarded[i])
        sums = [
            sums[0],
            xor_swap(sums[1], "y", 1),
            xor_swap(sums[2], "core", 1),
            xor_swap(sums[3], ("y", "core"), 3),
        ]
        at = [n for n, (head, heads) in enumerate(HALVES) if head <= chunk[0] < head + heads][0]
        result = final_attention(
            info, key_gain[None], query, sums, states[at], chunk[0] - HALVES[at][0], chunk, result
        )
    return result[None]


def solution(mesh):
    groups, blocks = mesh.devices.shape
    split = Mesh(mesh.devices.reshape(groups // 4, 2, 2, blocks), ("z", "y", "core", "blk"))
    fsdp = ("z", "y", "core")
    return jax.shard_map(
        per_device,
        mesh=split,
        in_specs=(
            P(fsdp, "blk", None),
            P(fsdp, "blk", None),
            P(fsdp, "blk", None),
            P(fsdp, None),
            P(),
            P(fsdp),
            P(fsdp, "blk", None),
            P(fsdp, "blk"),
        ),
        out_specs=P(fsdp, "blk", None),
        check_vma=False,
    )
```

```python
import functools

import jax
import jax.numpy as jnp
from jax import lax
from jax.experimental import pallas as pl
from jax.experimental.pallas import tpu as pltpu
from jax.sharding import Mesh
from jax.sharding import PartitionSpec as P

HQ = 32
KVH = 4
HD = 128
SHARED = HQ // KVH
BLOCK = 512
RESP_DEV = 2
RLEN = 64
ROWS = RESP_DEV * RLEN
PAIR = 2 * ROWS
GROUP = SHARED * HD
SCALE = HD ** (-0.5) * 1.4426950408889634
HIDDEN = -1e30
NT = (((1,), (1,)), ((), ()))
HINT = pl.CostEstimate(flops=1024, bytes_accessed=1024, transcendentals=0)
LONG = pl.CostEstimate(flops=2**33, bytes_accessed=2**23, transcendentals=2**22)

CHUNKS = ((0, 2), (2, 1), (3, 1))
HELP = (3, 4, 4)


def pair_scores(keys, q_ref, g):
    heads = [q_ref[:, i * HD : (i + 1) * HD] for i in (g, g + 1)]
    scores = lax.dot_general(keys, jnp.concatenate(heads, axis=0), NT, preferred_element_type=jnp.float32)
    return scores * SCALE


def prompt_kernel(first, info, q_ref, k_ref, v_ref, *refs):
    if first:
        acc_ref, ml_ref = refs
    else:
        old_acc, old_ml, acc_ref, ml_ref = refs
    count = k_ref.shape[0]
    place = info[0] + lax.broadcasted_iota(jnp.int32, (count, PAIR), 0)
    lane = lax.broadcasted_iota(jnp.int32, (count, PAIR), 1)
    listed = jnp.where(lane % ROWS < RLEN, info[2], info[3])
    bias = jnp.where((place < info[1]) & (listed == 1), 0.0, HIDDEN)
    keys = k_ref[...]
    values = v_ref[...].T
    for g in range(0, SHARED, 2):
        cols = slice(g * HD, (g + 2) * HD)
        scores = pair_scores(keys, q_ref, g) + bias
        largest = jnp.max(scores, axis=0, keepdims=True)
        if not first:
            before = old_ml[0:1, cols]
            largest = jnp.maximum(largest, before)
            faded = jnp.exp2(before - largest)
        weights = jnp.exp2(scores - largest)
        total = jnp.sum(weights, axis=0, keepdims=True)
        acc = jnp.dot(values, weights.astype(jnp.bfloat16), preferred_element_type=jnp.float32)
        if not first:
            total = total + faded * old_ml[1:2, cols]
            acc = acc + faded * old_acc[:, cols]
        acc_ref[:, cols] = acc
        ml_ref[0:1, cols] = largest
        ml_ref[1:2, cols] = total


def prompt_attention(info, query, cache, state, head, heads, offset=0):
    count = cache.shape[0]
    first = state is None
    wide = pl.BlockSpec((ROWS, GROUP), lambda k, s: (0, head + k))
    turned = pl.BlockSpec((HD, SHARED * ROWS), lambda k, s: (0, k))
    small = pl.BlockSpec((8, SHARED * ROWS), lambda k, s: (0, k))
    specs = [
        wide,
        pl.BlockSpec((count, HD), lambda k, s: (0, head + k)),
        pl.BlockSpec((count, HD), lambda k, s: (0, KVH + head + k)),
    ]
    operands = [query, cache, cache]
    if not first:
        specs += [
            pl.BlockSpec((HD, SHARED * ROWS), lambda k, s: (0, offset + k)),
            pl.BlockSpec((8, SHARED * ROWS), lambda k, s: (0, offset + k)),
        ]
        operands += list(state)
    return pl.pallas_call(
        functools.partial(prompt_kernel, first),
        grid_spec=pltpu.PrefetchScalarGridSpec(
            num_scalar_prefetch=1, grid=(heads,), in_specs=specs, out_specs=[turned, small]
        ),
        out_shape=[
            jax.ShapeDtypeStruct((HD, heads * SHARED * ROWS), jnp.float32),
            jax.ShapeDtypeStruct((8, heads * SHARED * ROWS), jnp.float32),
        ],
        compiler_params=pltpu.CompilerParams(vmem_limit_bytes=32 * 2**20),
        cost_estimate=LONG,
        name="prompt_attention",
    )(info, *operands)


VMEM = pl.BlockSpec(memory_space=pltpu.VMEM)
SMEM = pl.BlockSpec(memory_space=pltpu.SMEM)
PARAMS = pltpu.CompilerParams(vmem_limit_bytes=32 * 2**20)


def on_chip(kernel, name, outs, scalars, *operands, scratch=()):
    return pl.pallas_call(
        kernel,
        in_specs=[SMEM] + [VMEM] * len(operands),
        out_specs=[VMEM] * len(outs),
        out_shape=outs,
        scratch_shapes=scratch,
        compiler_params=PARAMS,
        cost_estimate=HINT,
        name=name,
    )(scalars, *operands)


def pack_rows_kernel(where, own_ref, got_ref, keep, send):
    steps, part = keep.shape[1], keep.shape[3]
    for z in range(steps):
        for out, y in ((keep, where[1]), (send, 1 - where[1])):
            columns = pl.ds(pl.multiple_of((2 * z + y) * part, 128), part)
            out[0, z] = own_ref[:, columns]
            out[1, z] = got_ref[:, columns]


def pack_rows(where, own, got, y, steps):
    part = own.shape[1] // (2 * steps)
    if part % 128:
        halves = jnp.stack([own, got]).reshape(2, ROWS, steps, 2, part)
        halves = jnp.transpose(halves, (3, 0, 2, 1, 4))
        return [lax.dynamic_index_in_dim(halves, i, axis=0, keepdims=False) for i in (y, 1 - y)]
    outs = [jax.ShapeDtypeStruct((2, steps, ROWS, part), own.dtype)] * 2
    return on_chip(pack_rows_kernel, "pack_rows", outs, where, own, got)


def row_split(rows, i):
    helped = rows * HELP[i] // 10
    return helped, rows - helped


def columns_of(chunk):
    return slice(chunk[0] * HD, (chunk[0] + chunk[1]) * HD)


def pack_weight_kernel(where, own_ref, got_ref, *outs):
    rows = own_ref.shape[0]
    core, plane = where[2], where[3]
    half = pl.ds(pl.multiple_of(core * KVH * HD, 128), KVH * HD)
    own, got = own_ref[:, half], got_ref[:, half]
    for whole, far, chunk in zip(outs[0::2], outs[1::2], CHUNKS):
        whole[pl.ds(pl.multiple_of(core * rows, 16), rows), :] = own[:, columns_of(chunk)]
        whole[pl.ds(pl.multiple_of((1 - core) * rows, 16), rows), :] = got[:, columns_of(chunk)]
        direct = far.shape[0]
        far[...] = whole[pl.ds(pl.multiple_of(plane * (2 * rows - direct), 16), direct), :]


def pack_weight(where, own, got):
    rows = 2 * own.shape[0]
    shapes = []
    for i, (_, heads) in enumerate(CHUNKS):
        shapes += [(rows, heads * HD), (row_split(rows, i)[1], heads * HD)]
    outs = [jax.ShapeDtypeStruct(shape, own.dtype) for shape in shapes]
    outs = on_chip(pack_weight_kernel, "pack_weight", outs, where, own, got)
    return list(outs[0::2]), list(outs[1::2])


def project_kernel(where, keep, other, own, near, forwarded, *refs):
    direct, mine, theirs, whole = refs[:-3], refs[-3], refs[-2], refs[-1]
    plane = where[3]
    count, extra = direct[0].shape[0], forwarded.shape[1]
    total = None
    for j in range(2 + len(direct)):
        if j == 0:
            weight = own[...]
        elif j == 1:
            weight = near[...]
        else:
            far = whole.at[j - 2]
            far[pl.ds(pl.multiple_of(plane * extra, 16), count), :] = direct[j - 2][...]
            far[pl.ds(pl.multiple_of((1 - plane) * count, 16), extra), :] = forwarded[j - 2]
            weight = far[...]
        place = where[0] ^ j
        left = jnp.concatenate([x[core, place] for x in (keep, other) for core in range(2)], axis=0)
        product = jnp.dot(left, weight, preferred_element_type=jnp.float32)
        total = product if total is None else total + product
    for i in range(2):
        mine[i] = total[i * ROWS : (i + 1) * ROWS]
        theirs[i] = total[(2 + i) * ROWS : (3 + i) * ROWS]


def project(where, keep, other, own, near, direct, forwarded):
    width = own.shape[1]
    out = jax.ShapeDtypeStruct((2, ROWS, width), jnp.float32)
    return on_chip(
        project_kernel,
        "project",
        [out, out],
        where,
        keep,
        other,
        own,
        near,
        forwarded,
        *direct,
        scratch=[pltpu.VMEM((len(direct), own.shape[0], width), jnp.bfloat16)],
    )


def final_kernel(chunk, offset, info, gain_ref, q_ref, acc_ref, ml_ref, mine, theirs, there, *refs):
    result, built, sem = refs[-3:]
    head, heads = chunk
    slot = lax.broadcasted_iota(jnp.int32, (ROWS, PAIR), 0)
    row = lax.broadcasted_iota(jnp.int32, (ROWS, PAIR), 1) % ROWS
    length = jnp.where(row < RLEN, info[0], info[1])
    base = jnp.where(row < RLEN, 0, RLEN)
    seen = (slot >= base) & (slot <= row) & (slot - base < length)
    live = jnp.where(row - base < length, 1.0, 0.0)[0:1]
    copies = []
    for k in range(heads):
        part = slice(k * HD, (k + 1) * HD)
        here = mine[0, :, part] + theirs[0, :, part]
        away = there[0, :, part] if there.shape[0] == 1 else there[0, :, part] + there[1, :, part]
        first_core = jnp.full(here.shape, info[2]) == 0
        raw = jnp.where(first_core, here, away)
        mean = jnp.mean(raw * raw, axis=1, keepdims=True)
        keys = (raw * lax.rsqrt(mean + 1e-06) * gain_ref[...]).astype(jnp.bfloat16)
        values = jnp.where(first_core, away, here).T.astype(jnp.bfloat16)
        for g in range(0, SHARED, 2):
            cols = slice(((offset + k) * SHARED + g) * HD, ((offset + k) * SHARED + g + 2) * HD)
            scores = jnp.where(seen, pair_scores(keys, q_ref, (head + k) * SHARED + g), HIDDEN)
            before = ml_ref[0:1, cols]
            largest = jnp.maximum(jnp.max(scores, axis=0, keepdims=True), before)
            faded = jnp.exp2(before - largest)
            weights = jnp.exp2(scores - largest)
            total = jnp.sum(weights, axis=0, keepdims=True) + faded * ml_ref[1:2, cols]
            acc = jnp.dot(values, weights.astype(jnp.bfloat16), preferred_element_type=jnp.float32)
            acc = (acc + faded * acc_ref[:, cols]) * (live / total)
            built[k, :, g * HD : (g + 1) * HD] = acc[:, :ROWS].T.astype(jnp.bfloat16)
            built[k, :, (g + 1) * HD : (g + 2) * HD] = acc[:, ROWS:].T.astype(jnp.bfloat16)
        place = result.at[:, pl.ds((head + k) * GROUP, GROUP)]
        copies.append(pltpu.make_async_copy(built.at[k], place, sem.at[k]))
        copies[-1].start()
    for copy in copies:
        copy.wait()


def final_attention(info, gain, query, state, offset, chunk, mine, theirs, there, result):
    heads = chunk[1]
    operands = [gain, query, *state, mine, theirs, there]
    specs = [SMEM] + [VMEM] * len(operands)
    aliases = {}
    if result is not None:
        operands.append(result)
        specs.append(pl.BlockSpec(memory_space=pl.ANY))
        aliases = {len(operands): 0}
    return pl.pallas_call(
        functools.partial(final_kernel, chunk, offset),
        in_specs=specs,
        out_specs=pl.BlockSpec(memory_space=pl.ANY),
        out_shape=jax.ShapeDtypeStruct((ROWS, HQ * HD), jnp.bfloat16),
        scratch_shapes=[pltpu.VMEM((heads, ROWS, GROUP), jnp.bfloat16), pltpu.SemaphoreType.DMA((heads,))],
        input_output_aliases=aliases,
        compiler_params=PARAMS,
        cost_estimate=HINT,
        name="final_attention",
    )(info, *operands)


def xor_swap(array, axis, by):
    return lax.ppermute(array, axis, [(i, i ^ by) for i in range(lax.axis_size(axis))])


def per_device(
    x_resp, queries, prompt_cache, kv_weight, key_gain, prompt_lengths, block_table, resp_lengths
):
    x, query = x_resp[0], queries[0]
    steps = lax.axis_size("z")
    z, y, core = lax.axis_index("z"), lax.axis_index("y"), lax.axis_index("core")
    holder, cycle = lax.axis_index("blk"), lax.axis_size("blk")
    plane = holder % 2
    where = jnp.stack([z, y, core, plane]).astype(jnp.int32)

    tie = lax.optimization_barrier

    got_weight = xor_swap(kv_weight, "core", 1)
    got_x = xor_swap(x, "core", 1)
    caches = [prompt_cache[0]]
    for _ in range(cycle - 1):
        caches.append(lax.ppermute(caches[-1], "blk", [(i, (i + 1) % cycle) for i in range(cycle)]))

    whole, far = pack_weight(where, kv_weight, got_weight)

    def send(whole, far):
        return xor_swap(whole, "z", 1), [xor_swap(far, "z", j) for j in range(2, steps)]

    def forward(i):
        helped, direct = row_split(whole[0].shape[0], i)
        parts = [lax.dynamic_slice_in_dim(p, plane * (direct - helped), helped, axis=0) for p in sent[i][1]]
        return xor_swap(jnp.stack(parts), "blk", 1)

    sent = [send(whole[0], far[0])]
    keep, given = pack_rows(where, x, got_x, y, steps)
    other = xor_swap(given, "y", 1)

    infos = []
    for stride in range(cycle):
        owner = lax.rem(holder + cycle - stride, cycle)
        place = owner * prompt_cache.shape[1]
        listed = lax.dynamic_index_in_dim(block_table[0], place // BLOCK, axis=1, keepdims=False)
        infos.append(jnp.concatenate([place[None], prompt_lengths, listed]).astype(jnp.int32))

    def rest(head, heads, state, offset):
        for stride in range(1, cycle):
            state = prompt_attention(infos[stride], query, caches[stride], state, head, heads, offset)
            offset = 0
        return state

    query, _, _ = tie((query, whole[0], given))
    state = prompt_attention(infos[0], query, caches[0], None, 0, KVH)

    sent[0], caches, state, next_chunk = tie((sent[0], caches, state, (whole[1], far[1])))
    sent.append(send(*next_chunk))
    forwarded = [forward(0)]
    halves = [rest(0, 2, state, 0)]
    sent[1], forwarded[0], halves[0], next_chunk = tie((sent[1], forwarded[0], halves[0], (whole[2], far[2])))
    sent.append(send(*next_chunk))
    forwarded.append(forward(1))

    def sums(i):
        return project(where, keep, other, whole[i], *sent[i], forwarded[i])

    info = jnp.concatenate([resp_lengths[0], core[None]]).astype(jnp.int32)
    gain = key_gain[None]
    mine_0, theirs_0 = sums(0)
    theirs_0 = xor_swap(theirs_0, "y", 1)
    mine_0, forwarded[1] = tie((mine_0, forwarded[1]))
    mine_1, theirs_1 = sums(1)
    theirs_1 = xor_swap(theirs_1, "y", 1)
    sent[2], mine_1, state = tie((sent[2], mine_1, state))
    forwarded.append(forward(2))
    halves.append(rest(2, 2, state, 2))
    theirs_0, theirs_1, halves[1] = tie((theirs_0, theirs_1, halves[1]))
    there_0 = xor_swap(mine_0[1:] + theirs_0[1:], "core", 1)
    there_1 = xor_swap(mine_1[1:] + theirs_1[1:], "core", 1)
    result = final_attention(info, gain, query, halves[0], 0, CHUNKS[0], mine_0, theirs_0, there_0, None)
    mine_2, theirs_2 = sums(2)
    there_2 = [xor_swap(mine_2[1], "core", 1), xor_swap(theirs_2[1], ("y", "core"), 3)]
    theirs_2 = xor_swap(theirs_2[:1], "y", 1)
    result = final_attention(info, gain, query, halves[1], 0, CHUNKS[1], mine_1, theirs_1, there_1, result)
    result = final_attention(
        info, gain, query, halves[1], 1, CHUNKS[2], mine_2, theirs_2, jnp.stack(there_2), result
    )
    return result[None]


def solution(mesh):
    groups, blocks = mesh.devices.shape
    split = Mesh(mesh.devices.reshape(groups // 4, 2, 2, blocks), ("z", "y", "core", "blk"))
    fsdp = ("z", "y", "core")
    return jax.shard_map(
        per_device,
        mesh=split,
        in_specs=(
            P(fsdp, "blk", None),
            P(fsdp, "blk", None),
            P(fsdp, "blk", None),
            P(fsdp, None),
            P(),
            P(fsdp),
            P(fsdp, "blk", None),
            P(fsdp, "blk"),
        ),
        out_specs=P(fsdp, "blk", None),
        check_vma=False,
    )
```

```python
import functools

import jax
import jax.numpy as jnp
from jax import lax
from jax.experimental import pallas as pl
from jax.experimental.pallas import tpu as pltpu
from jax.sharding import Mesh
from jax.sharding import PartitionSpec as P

HQ = 32
KVH = 4
HD = 128
SHARED = HQ // KVH
BLOCK = 512
RESP_DEV = 2
RLEN = 64
ROWS = RESP_DEV * RLEN
PAIR = 2 * ROWS
GROUP = SHARED * HD
SCALE = HD ** (-0.5) * 1.4426950408889634
HIDDEN = -1e30
NT = (((1,), (1,)), ((), ()))
HINT = pl.CostEstimate(flops=1024, bytes_accessed=1024, transcendentals=0)
LONG = pl.CostEstimate(flops=2**32, bytes_accessed=1024, transcendentals=0)

CHUNKS = ((0, 2), (2, 2))
HELP = (4, 5)


def pair_queries(q_ref, g, extra=None):
    heads = [q_ref[:, i * HD : (i + 1) * HD] for i in (g, g + 1)]
    if extra is not None:
        heads = [jnp.concatenate([head, extra], axis=1) for head in heads]
    return jnp.concatenate(heads, axis=0)


def scores_of(keys, queries):
    return lax.dot_general(keys, queries, NT, preferred_element_type=jnp.float32)


def prompt_kernel(first, info, q_ref, k_ref, v_ref, *refs):
    if first:
        acc_ref, ml_ref = refs
    else:
        old_acc, old_ml, acc_ref, ml_ref = refs
    count = k_ref.shape[0]
    place = info[0] + lax.broadcasted_iota(jnp.int32, (count, HD), 0)
    column = lax.broadcasted_iota(jnp.int32, (count, HD), 1)
    listed = jnp.where(column == 0, info[2], info[3])
    hidden = (column < RESP_DEV) & ((place >= info[1]) | (listed != 1))
    keys = jnp.concatenate([k_ref[...], jnp.where(hidden, HIDDEN, 0.0).astype(jnp.bfloat16)], axis=1)
    owner = lax.broadcasted_iota(jnp.int32, (ROWS, HD), 0) // RLEN
    ours = jnp.where(owner == lax.broadcasted_iota(jnp.int32, (ROWS, HD), 1), 1.0, 0.0).astype(jnp.bfloat16)
    values = v_ref[...].T
    ahead = scores_of(keys, pair_queries(q_ref, 0, ours))
    for g in range(0, SHARED, 2):
        cols = slice(g * HD, (g + 2) * HD)
        scores = ahead
        if g + 2 < SHARED:
            ahead = scores_of(keys, pair_queries(q_ref, g + 2, ours))
        largest = jnp.max(scores, axis=0, keepdims=True)
        if not first:
            before = old_ml[0:1, cols]
            largest = jnp.maximum(largest, before)
            faded = jnp.exp2((before - largest) * SCALE)
        weights = jnp.exp2((scores - largest) * SCALE)
        total = jnp.sum(weights, axis=0, keepdims=True)
        acc = jnp.dot(values, weights.astype(jnp.bfloat16), preferred_element_type=jnp.float32)
        if not first:
            total = total + faded * old_ml[1:2, cols]
            acc = acc + faded * old_acc[:, cols]
        acc_ref[:, cols] = acc
        ml_ref[0:1, cols] = largest
        ml_ref[1:2, cols] = total


def prompt_attention(info, query, cache, state, head, heads, offset=0):
    count = cache.shape[0]
    first = state is None
    wide = pl.BlockSpec((ROWS, GROUP), lambda k, s: (0, head + k))
    turned = pl.BlockSpec((HD, SHARED * ROWS), lambda k, s: (0, k))
    small = pl.BlockSpec((8, SHARED * ROWS), lambda k, s: (0, k))
    specs = [
        wide,
        pl.BlockSpec((count, HD), lambda k, s: (0, head + k)),
        pl.BlockSpec((count, HD), lambda k, s: (0, KVH + head + k)),
    ]
    operands = [query, cache, cache]
    if not first:
        specs += [
            pl.BlockSpec((HD, SHARED * ROWS), lambda k, s: (0, offset + k)),
            pl.BlockSpec((8, SHARED * ROWS), lambda k, s: (0, offset + k)),
        ]
        operands += list(state)
    return pl.pallas_call(
        functools.partial(prompt_kernel, first),
        grid_spec=pltpu.PrefetchScalarGridSpec(
            num_scalar_prefetch=1, grid=(heads,), in_specs=specs, out_specs=[turned, small]
        ),
        out_shape=[
            jax.ShapeDtypeStruct((HD, heads * SHARED * ROWS), jnp.float32),
            jax.ShapeDtypeStruct((8, heads * SHARED * ROWS), jnp.float32),
        ],
        compiler_params=pltpu.CompilerParams(vmem_limit_bytes=32 * 2**20),
        cost_estimate=LONG,
        name="prompt_attention",
    )(info, *operands)


VMEM = pl.BlockSpec(memory_space=pltpu.VMEM)
SMEM = pl.BlockSpec(memory_space=pltpu.SMEM)
PARAMS = pltpu.CompilerParams(vmem_limit_bytes=32 * 2**20)


def on_chip(kernel, name, outs, scalars, *operands, scratch=()):
    return pl.pallas_call(
        kernel,
        in_specs=[SMEM] + [VMEM] * len(operands),
        out_specs=[VMEM] * len(outs),
        out_shape=outs,
        scratch_shapes=scratch,
        compiler_params=PARAMS,
        cost_estimate=HINT,
        name=name,
    )(scalars, *operands)


def pack_rows_kernel(where, own_ref, got_ref, keep, send):
    steps, part = keep.shape[1], keep.shape[3]
    for z in range(steps):
        for out, y in ((keep, where[1]), (send, 1 - where[1])):
            columns = pl.ds(pl.multiple_of((2 * z + y) * part, 128), part)
            out[0, z] = own_ref[:, columns]
            out[1, z] = got_ref[:, columns]


def pack_rows(where, own, got, y, steps):
    part = own.shape[1] // (2 * steps)
    if part % 128:
        halves = jnp.stack([own, got]).reshape(2, ROWS, steps, 2, part)
        halves = jnp.transpose(halves, (3, 0, 2, 1, 4))
        return [lax.dynamic_index_in_dim(halves, i, axis=0, keepdims=False) for i in (y, 1 - y)]
    outs = [jax.ShapeDtypeStruct((2, steps, ROWS, part), own.dtype)] * 2
    return on_chip(pack_rows_kernel, "pack_rows", outs, where, own, got)


def row_split(rows, i):
    helped = rows * HELP[i] // 10
    return helped, rows - helped


def columns_of(chunk):
    return slice(chunk[0] * HD, (chunk[0] + chunk[1]) * HD)


def pack_weight_kernel(where, own_ref, got_ref, *outs):
    rows = own_ref.shape[0]
    core, plane = where[2], where[3]
    half = pl.ds(pl.multiple_of(core * KVH * HD, 128), KVH * HD)
    own, got = own_ref[:, half], got_ref[:, half]
    for whole, far, chunk in zip(outs[0::2], outs[1::2], CHUNKS):
        whole[pl.ds(pl.multiple_of(core * rows, 16), rows), :] = own[:, columns_of(chunk)]
        whole[pl.ds(pl.multiple_of((1 - core) * rows, 16), rows), :] = got[:, columns_of(chunk)]
        direct = far.shape[0]
        far[...] = whole[pl.ds(pl.multiple_of(plane * (2 * rows - direct), 16), direct), :]


def pack_weight(where, own, got):
    rows = 2 * own.shape[0]
    shapes = []
    for i, (_, heads) in enumerate(CHUNKS):
        shapes += [(rows, heads * HD), (row_split(rows, i)[1], heads * HD)]
    outs = [jax.ShapeDtypeStruct(shape, own.dtype) for shape in shapes]
    outs = on_chip(pack_weight_kernel, "pack_weight", outs, where, own, got)
    return list(outs[0::2]), list(outs[1::2])


def project_kernel(where, keep, other, own, near, forwarded, *refs):
    direct, mine, theirs, whole = refs[:-3], refs[-3], refs[-2], refs[-1]
    plane = where[3]
    count, extra = direct[0].shape[0], forwarded.shape[1]
    total = None
    for j in range(2 + len(direct)):
        if j == 0:
            weight = own[...]
        elif j == 1:
            weight = near[...]
        else:
            far = whole.at[j - 2]
            far[pl.ds(pl.multiple_of(plane * extra, 16), count), :] = direct[j - 2][...]
            far[pl.ds(pl.multiple_of((1 - plane) * count, 16), extra), :] = forwarded[j - 2]
            weight = far[...]
        place = where[0] ^ j
        left = jnp.concatenate([x[core, place] for x in (keep, other) for core in range(2)], axis=0)
        product = jnp.dot(left, weight, preferred_element_type=jnp.float32)
        total = product if total is None else total + product
    for i in range(2):
        mine[i] = total[i * ROWS : (i + 1) * ROWS]
        theirs[i] = total[(2 + i) * ROWS : (3 + i) * ROWS]


def project(where, keep, other, own, near, direct, forwarded):
    width = own.shape[1]
    out = jax.ShapeDtypeStruct((2, ROWS, width), jnp.float32)
    return on_chip(
        project_kernel,
        "project",
        [out, out],
        where,
        keep,
        other,
        own,
        near,
        forwarded,
        *direct,
        scratch=[pltpu.VMEM((len(direct), own.shape[0], width), jnp.bfloat16)],
    )


def final_kernel(chunk, offset, info, gain_ref, q_ref, acc_ref, ml_ref, mine, theirs, there, *refs):
    result, built, sem = refs[-3:]
    head, heads = chunk
    slot = lax.broadcasted_iota(jnp.int32, (ROWS, PAIR), 0)
    row = lax.broadcasted_iota(jnp.int32, (ROWS, PAIR), 1) % ROWS
    length = jnp.where(row < RLEN, info[0], info[1])
    base = jnp.where(row < RLEN, 0, RLEN)
    seen = (slot >= base) & (slot <= row) & (slot - base < length)
    live = jnp.where(row - base < length, 1.0, 0.0)[0:1]
    copies = []
    for k in range(heads):
        part = slice(k * HD, (k + 1) * HD)
        here = mine[0, :, part] + theirs[0, :, part]
        away = there[0, :, part] if there.shape[0] == 1 else there[0, :, part] + there[1, :, part]
        first_core = jnp.full(here.shape, info[2]) == 0
        raw = jnp.where(first_core, here, away)
        mean = jnp.mean(raw * raw, axis=1, keepdims=True)
        keys = (raw * lax.rsqrt(mean + 1e-06) * gain_ref[...]).astype(jnp.bfloat16)
        values = jnp.where(first_core, away, here).T.astype(jnp.bfloat16)
        pairs = range(0, SHARED, 2)
        products = [scores_of(keys, pair_queries(q_ref, (head + k) * SHARED + g)) for g in pairs]
        for g, scores in zip(pairs, products):
            cols = slice(((offset + k) * SHARED + g) * HD, ((offset + k) * SHARED + g + 2) * HD)
            scores = jnp.where(seen, scores, HIDDEN)
            before = ml_ref[0:1, cols]
            largest = jnp.maximum(jnp.max(scores, axis=0, keepdims=True), before)
            faded = jnp.exp2((before - largest) * SCALE)
            weights = jnp.exp2((scores - largest) * SCALE)
            total = jnp.sum(weights, axis=0, keepdims=True) + faded * ml_ref[1:2, cols]
            acc = jnp.dot(values, weights.astype(jnp.bfloat16), preferred_element_type=jnp.float32)
            acc = (acc + faded * acc_ref[:, cols]) * (live / total)
            built[k, :, g * HD : (g + 1) * HD] = acc[:, :ROWS].T.astype(jnp.bfloat16)
            built[k, :, (g + 1) * HD : (g + 2) * HD] = acc[:, ROWS:].T.astype(jnp.bfloat16)
        place = result.at[:, pl.ds((head + k) * GROUP, GROUP)]
        copies.append(pltpu.make_async_copy(built.at[k], place, sem.at[k]))
        copies[-1].start()
    for copy in copies:
        copy.wait()


def final_attention(info, gain, query, state, offset, chunk, mine, theirs, there, result):
    heads = chunk[1]
    operands = [gain, query, *state, mine, theirs, there]
    specs = [SMEM] + [VMEM] * len(operands)
    aliases = {}
    if result is not None:
        operands.append(result)
        specs.append(pl.BlockSpec(memory_space=pl.ANY))
        aliases = {len(operands): 0}
    return pl.pallas_call(
        functools.partial(final_kernel, chunk, offset),
        in_specs=specs,
        out_specs=pl.BlockSpec(memory_space=pl.ANY),
        out_shape=jax.ShapeDtypeStruct((ROWS, HQ * HD), jnp.bfloat16),
        scratch_shapes=[pltpu.VMEM((heads, ROWS, GROUP), jnp.bfloat16), pltpu.SemaphoreType.DMA((heads,))],
        input_output_aliases=aliases,
        compiler_params=PARAMS,
        cost_estimate=HINT,
        name="final_attention",
    )(info, *operands)


def xor_swap(array, axis, by):
    return lax.ppermute(array, axis, [(i, i ^ by) for i in range(lax.axis_size(axis))])


def per_device(
    x_resp, queries, prompt_cache, kv_weight, key_gain, prompt_lengths, block_table, resp_lengths
):
    x, query = x_resp[0], queries[0]
    steps = lax.axis_size("z")
    z, y, core = lax.axis_index("z"), lax.axis_index("y"), lax.axis_index("core")
    holder, cycle = lax.axis_index("blk"), lax.axis_size("blk")
    plane = holder % 2
    where = jnp.stack([z, y, core, plane]).astype(jnp.int32)

    tie = lax.optimization_barrier

    got_weight = xor_swap(kv_weight, "core", 1)
    got_x = xor_swap(x, "core", 1)
    caches = [prompt_cache[0]]
    for _ in range(cycle - 1):
        caches.append(lax.ppermute(caches[-1], "blk", [(i, (i + 1) % cycle) for i in range(cycle)]))

    whole, far = pack_weight(where, kv_weight, got_weight)

    def send(whole, far):
        return xor_swap(whole, "z", 1), [xor_swap(far, "z", j) for j in range(2, steps)]

    def forward(i):
        helped, direct = row_split(whole[0].shape[0], i)
        parts = [lax.dynamic_slice_in_dim(p, plane * (direct - helped), helped, axis=0) for p in sent[i][1]]
        return xor_swap(jnp.stack(parts), "blk", 1)

    sent = [send(whole[0], far[0])]
    keep, given = pack_rows(where, x, got_x, y, steps)
    other = xor_swap(given, "y", 1)

    infos = []
    for stride in range(cycle):
        owner = lax.rem(holder + cycle - stride, cycle)
        place = owner * prompt_cache.shape[1]
        listed = lax.dynamic_index_in_dim(block_table[0], place // BLOCK, axis=1, keepdims=False)
        infos.append(jnp.concatenate([place[None], prompt_lengths, listed]).astype(jnp.int32))

    query, _, _ = tie((query, whole[0], given))
    state = prompt_attention(infos[0], query, caches[0], None, 0, KVH)

    sent[0], caches, state, second = tie((sent[0], caches, state, (whole[1], far[1])))
    sent.append(send(*second))
    forwarded = [forward(0)]
    for stride in range(1, cycle):
        state = prompt_attention(infos[stride], query, caches[stride], state, 0, KVH)
    sent[1], forwarded[0], state = tie((sent[1], forwarded[0], state))
    forwarded.append(forward(1))

    def sums(i):
        return project(where, keep, other, whole[i], *sent[i], forwarded[i])

    info = jnp.concatenate([resp_lengths[0], core[None]]).astype(jnp.int32)
    gain = key_gain[None]
    mine_0, theirs_0 = sums(0)
    theirs_0 = xor_swap(theirs_0, "y", 1)
    forwarded[1], mine_0 = tie((forwarded[1], mine_0))
    mine_1, theirs_1 = sums(1)
    theirs_0, theirs_1 = tie((theirs_0, theirs_1))
    theirs_1 = xor_swap(theirs_1, "y", 1)
    there_0 = xor_swap(mine_0[1:] + theirs_0[1:], "core", 1)
    result = final_attention(info, gain, query, state, 0, CHUNKS[0], mine_0, theirs_0, there_0, None)
    theirs_1, result = tie((theirs_1, result))
    there_1 = xor_swap(mine_1[1:] + theirs_1[1:], "core", 1)
    result = final_attention(info, gain, query, state, 2, CHUNKS[1], mine_1, theirs_1, there_1, result)
    return result[None]


def solution(mesh):
    groups, blocks = mesh.devices.shape
    split = Mesh(mesh.devices.reshape(groups // 4, 2, 2, blocks), ("z", "y", "core", "blk"))
    fsdp = ("z", "y", "core")
    return jax.shard_map(
        per_device,
        mesh=split,
        in_specs=(
            P(fsdp, "blk", None),
            P(fsdp, "blk", None),
            P(fsdp, "blk", None),
            P(fsdp, None),
            P(),
            P(fsdp),
            P(fsdp, "blk", None),
            P(fsdp, "blk"),
        ),
        out_specs=P(fsdp, "blk", None),
        check_vma=False,
    )
```

```python
import functools

import jax
import jax.numpy as jnp
from jax import lax
from jax.experimental import pallas as pl
from jax.experimental.pallas import tpu as pltpu
from jax.sharding import Mesh
from jax.sharding import PartitionSpec as P

HQ = 32
KVH = 4
HD = 128
SHARED = HQ // KVH
BLOCK = 512
RESP_DEV = 2
RLEN = 64
ROWS = RESP_DEV * RLEN
PAIR = 2 * ROWS
GROUP = SHARED * HD
SCALE = HD ** (-0.5) * 1.4426950408889634
HIDDEN = -1e30
NT = (((1,), (1,)), ((), ()))
HINT = pl.CostEstimate(flops=1024, bytes_accessed=1024, transcendentals=0)
LONG = pl.CostEstimate(flops=2**32, bytes_accessed=1024, transcendentals=0)

CHUNKS = ((0, 2), (2, 2))
HELP = (4, 5)


def pair_queries(q_ref, g, extra=None):
    heads = [q_ref[:, i * HD : (i + 1) * HD] for i in (g, g + 1)]
    if extra is not None:
        heads = [jnp.concatenate([head, extra], axis=1) for head in heads]
    return jnp.concatenate(heads, axis=0)


def scores_of(keys, queries):
    return lax.dot_general(keys, queries, NT, preferred_element_type=jnp.float32)


def prompt_kernel(first, info, q_ref, k_ref, v_ref, *refs):
    if first:
        acc_ref, ml_ref = refs
    else:
        old_acc, old_ml, acc_ref, ml_ref = refs
    count = k_ref.shape[0]
    place = info[0] + lax.broadcasted_iota(jnp.int32, (count, HD), 0)
    column = lax.broadcasted_iota(jnp.int32, (count, HD), 1)
    listed = jnp.where(column == 0, info[2], info[3])
    hidden = (column < RESP_DEV) & ((place >= info[1]) | (listed != 1))
    keys = jnp.concatenate([k_ref[...], jnp.where(hidden, HIDDEN, 0.0).astype(jnp.bfloat16)], axis=1)
    owner = lax.broadcasted_iota(jnp.int32, (ROWS, HD), 0) // RLEN
    ours = jnp.where(owner == lax.broadcasted_iota(jnp.int32, (ROWS, HD), 1), 1.0, 0.0).astype(jnp.bfloat16)
    values = v_ref[...].T
    ahead = scores_of(keys, pair_queries(q_ref, 0, ours))
    for g in range(0, SHARED, 2):
        cols = slice(g * HD, (g + 2) * HD)
        scores = ahead
        if g + 2 < SHARED:
            ahead = scores_of(keys, pair_queries(q_ref, g + 2, ours))
        largest = jnp.max(scores, axis=0, keepdims=True)
        if not first:
            before = old_ml[0:1, cols]
            largest = jnp.maximum(largest, before)
            faded = jnp.exp2((before - largest) * SCALE)
        weights = jnp.exp2((scores - largest) * SCALE)
        total = jnp.sum(weights, axis=0, keepdims=True)
        acc = jnp.dot(values, weights.astype(jnp.bfloat16), preferred_element_type=jnp.float32)
        if not first:
            total = total + faded * old_ml[1:2, cols]
            acc = acc + faded * old_acc[:, cols]
        acc_ref[:, cols] = acc
        ml_ref[0:1, cols] = largest
        ml_ref[1:2, cols] = total


def prompt_attention(info, query, cache, state, head, heads, offset=0):
    count = cache.shape[0]
    first = state is None
    wide = pl.BlockSpec((ROWS, GROUP), lambda k, s: (0, head + k))
    turned = pl.BlockSpec((HD, SHARED * ROWS), lambda k, s: (0, k))
    small = pl.BlockSpec((8, SHARED * ROWS), lambda k, s: (0, k))
    specs = [
        wide,
        pl.BlockSpec((count, HD), lambda k, s: (0, head + k)),
        pl.BlockSpec((count, HD), lambda k, s: (0, KVH + head + k)),
    ]
    operands = [query, cache, cache]
    if not first:
        specs += [
            pl.BlockSpec((HD, SHARED * ROWS), lambda k, s: (0, offset + k)),
            pl.BlockSpec((8, SHARED * ROWS), lambda k, s: (0, offset + k)),
        ]
        operands += list(state)
    return pl.pallas_call(
        functools.partial(prompt_kernel, first),
        grid_spec=pltpu.PrefetchScalarGridSpec(
            num_scalar_prefetch=1, grid=(heads,), in_specs=specs, out_specs=[turned, small]
        ),
        out_shape=[
            jax.ShapeDtypeStruct((HD, heads * SHARED * ROWS), jnp.float32),
            jax.ShapeDtypeStruct((8, heads * SHARED * ROWS), jnp.float32),
        ],
        compiler_params=pltpu.CompilerParams(vmem_limit_bytes=32 * 2**20),
        cost_estimate=LONG,
        name="prompt_attention",
    )(info, *operands)


VMEM = pl.BlockSpec(memory_space=pltpu.VMEM)
SMEM = pl.BlockSpec(memory_space=pltpu.SMEM)
PARAMS = pltpu.CompilerParams(vmem_limit_bytes=32 * 2**20)


def on_chip(kernel, name, outs, scalars, *operands, scratch=()):
    return pl.pallas_call(
        kernel,
        in_specs=[SMEM] + [VMEM] * len(operands),
        out_specs=[VMEM] * len(outs),
        out_shape=outs,
        scratch_shapes=scratch,
        compiler_params=PARAMS,
        cost_estimate=HINT,
        name=name,
    )(scalars, *operands)


def pack_rows_kernel(where, own_ref, got_ref, keep, send):
    steps, part = keep.shape[1], keep.shape[3]
    for z in range(steps):
        for out, y in ((keep, where[1]), (send, 1 - where[1])):
            columns = pl.ds(pl.multiple_of((2 * z + y) * part, 128), part)
            out[0, z] = own_ref[:, columns]
            out[1, z] = got_ref[:, columns]


def pack_rows(where, own, got, y, steps):
    part = own.shape[1] // (2 * steps)
    if part % 128:
        halves = jnp.stack([own, got]).reshape(2, ROWS, steps, 2, part)
        halves = jnp.transpose(halves, (3, 0, 2, 1, 4))
        return [lax.dynamic_index_in_dim(halves, i, axis=0, keepdims=False) for i in (y, 1 - y)]
    outs = [jax.ShapeDtypeStruct((2, steps, ROWS, part), own.dtype)] * 2
    return on_chip(pack_rows_kernel, "pack_rows", outs, where, own, got)


def row_split(rows, i):
    helped = rows * HELP[i] // 10
    return helped, rows - helped


def columns_of(chunk):
    return slice(chunk[0] * HD, (chunk[0] + chunk[1]) * HD)


def pack_weight_kernel(where, got_ref, own_ref, whole, *refs):
    far, sem = refs[:-1], refs[-1]
    rows = got_ref.shape[0]
    core, plane = where[2], where[3]
    half = pl.ds(pl.multiple_of(core * KVH * HD, 128), KVH * HD)
    own_place = pl.ds(pl.multiple_of(core * rows, 16), rows)
    copy = pltpu.make_async_copy(own_ref.at[:, half], whole.at[own_place, :], sem)
    copy.start()
    whole[pl.ds(pl.multiple_of((1 - core) * rows, 16), rows), :] = got_ref[:, half]
    copy.wait()
    for out, chunk in zip(far, CHUNKS):
        direct = out.shape[0]
        out[...] = whole[pl.ds(pl.multiple_of(plane * (2 * rows - direct), 16), direct), columns_of(chunk)]


def pack_weight(where, own, got):
    rows = 2 * own.shape[0]
    shapes = [(rows, KVH * HD)] + [(row_split(rows, i)[1], heads * HD) for i, (_, heads) in enumerate(CHUNKS)]
    whole, *far = pl.pallas_call(
        pack_weight_kernel,
        in_specs=[SMEM, VMEM, pl.BlockSpec(memory_space=pltpu.HBM)],
        out_specs=[VMEM] * len(shapes),
        out_shape=[jax.ShapeDtypeStruct(shape, own.dtype) for shape in shapes],
        scratch_shapes=[pltpu.SemaphoreType.DMA],
        compiler_params=PARAMS,
        cost_estimate=HINT,
        name="pack_weight",
    )(where, got, own)
    return whole, far


def project_kernel(columns, where, keep, other, own, near, forwarded, *refs):
    direct, mine, theirs, whole = refs[:-3], refs[-3], refs[-2], refs[-1]
    plane = where[3]
    count, extra = direct[0].shape[0], forwarded.shape[1]
    total = None
    for j in range(2 + len(direct)):
        if j == 0:
            weight = own[:, columns]
        elif j == 1:
            weight = near[:, columns]
        else:
            far = whole.at[j - 2]
            far[pl.ds(pl.multiple_of(plane * extra, 16), count), :] = direct[j - 2][...]
            far[pl.ds(pl.multiple_of((1 - plane) * count, 16), extra), :] = forwarded[j - 2]
            weight = far[...]
        place = where[0] ^ j
        left = jnp.concatenate([x[core, place] for x in (keep, other) for core in range(2)], axis=0)
        product = jnp.dot(left, weight, preferred_element_type=jnp.float32)
        total = product if total is None else total + product
    for i in range(2):
        mine[i] = total[i * ROWS : (i + 1) * ROWS]
        theirs[i] = total[(2 + i) * ROWS : (3 + i) * ROWS]


def project(where, keep, other, chunk, own, near, direct, forwarded):
    width = chunk[1] * HD
    out = jax.ShapeDtypeStruct((2, ROWS, width), jnp.float32)
    return on_chip(
        functools.partial(project_kernel, columns_of(chunk)),
        "project",
        [out, out],
        where,
        keep,
        other,
        own,
        near,
        forwarded,
        *direct,
        scratch=[pltpu.VMEM((len(direct), own.shape[0], width), jnp.bfloat16)],
    )


def final_kernel(chunk, offset, info, gain_ref, q_ref, acc_ref, ml_ref, mine, theirs, there, *refs):
    result, built, sem = refs[-3:]
    head, heads = chunk
    slot = lax.broadcasted_iota(jnp.int32, (ROWS, PAIR), 0)
    row = lax.broadcasted_iota(jnp.int32, (ROWS, PAIR), 1) % ROWS
    length = jnp.where(row < RLEN, info[0], info[1])
    base = jnp.where(row < RLEN, 0, RLEN)
    seen = (slot >= base) & (slot <= row) & (slot - base < length)
    live = jnp.where(row - base < length, 1.0, 0.0)[0:1]
    copies = []
    for k in range(heads):
        part = slice(k * HD, (k + 1) * HD)
        here = mine[0, :, part] + theirs[0, :, part]
        away = there[0, :, part] if there.shape[0] == 1 else there[0, :, part] + there[1, :, part]
        first_core = jnp.full(here.shape, info[2]) == 0
        raw = jnp.where(first_core, here, away)
        mean = jnp.mean(raw * raw, axis=1, keepdims=True)
        keys = (raw * lax.rsqrt(mean + 1e-06) * gain_ref[...]).astype(jnp.bfloat16)
        values = jnp.where(first_core, away, here).T.astype(jnp.bfloat16)
        pairs = range(0, SHARED, 2)
        products = [scores_of(keys, pair_queries(q_ref, (head + k) * SHARED + g)) for g in pairs]
        for g, scores in zip(pairs, products):
            cols = slice(((offset + k) * SHARED + g) * HD, ((offset + k) * SHARED + g + 2) * HD)
            scores = jnp.where(seen, scores, HIDDEN)
            before = ml_ref[0:1, cols]
            largest = jnp.maximum(jnp.max(scores, axis=0, keepdims=True), before)
            faded = jnp.exp2((before - largest) * SCALE)
            weights = jnp.exp2((scores - largest) * SCALE)
            total = jnp.sum(weights, axis=0, keepdims=True) + faded * ml_ref[1:2, cols]
            acc = jnp.dot(values, weights.astype(jnp.bfloat16), preferred_element_type=jnp.float32)
            acc = (acc + faded * acc_ref[:, cols]) * (live / total)
            built[k, :, g * HD : (g + 1) * HD] = acc[:, :ROWS].T.astype(jnp.bfloat16)
            built[k, :, (g + 1) * HD : (g + 2) * HD] = acc[:, ROWS:].T.astype(jnp.bfloat16)
        place = result.at[:, pl.ds((head + k) * GROUP, GROUP)]
        copies.append(pltpu.make_async_copy(built.at[k], place, sem.at[k]))
        copies[-1].start()
    for copy in copies:
        copy.wait()


def final_attention(info, gain, query, state, offset, chunk, mine, theirs, there, result):
    heads = chunk[1]
    operands = [gain, query, *state, mine, theirs, there]
    specs = [SMEM] + [VMEM] * len(operands)
    aliases = {}
    if result is not None:
        operands.append(result)
        specs.append(pl.BlockSpec(memory_space=pl.ANY))
        aliases = {len(operands): 0}
    return pl.pallas_call(
        functools.partial(final_kernel, chunk, offset),
        in_specs=specs,
        out_specs=pl.BlockSpec(memory_space=pl.ANY),
        out_shape=jax.ShapeDtypeStruct((ROWS, HQ * HD), jnp.bfloat16),
        scratch_shapes=[pltpu.VMEM((heads, ROWS, GROUP), jnp.bfloat16), pltpu.SemaphoreType.DMA((heads,))],
        input_output_aliases=aliases,
        compiler_params=PARAMS,
        cost_estimate=HINT,
        name="final_attention",
    )(info, *operands)


def xor_swap(array, axis, by):
    return lax.ppermute(array, axis, [(i, i ^ by) for i in range(lax.axis_size(axis))])


def per_device(
    x_resp, queries, prompt_cache, kv_weight, key_gain, prompt_lengths, block_table, resp_lengths
):
    x, query = x_resp[0], queries[0]
    steps = lax.axis_size("z")
    z, y, core = lax.axis_index("z"), lax.axis_index("y"), lax.axis_index("core")
    holder, cycle = lax.axis_index("blk"), lax.axis_size("blk")
    plane = holder % 2
    where = jnp.stack([z, y, core, plane]).astype(jnp.int32)

    tie = lax.optimization_barrier

    got_weight = xor_swap(kv_weight, "core", 1)
    got_x = xor_swap(x, "core", 1)
    caches = [prompt_cache[0]]
    for _ in range(cycle - 1):
        caches.append(lax.ppermute(caches[-1], "blk", [(i, (i + 1) % cycle) for i in range(cycle)]))

    whole, far = pack_weight(where, kv_weight, got_weight)

    def send(far):
        return [xor_swap(far, "z", j) for j in range(2, steps)]

    def forward(i):
        helped, direct = row_split(whole.shape[0], i)
        parts = [lax.dynamic_slice_in_dim(p, plane * (direct - helped), helped, axis=0) for p in sent[i]]
        return xor_swap(jnp.stack(parts), "blk", 1)

    sent = [send(far[0])]
    near = xor_swap(whole, "z", 1)
    keep, given = pack_rows(where, x, got_x, y, steps)
    other = xor_swap(given, "y", 1)

    block_table, _ = tie((block_table, whole))
    infos = []
    for stride in range(cycle):
        owner = lax.rem(holder + cycle - stride, cycle)
        place = owner * prompt_cache.shape[1]
        listed = lax.dynamic_index_in_dim(block_table[0], place // BLOCK, axis=1, keepdims=False)
        infos.append(jnp.concatenate([place[None], prompt_lengths, listed]).astype(jnp.int32))

    query, _, _ = tie((query, whole, given))
    state = prompt_attention(infos[0], query, caches[0], None, 0, KVH)

    sent[0], caches, state, far[1] = tie((sent[0], caches, state, far[1]))
    sent.append(send(far[1]))
    forwarded = [forward(0)]
    for stride in range(1, cycle):
        state = prompt_attention(infos[stride], query, caches[stride], state, 0, KVH)
    sent[1], forwarded[0], state = tie((sent[1], forwarded[0], state))
    forwarded.append(forward(1))

    def sums(i):
        return project(where, keep, other, CHUNKS[i], whole, near, sent[i], forwarded[i])

    info = jnp.concatenate([resp_lengths[0], core[None]]).astype(jnp.int32)
    gain = key_gain[None]
    mine_0, theirs_0 = sums(0)
    theirs_0 = xor_swap(theirs_0, "y", 1)
    forwarded[1], mine_0 = tie((forwarded[1], mine_0))
    mine_1, theirs_1 = sums(1)
    theirs_0, theirs_1 = tie((theirs_0, theirs_1))
    theirs_1 = xor_swap(theirs_1, "y", 1)
    there_0 = xor_swap(mine_0[1:] + theirs_0[1:], "core", 1)
    result = final_attention(info, gain, query, state, 0, CHUNKS[0], mine_0, theirs_0, there_0, None)
    theirs_1, result = tie((theirs_1, result))
    there_1 = xor_swap(mine_1[1:] + theirs_1[1:], "core", 1)
    result = final_attention(info, gain, query, state, 2, CHUNKS[1], mine_1, theirs_1, there_1, result)
    return result[None]


def solution(mesh):
    groups, blocks = mesh.devices.shape
    split = Mesh(mesh.devices.reshape(groups // 4, 2, 2, blocks), ("z", "y", "core", "blk"))
    fsdp = ("z", "y", "core")
    return jax.shard_map(
        per_device,
        mesh=split,
        in_specs=(
            P(fsdp, "blk", None),
            P(fsdp, "blk", None),
            P(fsdp, "blk", None),
            P(fsdp, None),
            P(),
            P(fsdp),
            P(fsdp, "blk", None),
            P(fsdp, "blk"),
        ),
        out_specs=P(fsdp, "blk", None),
        check_vma=False,
    )
```

```python
import functools

import jax
import jax.numpy as jnp
from jax import lax
from jax.experimental import pallas as pl
from jax.experimental.pallas import tpu as pltpu
from jax.sharding import Mesh
from jax.sharding import PartitionSpec as P

HQ = 32
KVH = 4
HD = 128
SHARED = HQ // KVH
BLOCK = 512
RESP_DEV = 2
RLEN = 64
ROWS = RESP_DEV * RLEN
PAIR = 2 * ROWS
GROUP = SHARED * HD
SCALE = HD ** (-0.5) * 1.4426950408889634
HIDDEN = -1e30
NT = (((1,), (1,)), ((), ()))
HINT = pl.CostEstimate(flops=1024, bytes_accessed=1024, transcendentals=0)
LONG = pl.CostEstimate(flops=2**32, bytes_accessed=1024, transcendentals=0)

CHUNKS = ((0, 2), (2, 2))
HELP = (5, 5)


def pair_queries(q_ref, g, extra=None):
    heads = [q_ref[:, i * HD : (i + 1) * HD] for i in (g, g + 1)]
    if extra is not None:
        heads = [jnp.concatenate([head, extra], axis=1) for head in heads]
    return jnp.concatenate(heads, axis=0)


def scores_of(keys, queries):
    return lax.dot_general(keys, queries, NT, preferred_element_type=jnp.float32)


def prompt_kernel(first, info, q_ref, k_ref, v_ref, *refs):
    if first:
        acc_ref, ml_ref = refs
    else:
        old_acc, old_ml, acc_ref, ml_ref = refs
    count = k_ref.shape[0]
    place = info[0] + lax.broadcasted_iota(jnp.int32, (count, HD), 0)
    column = lax.broadcasted_iota(jnp.int32, (count, HD), 1)
    listed = jnp.where(column == 0, info[2], info[3])
    hidden = (column < RESP_DEV) & ((place >= info[1]) | (listed != 1))
    keys = jnp.concatenate([k_ref[...], jnp.where(hidden, HIDDEN, 0.0).astype(jnp.bfloat16)], axis=1)
    owner = lax.broadcasted_iota(jnp.int32, (ROWS, HD), 0) // RLEN
    ours = jnp.where(owner == lax.broadcasted_iota(jnp.int32, (ROWS, HD), 1), 1.0, 0.0).astype(jnp.bfloat16)
    values = v_ref[...].T
    ahead = scores_of(keys, pair_queries(q_ref, 0, ours))
    for g in range(0, SHARED, 2):
        cols = slice(g * HD, (g + 2) * HD)
        scores = ahead
        if g + 2 < SHARED:
            ahead = scores_of(keys, pair_queries(q_ref, g + 2, ours))
        largest = jnp.max(scores, axis=0, keepdims=True)
        if not first:
            before = old_ml[0:1, cols]
            largest = jnp.maximum(largest, before)
            faded = jnp.exp2((before - largest) * SCALE)
        weights = jnp.exp2((scores - largest) * SCALE)
        total = jnp.sum(weights, axis=0, keepdims=True)
        acc = jnp.dot(values, weights.astype(jnp.bfloat16), preferred_element_type=jnp.float32)
        if not first:
            total = total + faded * old_ml[1:2, cols]
            acc = acc + faded * old_acc[:, cols]
        acc_ref[:, cols] = acc
        ml_ref[0:1, cols] = largest
        ml_ref[1:2, cols] = total


def prompt_attention(info, query, cache, state, head, heads, offset=0):
    count = cache.shape[0]
    first = state is None
    wide = pl.BlockSpec((ROWS, GROUP), lambda k, s: (0, head + k))
    turned = pl.BlockSpec((HD, SHARED * ROWS), lambda k, s: (0, k))
    small = pl.BlockSpec((8, SHARED * ROWS), lambda k, s: (0, k))
    specs = [
        wide,
        pl.BlockSpec((count, HD), lambda k, s: (0, head + k)),
        pl.BlockSpec((count, HD), lambda k, s: (0, KVH + head + k)),
    ]
    operands = [query, cache, cache]
    if not first:
        specs += [
            pl.BlockSpec((HD, SHARED * ROWS), lambda k, s: (0, offset + k)),
            pl.BlockSpec((8, SHARED * ROWS), lambda k, s: (0, offset + k)),
        ]
        operands += list(state)
    return pl.pallas_call(
        functools.partial(prompt_kernel, first),
        grid_spec=pltpu.PrefetchScalarGridSpec(
            num_scalar_prefetch=1, grid=(heads,), in_specs=specs, out_specs=[turned, small]
        ),
        out_shape=[
            jax.ShapeDtypeStruct((HD, heads * SHARED * ROWS), jnp.float32),
            jax.ShapeDtypeStruct((8, heads * SHARED * ROWS), jnp.float32),
        ],
        compiler_params=pltpu.CompilerParams(vmem_limit_bytes=32 * 2**20),
        cost_estimate=LONG,
        name="prompt_attention",
    )(info, *operands)


VMEM = pl.BlockSpec(memory_space=pltpu.VMEM)
SMEM = pl.BlockSpec(memory_space=pltpu.SMEM)
PARAMS = pltpu.CompilerParams(vmem_limit_bytes=32 * 2**20)


def on_chip(kernel, name, outs, scalars, *operands, scratch=()):
    return pl.pallas_call(
        kernel,
        in_specs=[SMEM] + [VMEM] * len(operands),
        out_specs=[VMEM] * len(outs),
        out_shape=outs,
        scratch_shapes=scratch,
        compiler_params=PARAMS,
        cost_estimate=HINT,
        name=name,
    )(scalars, *operands)


def pack_rows_kernel(where, x_ref, keep, send):
    steps, _, part = keep.shape
    for z in range(steps):
        for out, y in ((keep, where[1]), (send, 1 - where[1])):
            out[z] = x_ref[:, pl.ds(pl.multiple_of((2 * z + y) * part, 128), part)]


def pack_rows(where, x, y, steps):
    part = x.shape[1] // (2 * steps)
    if part % 128:
        halves = jnp.transpose(x.reshape(ROWS, steps, 2, part), (2, 1, 0, 3))
        return [lax.dynamic_index_in_dim(halves, i, axis=0, keepdims=False) for i in (y, 1 - y)]
    outs = [jax.ShapeDtypeStruct((steps, ROWS, part), x.dtype)] * 2
    return on_chip(pack_rows_kernel, "pack_rows", outs, where, x)


def row_split(rows, i):
    helped = rows * HELP[i] // 10
    return helped, rows - helped


def pack_weight_kernel(where, got_ref, own_ref, *refs):
    outs, sems = refs[:-1], refs[-1]
    rows = got_ref.shape[0]
    core, plane = where[2], where[3]
    own_place = pl.ds(pl.multiple_of(core * rows, 16), rows)
    got_place = pl.ds(pl.multiple_of((1 - core) * rows, 16), rows)
    copies = []
    for i, (head, heads) in enumerate(CHUNKS):
        columns = pl.ds(pl.multiple_of((core * KVH + head) * HD, 128), heads * HD)
        copies.append(pltpu.make_async_copy(own_ref.at[:, columns], outs[2 * i].at[own_place, :], sems.at[i]))
        copies[-1].start()
        outs[2 * i][got_place, :] = got_ref[:, columns]
    for copy, whole, far in zip(copies, outs[0::2], outs[1::2]):
        copy.wait()
        direct = far.shape[0]
        far[...] = whole[pl.ds(pl.multiple_of(plane * (2 * rows - direct), 16), direct), :]


def pack_weight(where, own, got):
    rows = 2 * own.shape[0]
    shapes = []
    for i, (_, heads) in enumerate(CHUNKS):
        shapes += [(rows, heads * HD), (row_split(rows, i)[1], heads * HD)]
    outs = pl.pallas_call(
        pack_weight_kernel,
        in_specs=[SMEM, VMEM, pl.BlockSpec(memory_space=pltpu.HBM)],
        out_specs=[VMEM] * len(shapes),
        out_shape=[jax.ShapeDtypeStruct(shape, own.dtype) for shape in shapes],
        scratch_shapes=[pltpu.SemaphoreType.DMA((len(CHUNKS),))],
        compiler_params=PARAMS,
        cost_estimate=HINT,
        name="pack_weight",
    )(where, got, own)
    return list(outs[0::2]), list(outs[1::2])


def project_kernel(where, keep, other, others, own, near, forwarded, *refs):
    direct, mine, theirs, whole = refs[:-3], refs[-3], refs[-2], refs[-1]
    plane = where[3]
    count, extra = direct[0].shape[0], forwarded.shape[1]
    total = None
    for j in range(2 + len(direct)):
        if j == 0:
            weight = own[...]
        elif j == 1:
            weight = near[...]
        else:
            far = whole.at[j - 2]
            far[pl.ds(pl.multiple_of(plane * extra, 16), count), :] = direct[j - 2][...]
            far[pl.ds(pl.multiple_of((1 - plane) * count, 16), extra), :] = forwarded[j - 2]
            weight = far[...]
        place = where[0] ^ j
        left = jnp.concatenate([keep[place], others[0, place], other[place], others[1, place]], axis=0)
        product = jnp.dot(left, weight, preferred_element_type=jnp.float32)
        total = product if total is None else total + product
    for i in range(2):
        mine[i] = total[i * ROWS : (i + 1) * ROWS]
        theirs[i] = total[(2 + i) * ROWS : (3 + i) * ROWS]


def project(where, rows_of_x, own, near, direct, forwarded):
    width = own.shape[1]
    out = jax.ShapeDtypeStruct((2, ROWS, width), jnp.float32)
    return on_chip(
        project_kernel,
        "project",
        [out, out],
        where,
        *rows_of_x,
        own,
        near,
        forwarded,
        *direct,
        scratch=[pltpu.VMEM((len(direct), own.shape[0], width), jnp.bfloat16)],
    )


def final_kernel(chunk, offset, info, gain_ref, q_ref, acc_ref, ml_ref, mine, theirs, there, *refs):
    result, built, sem = refs[-3:]
    head, heads = chunk
    slot = lax.broadcasted_iota(jnp.int32, (ROWS, PAIR), 0)
    row = lax.broadcasted_iota(jnp.int32, (ROWS, PAIR), 1) % ROWS
    length = jnp.where(row < RLEN, info[0], info[1])
    base = jnp.where(row < RLEN, 0, RLEN)
    seen = (slot >= base) & (slot <= row) & (slot - base < length)
    live = jnp.where(row - base < length, 1.0, 0.0)[0:1]
    copies = []
    for k in range(heads):
        part = slice(k * HD, (k + 1) * HD)
        here = mine[0, :, part] + theirs[0, :, part]
        away = there[0, :, part] if there.shape[0] == 1 else there[0, :, part] + there[1, :, part]
        first_core = jnp.full(here.shape, info[2]) == 0
        raw = jnp.where(first_core, here, away)
        mean = jnp.mean(raw * raw, axis=1, keepdims=True)
        keys = (raw * lax.rsqrt(mean + 1e-06) * gain_ref[...]).astype(jnp.bfloat16)
        values = jnp.where(first_core, away, here).T.astype(jnp.bfloat16)
        pairs = range(0, SHARED, 2)
        products = [scores_of(keys, pair_queries(q_ref, (head + k) * SHARED + g)) for g in pairs]
        for g, scores in zip(pairs, products):
            cols = slice(((offset + k) * SHARED + g) * HD, ((offset + k) * SHARED + g + 2) * HD)
            scores = jnp.where(seen, scores, HIDDEN)
            before = ml_ref[0:1, cols]
            largest = jnp.maximum(jnp.max(scores, axis=0, keepdims=True), before)
            faded = jnp.exp2((before - largest) * SCALE)
            weights = jnp.exp2((scores - largest) * SCALE)
            total = jnp.sum(weights, axis=0, keepdims=True) + faded * ml_ref[1:2, cols]
            acc = jnp.dot(values, weights.astype(jnp.bfloat16), preferred_element_type=jnp.float32)
            acc = (acc + faded * acc_ref[:, cols]) * (live / total)
            built[k, :, g * HD : (g + 1) * HD] = acc[:, :ROWS].T.astype(jnp.bfloat16)
            built[k, :, (g + 1) * HD : (g + 2) * HD] = acc[:, ROWS:].T.astype(jnp.bfloat16)
        place = result.at[:, pl.ds((head + k) * GROUP, GROUP)]
        copies.append(pltpu.make_async_copy(built.at[k], place, sem.at[k]))
        copies[-1].start()
    for copy in copies:
        copy.wait()


def final_attention(info, gain, query, state, offset, chunk, mine, theirs, there, result):
    heads = chunk[1]
    operands = [gain, query, *state, mine, theirs, there]
    specs = [SMEM] + [VMEM] * len(operands)
    aliases = {}
    if result is not None:
        operands.append(result)
        specs.append(pl.BlockSpec(memory_space=pl.ANY))
        aliases = {len(operands): 0}
    return pl.pallas_call(
        functools.partial(final_kernel, chunk, offset),
        in_specs=specs,
        out_specs=pl.BlockSpec(memory_space=pl.ANY),
        out_shape=jax.ShapeDtypeStruct((ROWS, HQ * HD), jnp.bfloat16),
        scratch_shapes=[pltpu.VMEM((heads, ROWS, GROUP), jnp.bfloat16), pltpu.SemaphoreType.DMA((heads,))],
        input_output_aliases=aliases,
        compiler_params=PARAMS,
        cost_estimate=HINT,
        name="final_attention",
    )(info, *operands)


def xor_swap(array, axis, by):
    return lax.ppermute(array, axis, [(i, i ^ by) for i in range(lax.axis_size(axis))])


def per_device(
    x_resp, queries, prompt_cache, kv_weight, key_gain, prompt_lengths, block_table, resp_lengths
):
    x, query = x_resp[0], queries[0]
    steps = lax.axis_size("z")
    z, y, core = lax.axis_index("z"), lax.axis_index("y"), lax.axis_index("core")
    holder, cycle = lax.axis_index("blk"), lax.axis_size("blk")
    plane = holder % 2
    where = jnp.stack([z, y, core, plane]).astype(jnp.int32)

    tie = lax.optimization_barrier

    got_weight = xor_swap(kv_weight, "core", 1)
    caches = [prompt_cache[0]]
    for _ in range(cycle - 1):
        caches.append(lax.ppermute(caches[-1], "blk", [(i, (i + 1) % cycle) for i in range(cycle)]))

    keep, given = pack_rows(where, x, y, steps)
    other = xor_swap(given, "y", 1)
    got_weight, given = tie((got_weight, given))
    whole, far = pack_weight(where, kv_weight, got_weight)

    def send(far):
        return [xor_swap(far, "z", j) for j in range(2, steps)]

    def forward(i):
        helped, direct = row_split(whole[0].shape[0], i)
        parts = [lax.dynamic_slice_in_dim(p, plane * (direct - helped), helped, axis=0) for p in sent[i]]
        return xor_swap(jnp.stack(parts), "blk", 1)

    sent = [send(far[0])]
    near = [xor_swap(whole[0], "z", 1)]
    block_table, _ = tie((block_table, whole[0]))
    infos = []
    for stride in range(cycle):
        owner = lax.rem(holder + cycle - stride, cycle)
        place = owner * prompt_cache.shape[1]
        listed = lax.dynamic_index_in_dim(block_table[0], place // BLOCK, axis=1, keepdims=False)
        infos.append(jnp.concatenate([place[None], prompt_lengths, listed]).astype(jnp.int32))

    query, _ = tie((query, whole[0]))
    state = prompt_attention(infos[0], query, caches[0], None, 0, KVH)

    sent[0], near[0], state, second, other = tie((sent[0], near[0], state, (far[1], whole[1]), other))
    sent.append(send(second[0]))
    near.append(xor_swap(second[1], "z", 1))
    rows_of_x = [keep, other, xor_swap(jnp.stack([keep, other]), "core", 1)]
    sent[0], caches = tie((sent[0], caches))
    forwarded = [forward(0)]
    for stride in range(1, cycle):
        state = prompt_attention(infos[stride], query, caches[stride], state, 0, KVH)

    def sums(i):
        return project(where, rows_of_x, whole[i], near[i], sent[i], forwarded[i])

    forwarded[0], state = tie((forwarded[0], state))
    mine_0, theirs_0 = sums(0)
    theirs_0 = xor_swap(theirs_0, "y", 1)
    sent[1], near[1], mine_0 = tie((sent[1], near[1], mine_0))
    forwarded.append(forward(1))

    info = jnp.concatenate([resp_lengths[0], core[None]]).astype(jnp.int32)
    gain = key_gain[None]
    forwarded[1], mine_0 = tie((forwarded[1], mine_0))
    mine_1, theirs_1 = sums(1)
    theirs_0, theirs_1 = tie((theirs_0, theirs_1))
    theirs_1 = xor_swap(theirs_1, "y", 1)
    there_0 = xor_swap(mine_0[1:] + theirs_0[1:], "core", 1)
    result = final_attention(info, gain, query, state, 0, CHUNKS[0], mine_0, theirs_0, there_0, None)
    theirs_1, result = tie((theirs_1, result))
    there_1 = xor_swap(mine_1[1:] + theirs_1[1:], "core", 1)
    result = final_attention(info, gain, query, state, 2, CHUNKS[1], mine_1, theirs_1, there_1, result)
    return result[None]


def solution(mesh):
    groups, blocks = mesh.devices.shape
    split = Mesh(mesh.devices.reshape(groups // 4, 2, 2, blocks), ("z", "y", "core", "blk"))
    fsdp = ("z", "y", "core")
    return jax.shard_map(
        per_device,
        mesh=split,
        in_specs=(
            P(fsdp, "blk", None),
            P(fsdp, "blk", None),
            P(fsdp, "blk", None),
            P(fsdp, None),
            P(),
            P(fsdp),
            P(fsdp, "blk", None),
            P(fsdp, "blk"),
        ),
        out_specs=P(fsdp, "blk", None),
        check_vma=False,
    )
```

```python
import functools

import jax
import jax.numpy as jnp
from jax import lax
from jax.experimental import pallas as pl
from jax.experimental.pallas import tpu as pltpu
from jax.sharding import Mesh
from jax.sharding import PartitionSpec as P

HQ = 32
KVH = 4
HD = 128
SHARED = HQ // KVH
BLOCK = 512
RESP_DEV = 2
RLEN = 64
ROWS = RESP_DEV * RLEN
PAIR = 2 * ROWS
GROUP = SHARED * HD
SCALE = HD ** (-0.5) * 1.4426950408889634
HIDDEN = -1e30
NT = (((1,), (1,)), ((), ()))
HINT = pl.CostEstimate(flops=1024, bytes_accessed=1024, transcendentals=0)

CHUNKS = ((0, 2), (2, 2))
HELP = (5, 5)


def pair_queries(q_ref, g, extra=None):
    heads = [q_ref[:, i * HD : (i + 1) * HD] for i in (g, g + 1)]
    if extra is not None:
        heads = [jnp.concatenate([head, extra], axis=1) for head in heads]
    return jnp.concatenate(heads, axis=0)


def scores_of(keys, queries):
    return lax.dot_general(keys, queries, NT, preferred_element_type=jnp.float32)


def prompt_kernel(first, info, q_ref, k_ref, v_ref, *refs):
    if first:
        acc_ref, ml_ref = refs
    else:
        old_acc, old_ml, acc_ref, ml_ref = refs
    count = k_ref.shape[0]
    place = info[0] + lax.broadcasted_iota(jnp.int32, (count, HD), 0)
    column = lax.broadcasted_iota(jnp.int32, (count, HD), 1)
    listed = jnp.where(column == 0, info[2], info[3])
    hidden = (column < RESP_DEV) & ((place >= info[1]) | (listed != 1))
    keys = jnp.concatenate([k_ref[...], jnp.where(hidden, HIDDEN, 0.0).astype(jnp.bfloat16)], axis=1)
    owner = lax.broadcasted_iota(jnp.int32, (ROWS, HD), 0) // RLEN
    ours = jnp.where(owner == lax.broadcasted_iota(jnp.int32, (ROWS, HD), 1), 1.0, 0.0).astype(jnp.bfloat16)
    values = v_ref[...].T
    ahead = scores_of(keys, pair_queries(q_ref, 0, ours))
    for g in range(0, SHARED, 2):
        cols = slice(g * HD, (g + 2) * HD)
        scores = ahead
        if g + 2 < SHARED:
            ahead = scores_of(keys, pair_queries(q_ref, g + 2, ours))
        largest = jnp.max(scores, axis=0, keepdims=True)
        if not first:
            before = old_ml[0:1, cols]
            largest = jnp.maximum(largest, before)
            faded = jnp.exp2((before - largest) * SCALE)
        weights = jnp.exp2((scores - largest) * SCALE)
        total = jnp.sum(weights, axis=0, keepdims=True)
        acc = jnp.dot(values, weights.astype(jnp.bfloat16), preferred_element_type=jnp.float32)
        if not first:
            total = total + faded * old_ml[1:2, cols]
            acc = acc + faded * old_acc[:, cols]
        acc_ref[:, cols] = acc
        ml_ref[0:1, cols] = largest
        ml_ref[1:2, cols] = total


def prompt_attention(info, query, cache, state, head, heads, offset=0):
    count = cache.shape[0]
    first = state is None
    wide = pl.BlockSpec((ROWS, GROUP), lambda k, s: (0, head + k))
    turned = pl.BlockSpec((HD, SHARED * ROWS), lambda k, s: (0, k))
    small = pl.BlockSpec((8, SHARED * ROWS), lambda k, s: (0, k))
    specs = [
        wide,
        pl.BlockSpec((count, HD), lambda k, s: (0, head + k)),
        pl.BlockSpec((count, HD), lambda k, s: (0, KVH + head + k)),
    ]
    operands = [query, cache, cache]
    if not first:
        specs += [
            pl.BlockSpec((HD, SHARED * ROWS), lambda k, s: (0, offset + k)),
            pl.BlockSpec((8, SHARED * ROWS), lambda k, s: (0, offset + k)),
        ]
        operands += list(state)
    return pl.pallas_call(
        functools.partial(prompt_kernel, first),
        grid_spec=pltpu.PrefetchScalarGridSpec(
            num_scalar_prefetch=1, grid=(heads,), in_specs=specs, out_specs=[turned, small]
        ),
        out_shape=[
            jax.ShapeDtypeStruct((HD, heads * SHARED * ROWS), jnp.float32),
            jax.ShapeDtypeStruct((8, heads * SHARED * ROWS), jnp.float32),
        ],
        compiler_params=pltpu.CompilerParams(vmem_limit_bytes=32 * 2**20),
        cost_estimate=pl.CostEstimate(
            flops=2**33 if first else 2**32, bytes_accessed=1024, transcendentals=0
        ),
        name="prompt_attention",
    )(info, *operands)


VMEM = pl.BlockSpec(memory_space=pltpu.VMEM)
SMEM = pl.BlockSpec(memory_space=pltpu.SMEM)
PARAMS = pltpu.CompilerParams(vmem_limit_bytes=32 * 2**20)


def on_chip(kernel, name, outs, scalars, *operands, scratch=()):
    return pl.pallas_call(
        kernel,
        in_specs=[SMEM] + [VMEM] * len(operands),
        out_specs=[VMEM] * len(outs),
        out_shape=outs,
        scratch_shapes=scratch,
        compiler_params=PARAMS,
        cost_estimate=HINT,
        name=name,
    )(scalars, *operands)


def pack_rows_kernel(where, own_ref, got_ref, keep, send):
    steps, part = keep.shape[1], keep.shape[3]
    for z in range(steps):
        for out, y in ((keep, where[1]), (send, 1 - where[1])):
            columns = pl.ds(pl.multiple_of((2 * z + y) * part, 128), part)
            out[0, z] = own_ref[:, columns]
            out[1, z] = got_ref[:, columns]


def pack_rows(where, own, got, y, steps):
    part = own.shape[1] // (2 * steps)
    if part % 128:
        halves = jnp.stack([own, got]).reshape(2, ROWS, steps, 2, part)
        halves = jnp.transpose(halves, (3, 0, 2, 1, 4))
        return [lax.dynamic_index_in_dim(halves, i, axis=0, keepdims=False) for i in (y, 1 - y)]
    outs = [jax.ShapeDtypeStruct((2, steps, ROWS, part), own.dtype)] * 2
    return on_chip(pack_rows_kernel, "pack_rows", outs, where, own, got)


def row_split(rows, i):
    helped = rows * HELP[i] // 10
    return helped, rows - helped


def columns_of(chunk):
    return slice(chunk[0] * HD, (chunk[0] + chunk[1]) * HD)


def pack_weight_kernel(where, got_ref, own_ref, whole, *refs):
    far, sem = refs[:-1], refs[-1]
    rows = got_ref.shape[0]
    core, plane = where[2], where[3]
    half = pl.ds(pl.multiple_of(core * KVH * HD, 128), KVH * HD)
    own_place = pl.ds(pl.multiple_of(core * rows, 16), rows)
    copy = pltpu.make_async_copy(own_ref.at[:, half], whole.at[own_place, :], sem)
    copy.start()
    whole[pl.ds(pl.multiple_of((1 - core) * rows, 16), rows), :] = got_ref[:, half]
    copy.wait()
    for out, chunk in zip(far, CHUNKS):
        direct = out.shape[0]
        out[...] = whole[pl.ds(pl.multiple_of(plane * (2 * rows - direct), 16), direct), columns_of(chunk)]


def pack_weight(where, own, got):
    rows = 2 * own.shape[0]
    shapes = [(rows, KVH * HD)] + [(row_split(rows, i)[1], heads * HD) for i, (_, heads) in enumerate(CHUNKS)]
    whole, *far = pl.pallas_call(
        pack_weight_kernel,
        in_specs=[SMEM, VMEM, pl.BlockSpec(memory_space=pltpu.HBM)],
        out_specs=[VMEM] * len(shapes),
        out_shape=[jax.ShapeDtypeStruct(shape, own.dtype) for shape in shapes],
        scratch_shapes=[pltpu.SemaphoreType.DMA],
        compiler_params=PARAMS,
        cost_estimate=HINT,
        name="pack_weight",
    )(where, got, own)
    return whole, far


def project_kernel(columns, where, keep, other, own, near, forwarded, *refs):
    direct, mine, theirs, whole = refs[:-3], refs[-3], refs[-2], refs[-1]
    plane = where[3]
    count, extra = direct[0].shape[0], forwarded.shape[1]
    total = None
    for j in range(2 + len(direct)):
        if j == 0:
            weight = own[:, columns]
        elif j == 1:
            weight = near[:, columns]
        else:
            far = whole.at[j - 2]
            far[pl.ds(pl.multiple_of(plane * extra, 16), count), :] = direct[j - 2][...]
            far[pl.ds(pl.multiple_of((1 - plane) * count, 16), extra), :] = forwarded[j - 2]
            weight = far[...]
        place = where[0] ^ j
        left = jnp.concatenate([x[core, place] for x in (keep, other) for core in range(2)], axis=0)
        product = jnp.dot(left, weight, preferred_element_type=jnp.float32)
        total = product if total is None else total + product
    for i in range(2):
        mine[i] = total[i * ROWS : (i + 1) * ROWS]
        theirs[i] = total[(2 + i) * ROWS : (3 + i) * ROWS]


def project(where, keep, other, chunk, own, near, direct, forwarded):
    width = chunk[1] * HD
    out = jax.ShapeDtypeStruct((2, ROWS, width), jnp.float32)
    return on_chip(
        functools.partial(project_kernel, columns_of(chunk)),
        "project",
        [out, out],
        where,
        keep,
        other,
        own,
        near,
        forwarded,
        *direct,
        scratch=[pltpu.VMEM((len(direct), own.shape[0], width), jnp.bfloat16)],
    )


def final_kernel(chunk, offset, info, gain_ref, q_ref, acc_ref, ml_ref, mine, theirs, there, *refs):
    result, built, sem = refs[-3:]
    head, heads = chunk
    slot = lax.broadcasted_iota(jnp.int32, (ROWS, PAIR), 0)
    row = lax.broadcasted_iota(jnp.int32, (ROWS, PAIR), 1) % ROWS
    length = jnp.where(row < RLEN, info[0], info[1])
    base = jnp.where(row < RLEN, 0, RLEN)
    seen = (slot >= base) & (slot <= row) & (slot - base < length)
    live = jnp.where(row - base < length, 1.0, 0.0)[0:1]
    copies = []
    for k in range(heads):
        part = slice(k * HD, (k + 1) * HD)
        here = mine[0, :, part] + theirs[0, :, part]
        away = there[0, :, part] if there.shape[0] == 1 else there[0, :, part] + there[1, :, part]
        first_core = jnp.full(here.shape, info[2]) == 0
        raw = jnp.where(first_core, here, away)
        mean = jnp.mean(raw * raw, axis=1, keepdims=True)
        keys = (raw * lax.rsqrt(mean + 1e-06) * gain_ref[...]).astype(jnp.bfloat16)
        values = jnp.where(first_core, away, here).T.astype(jnp.bfloat16)
        pairs = range(0, SHARED, 2)
        products = [scores_of(keys, pair_queries(q_ref, (head + k) * SHARED + g)) for g in pairs]
        for g, scores in zip(pairs, products):
            cols = slice(((offset + k) * SHARED + g) * HD, ((offset + k) * SHARED + g + 2) * HD)
            scores = jnp.where(seen, scores, HIDDEN)
            before = ml_ref[0:1, cols]
            largest = jnp.maximum(jnp.max(scores, axis=0, keepdims=True), before)
            faded = jnp.exp2((before - largest) * SCALE)
            weights = jnp.exp2((scores - largest) * SCALE)
            total = jnp.sum(weights, axis=0, keepdims=True) + faded * ml_ref[1:2, cols]
            acc = jnp.dot(values, weights.astype(jnp.bfloat16), preferred_element_type=jnp.float32)
            acc = (acc + faded * acc_ref[:, cols]) * (live / total)
            built[k, :, g * HD : (g + 1) * HD] = acc[:, :ROWS].T.astype(jnp.bfloat16)
            built[k, :, (g + 1) * HD : (g + 2) * HD] = acc[:, ROWS:].T.astype(jnp.bfloat16)
        place = result.at[:, pl.ds((head + k) * GROUP, GROUP)]
        copies.append(pltpu.make_async_copy(built.at[k], place, sem.at[k]))
        copies[-1].start()
    for copy in copies:
        copy.wait()


def final_attention(info, gain, query, state, offset, chunk, mine, theirs, there, result):
    heads = chunk[1]
    operands = [gain, query, *state, mine, theirs, there]
    specs = [SMEM] + [VMEM] * len(operands)
    aliases = {}
    if result is not None:
        operands.append(result)
        specs.append(pl.BlockSpec(memory_space=pl.ANY))
        aliases = {len(operands): 0}
    return pl.pallas_call(
        functools.partial(final_kernel, chunk, offset),
        in_specs=specs,
        out_specs=pl.BlockSpec(memory_space=pl.ANY),
        out_shape=jax.ShapeDtypeStruct((ROWS, HQ * HD), jnp.bfloat16),
        scratch_shapes=[pltpu.VMEM((heads, ROWS, GROUP), jnp.bfloat16), pltpu.SemaphoreType.DMA((heads,))],
        input_output_aliases=aliases,
        compiler_params=PARAMS,
        cost_estimate=HINT,
        name="final_attention",
    )(info, *operands)


def xor_swap(array, axis, by):
    return lax.ppermute(array, axis, [(i, i ^ by) for i in range(lax.axis_size(axis))])


def per_device(
    x_resp, queries, prompt_cache, kv_weight, key_gain, prompt_lengths, block_table, resp_lengths
):
    x, query = x_resp[0], queries[0]
    steps = lax.axis_size("z")
    z, y, core = lax.axis_index("z"), lax.axis_index("y"), lax.axis_index("core")
    holder, cycle = lax.axis_index("blk"), lax.axis_size("blk")
    plane = holder % 2
    where = jnp.stack([z, y, core, plane]).astype(jnp.int32)

    tie = lax.optimization_barrier

    got_weight = xor_swap(kv_weight, "core", 1)
    got_x = xor_swap(x, "core", 1)
    caches = [prompt_cache[0]]
    for _ in range(cycle - 1):
        caches.append(lax.ppermute(caches[-1], "blk", [(i, (i + 1) % cycle) for i in range(cycle)]))

    whole, far = pack_weight(where, kv_weight, got_weight)

    def send(far):
        return [xor_swap(far, "z", j) for j in range(2, steps)]

    def forward(i):
        helped, direct = row_split(whole.shape[0], i)
        parts = [lax.dynamic_slice_in_dim(p, plane * (direct - helped), helped, axis=0) for p in sent[i]]
        return xor_swap(jnp.stack(parts), "blk", 1)

    sent = [send(far[0])]
    near = xor_swap(whole, "z", 1)
    got_x, whole = tie((got_x, whole))
    keep, given = pack_rows(where, x, got_x, y, steps)
    other = xor_swap(given, "y", 1)

    block_table, _ = tie((block_table, whole))
    infos = []
    for stride in range(cycle):
        owner = lax.rem(holder + cycle - stride, cycle)
        place = owner * prompt_cache.shape[1]
        listed = lax.dynamic_index_in_dim(block_table[0], place // BLOCK, axis=1, keepdims=False)
        infos.append(jnp.concatenate([place[None], prompt_lengths, listed]).astype(jnp.int32))

    query, _, _ = tie((query, whole, given))
    state = prompt_attention(infos[0], query, caches[0], None, 0, KVH)

    sent[0], state, far[1] = tie((sent[0], state, far[1]))
    sent.append(send(far[1]))
    sent[0], caches = tie((sent[0], caches))
    forwarded = [forward(0)]
    for stride in range(1, cycle):
        state = prompt_attention(infos[stride], query, caches[stride], state, 0, KVH)
    sent[1], forwarded[0], state = tie((sent[1], forwarded[0], state))
    forwarded.append(forward(1))

    def sums(i):
        return project(where, keep, other, CHUNKS[i], whole, near, sent[i], forwarded[i])

    info = jnp.concatenate([resp_lengths[0], core[None]]).astype(jnp.int32)
    gain = key_gain[None]
    mine_0, theirs_0 = sums(0)
    theirs_0 = xor_swap(theirs_0, "y", 1)
    forwarded[1], mine_0 = tie((forwarded[1], mine_0))
    mine_1, theirs_1 = sums(1)
    theirs_0, theirs_1, mine_1 = tie((theirs_0, theirs_1, mine_1))
    there_0 = xor_swap(mine_0[1:] + theirs_0[1:], "core", 1)
    there_1 = [xor_swap(theirs_1[1:], ("y", "core"), 3), xor_swap(mine_1[1:], "core", 1)]
    theirs_1 = xor_swap(theirs_1[:1], "y", 1)
    result = final_attention(info, gain, query, state, 0, CHUNKS[0], mine_0, theirs_0, there_0, None)
    result = final_attention(
        info, gain, query, state, 2, CHUNKS[1], mine_1, theirs_1, jnp.concatenate(there_1), result
    )
    return result[None]


def solution(mesh):
    groups, blocks = mesh.devices.shape
    split = Mesh(mesh.devices.reshape(groups // 4, 2, 2, blocks), ("z", "y", "core", "blk"))
    fsdp = ("z", "y", "core")
    return jax.shard_map(
        per_device,
        mesh=split,
        in_specs=(
            P(fsdp, "blk", None),
            P(fsdp, "blk", None),
            P(fsdp, "blk", None),
            P(fsdp, None),
            P(),
            P(fsdp),
            P(fsdp, "blk", None),
            P(fsdp, "blk"),
        ),
        out_specs=P(fsdp, "blk", None),
        check_vma=False,
    )
```

```python
import functools

import jax
import jax.numpy as jnp
from jax import lax
from jax.experimental import pallas as pl
from jax.experimental.pallas import tpu as pltpu
from jax.sharding import Mesh
from jax.sharding import PartitionSpec as P

HQ = 32
KVH = 4
HD = 128
SHARED = HQ // KVH
BLOCK = 512
RESP_DEV = 2
RLEN = 64
ROWS = RESP_DEV * RLEN
PAIR = 2 * ROWS
GROUP = SHARED * HD
SCALE = HD ** (-0.5) * 1.4426950408889634
HIDDEN = -1e30
NT = (((1,), (1,)), ((), ()))
HINT = pl.CostEstimate(flops=1024, bytes_accessed=1024, transcendentals=0)

CHUNKS = ((0, 2), (2, 2))
HELP = (5, 5)


def pair_queries(q_ref, g, extra=None):
    heads = [q_ref[:, i * HD : (i + 1) * HD] for i in (g, g + 1)]
    if extra is not None:
        heads = [jnp.concatenate([head, extra], axis=1) for head in heads]
    return jnp.concatenate(heads, axis=0)


def scores_of(keys, queries):
    return lax.dot_general(keys, queries, NT, preferred_element_type=jnp.float32)


def prompt_kernel(first, info, q_ref, k_ref, v_ref, *refs):
    if first:
        acc_ref, ml_ref = refs
    else:
        old_acc, old_ml, acc_ref, ml_ref = refs
    count = k_ref.shape[0]
    place = info[0] + lax.broadcasted_iota(jnp.int32, (count, HD), 0)
    column = lax.broadcasted_iota(jnp.int32, (count, HD), 1)
    listed = jnp.where(column == 0, info[2], info[3])
    hidden = (column < RESP_DEV) & ((place >= info[1]) | (listed != 1))
    keys = jnp.concatenate([k_ref[...], jnp.where(hidden, HIDDEN, 0.0).astype(jnp.bfloat16)], axis=1)
    owner = lax.broadcasted_iota(jnp.int32, (ROWS, HD), 0) // RLEN
    ours = jnp.where(owner == lax.broadcasted_iota(jnp.int32, (ROWS, HD), 1), 1.0, 0.0).astype(jnp.bfloat16)
    values = v_ref[...].T
    ahead = scores_of(keys, pair_queries(q_ref, 0, ours))
    for g in range(0, SHARED, 2):
        cols = slice(g * HD, (g + 2) * HD)
        scores = ahead
        if g + 2 < SHARED:
            ahead = scores_of(keys, pair_queries(q_ref, g + 2, ours))
        largest = jnp.max(scores, axis=0, keepdims=True)
        if not first:
            before = old_ml[0:1, cols]
            largest = jnp.maximum(largest, before)
            faded = jnp.exp2((before - largest) * SCALE)
        weights = jnp.exp2((scores - largest) * SCALE)
        total = jnp.sum(weights, axis=0, keepdims=True)
        acc = jnp.dot(values, weights.astype(jnp.bfloat16), preferred_element_type=jnp.float32)
        if not first:
            total = total + faded * old_ml[1:2, cols]
            acc = acc + faded * old_acc[:, cols]
        acc_ref[:, cols] = acc
        ml_ref[0:1, cols] = largest
        ml_ref[1:2, cols] = total


def prompt_attention(info, query, cache, state, head, heads, offset=0):
    count = cache.shape[0]
    first = state is None
    wide = pl.BlockSpec((ROWS, GROUP), lambda k, s: (0, head + k))
    turned = pl.BlockSpec((HD, SHARED * ROWS), lambda k, s: (0, k))
    small = pl.BlockSpec((8, SHARED * ROWS), lambda k, s: (0, k))
    specs = [
        wide,
        pl.BlockSpec((count, HD), lambda k, s: (0, head + k)),
        pl.BlockSpec((count, HD), lambda k, s: (0, KVH + head + k)),
    ]
    operands = [query, cache, cache]
    if not first:
        specs += [
            pl.BlockSpec((HD, SHARED * ROWS), lambda k, s: (0, offset + k)),
            pl.BlockSpec((8, SHARED * ROWS), lambda k, s: (0, offset + k)),
        ]
        operands += list(state)
    return pl.pallas_call(
        functools.partial(prompt_kernel, first),
        grid_spec=pltpu.PrefetchScalarGridSpec(
            num_scalar_prefetch=1, grid=(heads,), in_specs=specs, out_specs=[turned, small]
        ),
        out_shape=[
            jax.ShapeDtypeStruct((HD, heads * SHARED * ROWS), jnp.float32),
            jax.ShapeDtypeStruct((8, heads * SHARED * ROWS), jnp.float32),
        ],
        compiler_params=pltpu.CompilerParams(vmem_limit_bytes=32 * 2**20),
        cost_estimate=pl.CostEstimate(
            flops=2**34 if first else 2**33, bytes_accessed=1024, transcendentals=0
        ),
        name="prompt_attention",
    )(info, *operands)


VMEM = pl.BlockSpec(memory_space=pltpu.VMEM)
SMEM = pl.BlockSpec(memory_space=pltpu.SMEM)
PARAMS = pltpu.CompilerParams(vmem_limit_bytes=32 * 2**20)


def on_chip(kernel, name, outs, scalars, *operands, scratch=()):
    return pl.pallas_call(
        kernel,
        in_specs=[SMEM] + [VMEM] * len(operands),
        out_specs=[VMEM] * len(outs),
        out_shape=outs,
        scratch_shapes=scratch,
        compiler_params=PARAMS,
        cost_estimate=HINT,
        name=name,
    )(scalars, *operands)


def pack_rows_kernel(where, own_ref, got_ref, keep, send):
    _, steps, _, part = keep.shape
    for z in range(steps):
        columns = [pl.ds(pl.multiple_of((2 * z + y) * part, 128), part) for y in (where[1], 1 - where[1])]
        keep[0, z] = own_ref[:, columns[0]]
        keep[1, z] = got_ref[:, columns[0]]
        send[z] = own_ref[:, columns[1]]


def pack_rows(where, own, got, y, steps):
    part = own.shape[1] // (2 * steps)
    if part % 128:
        halves = jnp.stack([own, got]).reshape(2, ROWS, steps, 2, part)
        halves = jnp.transpose(halves, (3, 0, 2, 1, 4))
        keep, send = [lax.dynamic_index_in_dim(halves, i, axis=0, keepdims=False) for i in (y, 1 - y)]
        return keep, send[0]
    shapes = [(2, steps, ROWS, part), (steps, ROWS, part)]
    outs = [jax.ShapeDtypeStruct(shape, own.dtype) for shape in shapes]
    return on_chip(pack_rows_kernel, "pack_rows", outs, where, own, got)


def row_split(rows, i):
    helped = rows * HELP[i] // 10
    return helped, rows - helped


def columns_of(chunk):
    return slice(chunk[0] * HD, (chunk[0] + chunk[1]) * HD)


def own_half_kernel(where, weight_ref, out):
    out[...] = weight_ref[:, pl.ds(pl.multiple_of(where[2] * KVH * HD, 128), KVH * HD)]


def own_half(where, weight):
    out = jax.ShapeDtypeStruct((weight.shape[0], KVH * HD), weight.dtype)
    return on_chip(own_half_kernel, "own_half", [out], where, weight)[0]


def pack_weight_kernel(where, own_ref, got_ref, whole, *far):
    rows = got_ref.shape[0]
    core, plane = where[2], where[3]
    half = pl.ds(pl.multiple_of(core * KVH * HD, 128), KVH * HD)
    whole[pl.ds(pl.multiple_of(core * rows, 16), rows), :] = own_ref[...]
    whole[pl.ds(pl.multiple_of((1 - core) * rows, 16), rows), :] = got_ref[:, half]
    for out, chunk in zip(far, CHUNKS):
        direct = out.shape[0]
        out[...] = whole[pl.ds(pl.multiple_of(plane * (2 * rows - direct), 16), direct), columns_of(chunk)]


def pack_weight(where, own, got):
    rows = 2 * own.shape[0]
    shapes = [(rows, KVH * HD)] + [(row_split(rows, i)[1], heads * HD) for i, (_, heads) in enumerate(CHUNKS)]
    outs = [jax.ShapeDtypeStruct(shape, own.dtype) for shape in shapes]
    whole, *far = on_chip(pack_weight_kernel, "pack_weight", outs, where, own, got)
    return whole, far


def project_kernel(columns, where, keep, other, other_2, own, near, forwarded, *refs):
    direct, mine, theirs, whole = refs[:-3], refs[-3], refs[-2], refs[-1]
    plane = where[3]
    count, extra = direct[0].shape[0], forwarded.shape[1]
    total = None
    for j in range(2 + len(direct)):
        if j == 0:
            weight = own[:, columns]
        elif j == 1:
            weight = near[:, columns]
        else:
            far = whole.at[j - 2]
            far[pl.ds(pl.multiple_of(plane * extra, 16), count), :] = direct[j - 2][...]
            far[pl.ds(pl.multiple_of((1 - plane) * count, 16), extra), :] = forwarded[j - 2]
            weight = far[...]
        place = where[0] ^ j
        left = jnp.concatenate([keep[0, place], keep[1, place], other[place], other_2[place]], axis=0)
        product = jnp.dot(left, weight, preferred_element_type=jnp.float32)
        total = product if total is None else total + product
    for i in range(2):
        mine[i] = total[i * ROWS : (i + 1) * ROWS]
        theirs[i] = total[(2 + i) * ROWS : (3 + i) * ROWS]


def project(where, rows_of_x, chunk, own, near, direct, forwarded):
    width = chunk[1] * HD
    out = jax.ShapeDtypeStruct((2, ROWS, width), jnp.float32)
    return on_chip(
        functools.partial(project_kernel, columns_of(chunk)),
        "project",
        [out, out],
        where,
        *rows_of_x,
        own,
        near,
        forwarded,
        *direct,
        scratch=[pltpu.VMEM((len(direct), own.shape[0], width), jnp.bfloat16)],
    )


def final_kernel(chunk, offset, info, gain_ref, q_ref, acc_ref, ml_ref, mine, theirs, there, there_2, *refs):
    result, built, sem = refs[-3:]
    head, heads = chunk
    slot = lax.broadcasted_iota(jnp.int32, (ROWS, PAIR), 0)
    row = lax.broadcasted_iota(jnp.int32, (ROWS, PAIR), 1) % ROWS
    length = jnp.where(row < RLEN, info[0], info[1])
    base = jnp.where(row < RLEN, 0, RLEN)
    seen = (slot >= base) & (slot <= row) & (slot - base < length)
    live = jnp.where(row - base < length, 1.0, 0.0)[0:1]
    copies = []
    for k in range(heads):
        part = slice(k * HD, (k + 1) * HD)
        here = mine[0, :, part] + theirs[0, :, part]
        away = there[0, :, part] + there_2[0, :, part]
        first_core = jnp.full(here.shape, info[2]) == 0
        raw = jnp.where(first_core, here, away)
        mean = jnp.mean(raw * raw, axis=1, keepdims=True)
        keys = (raw * lax.rsqrt(mean + 1e-06) * gain_ref[...]).astype(jnp.bfloat16)
        values = jnp.where(first_core, away, here).T.astype(jnp.bfloat16)
        pairs = range(0, SHARED, 2)
        products = [scores_of(keys, pair_queries(q_ref, (head + k) * SHARED + g)) for g in pairs]
        for g, scores in zip(pairs, products):
            cols = slice(((offset + k) * SHARED + g) * HD, ((offset + k) * SHARED + g + 2) * HD)
            scores = jnp.where(seen, scores, HIDDEN)
            before = ml_ref[0:1, cols]
            largest = jnp.maximum(jnp.max(scores, axis=0, keepdims=True), before)
            faded = jnp.exp2((before - largest) * SCALE)
            weights = jnp.exp2((scores - largest) * SCALE)
            total = jnp.sum(weights, axis=0, keepdims=True) + faded * ml_ref[1:2, cols]
            acc = jnp.dot(values, weights.astype(jnp.bfloat16), preferred_element_type=jnp.float32)
            acc = (acc + faded * acc_ref[:, cols]) * (live / total)
            built[k, :, g * HD : (g + 1) * HD] = acc[:, :ROWS].T.astype(jnp.bfloat16)
            built[k, :, (g + 1) * HD : (g + 2) * HD] = acc[:, ROWS:].T.astype(jnp.bfloat16)
        place = result.at[:, pl.ds((head + k) * GROUP, GROUP)]
        copies.append(pltpu.make_async_copy(built.at[k], place, sem.at[k]))
        copies[-1].start()
    for copy in copies:
        copy.wait()


def final_attention(info, gain, query, state, offset, chunk, mine, theirs, there, result):
    heads = chunk[1]
    operands = [gain, query, *state, mine, theirs, *there]
    specs = [SMEM] + [VMEM] * len(operands)
    aliases = {}
    if result is not None:
        operands.append(result)
        specs.append(pl.BlockSpec(memory_space=pl.ANY))
        aliases = {len(operands): 0}
    return pl.pallas_call(
        functools.partial(final_kernel, chunk, offset),
        in_specs=specs,
        out_specs=pl.BlockSpec(memory_space=pl.ANY),
        out_shape=jax.ShapeDtypeStruct((ROWS, HQ * HD), jnp.bfloat16),
        scratch_shapes=[pltpu.VMEM((heads, ROWS, GROUP), jnp.bfloat16), pltpu.SemaphoreType.DMA((heads,))],
        input_output_aliases=aliases,
        compiler_params=PARAMS,
        cost_estimate=HINT,
        name="final_attention",
    )(info, *operands)


def xor_swap(array, axis, by):
    return lax.ppermute(array, axis, [(i, i ^ by) for i in range(lax.axis_size(axis))])


def per_device(
    x_resp, queries, prompt_cache, kv_weight, key_gain, prompt_lengths, block_table, resp_lengths
):
    x, query = x_resp[0], queries[0]
    steps = lax.axis_size("z")
    z, y, core = lax.axis_index("z"), lax.axis_index("y"), lax.axis_index("core")
    holder, cycle = lax.axis_index("blk"), lax.axis_size("blk")
    plane = holder % 2
    where = jnp.stack([z, y, core, plane]).astype(jnp.int32)

    tie = lax.optimization_barrier

    got_weight = xor_swap(kv_weight, "core", 1)
    got_x = xor_swap(x, "core", 1)
    caches = [prompt_cache[0]]
    for _ in range(cycle - 1):
        caches.append(lax.ppermute(caches[-1], "blk", [(i, (i + 1) % cycle) for i in range(cycle)]))

    own, got_weight = tie((own_half(where, kv_weight), got_weight))
    whole, far = pack_weight(where, own, got_weight)

    def send(far):
        return [xor_swap(far, "z", j) for j in range(2, steps)]

    def forward(i):
        helped, direct = row_split(whole.shape[0], i)
        parts = [lax.dynamic_slice_in_dim(p, plane * (direct - helped), helped, axis=0) for p in sent[i]]
        return xor_swap(jnp.stack(parts), "blk", 1)

    sent = [send(far[0])]
    near = xor_swap(whole, "z", 1)
    got_x, whole = tie((got_x, whole))
    keep, given = pack_rows(where, x, got_x, y, steps)
    other = xor_swap(given, "y", 1)

    block_table, _ = tie((block_table, whole))
    infos = []
    for stride in range(cycle):
        owner = lax.rem(holder + cycle - stride, cycle)
        place = owner * prompt_cache.shape[1]
        listed = lax.dynamic_index_in_dim(block_table[0], place // BLOCK, axis=1, keepdims=False)
        infos.append(jnp.concatenate([place[None], prompt_lengths, listed]).astype(jnp.int32))

    query, _, _ = tie((query, whole, given))
    state = prompt_attention(infos[0], query, caches[0], None, 0, KVH)

    sent[0], state, far[1] = tie((sent[0], state, far[1]))
    sent.append(send(far[1]))
    sent[0], caches = tie((sent[0], caches))
    state, other = tie((state, other))
    rows_of_x = [keep, other, xor_swap(other, "core", 1)]
    forwarded = [forward(0)]
    for stride in range(1, cycle):
        state = prompt_attention(infos[stride], query, caches[stride], state, 0, KVH)
    forwarded[0], state = tie((forwarded[0], state))

    def sums(i):
        return project(where, rows_of_x, CHUNKS[i], whole, near, sent[i], forwarded[i])

    def owners(mine, theirs):
        there = [xor_swap(theirs[1:], ("y", "core"), 3), xor_swap(mine[1:], "core", 1)]
        return xor_swap(theirs[:1], "y", 1), there

    mine_0, theirs_0 = sums(0)
    sent[1], mine_0 = tie((sent[1], mine_0))
    forwarded.append(forward(1))
    here_0, there_0 = owners(mine_0, theirs_0)
    forwarded[1], mine_0 = tie((forwarded[1], mine_0))
    mine_1, theirs_1 = sums(1)
    here_0, there_0, mine_1, theirs_1 = tie((here_0, there_0, mine_1, theirs_1))
    here_1, there_1 = owners(mine_1, theirs_1)
    info = jnp.concatenate([resp_lengths[0], core[None]]).astype(jnp.int32)
    gain = key_gain[None]
    result = final_attention(info, gain, query, state, 0, CHUNKS[0], mine_0, here_0, there_0, None)
    result = final_attention(info, gain, query, state, 2, CHUNKS[1], mine_1, here_1, there_1, result)
    return result[None]


def solution(mesh):
    groups, blocks = mesh.devices.shape
    split = Mesh(mesh.devices.reshape(groups // 4, 2, 2, blocks), ("z", "y", "core", "blk"))
    fsdp = ("z", "y", "core")
    return jax.shard_map(
        per_device,
        mesh=split,
        in_specs=(
            P(fsdp, "blk", None),
            P(fsdp, "blk", None),
            P(fsdp, "blk", None),
            P(fsdp, None),
            P(),
            P(fsdp),
            P(fsdp, "blk", None),
            P(fsdp, "blk"),
        ),
        out_specs=P(fsdp, "blk", None),
        check_vma=False,
    )
```

```python
import functools

import jax
import jax.numpy as jnp
from jax import lax
from jax.experimental import pallas as pl
from jax.experimental.pallas import tpu as pltpu
from jax.sharding import Mesh
from jax.sharding import PartitionSpec as P

HQ = 32
KVH = 4
HD = 128
SHARED = HQ // KVH
BLOCK = 512
RESP_DEV = 2
RLEN = 64
ROWS = RESP_DEV * RLEN
PAIR = 2 * ROWS
GROUP = SHARED * HD
SCALE = HD ** (-0.5) * 1.4426950408889634
HIDDEN = -1e30
NT = (((1,), (1,)), ((), ()))
HINT = pl.CostEstimate(flops=1024, bytes_accessed=1024, transcendentals=0)

CHUNKS = ((0, 2), (2, 2))
HELP = (5, 5)


def pair_queries(q_ref, g, extra=None):
    heads = [q_ref[:, i * HD : (i + 1) * HD] for i in (g, g + 1)]
    if extra is not None:
        heads = [jnp.concatenate([head, extra], axis=1) for head in heads]
    return jnp.concatenate(heads, axis=0)


def scores_of(keys, queries):
    return lax.dot_general(keys, queries, NT, preferred_element_type=jnp.float32)


def prompt_kernel(first, info, q_ref, k_ref, v_ref, *refs):
    if first:
        acc_ref, ml_ref = refs
    else:
        old_acc, old_ml, acc_ref, ml_ref = refs
    count = k_ref.shape[0]
    place = info[0] + lax.broadcasted_iota(jnp.int32, (count, HD), 0)
    column = lax.broadcasted_iota(jnp.int32, (count, HD), 1)
    listed = jnp.where(column == 0, info[2], info[3])
    hidden = (column < RESP_DEV) & ((place >= info[1]) | (listed != 1))
    keys = jnp.concatenate([k_ref[...], jnp.where(hidden, HIDDEN, 0.0).astype(jnp.bfloat16)], axis=1)
    owner = lax.broadcasted_iota(jnp.int32, (ROWS, HD), 0) // RLEN
    ours = jnp.where(owner == lax.broadcasted_iota(jnp.int32, (ROWS, HD), 1), 1.0, 0.0).astype(jnp.bfloat16)
    values = v_ref[...].T
    ahead = scores_of(keys, pair_queries(q_ref, 0, ours))
    for g in range(0, SHARED, 2):
        cols = slice(g * HD, (g + 2) * HD)
        scores = ahead
        if g + 2 < SHARED:
            ahead = scores_of(keys, pair_queries(q_ref, g + 2, ours))
        largest = jnp.max(scores, axis=0, keepdims=True)
        if not first:
            before = old_ml[0:1, cols]
            largest = jnp.maximum(largest, before)
            faded = jnp.exp2((before - largest) * SCALE)
        weights = jnp.exp2((scores - largest) * SCALE)
        total = jnp.sum(weights, axis=0, keepdims=True)
        acc = jnp.dot(values, weights.astype(jnp.bfloat16), preferred_element_type=jnp.float32)
        if not first:
            total = total + faded * old_ml[1:2, cols]
            acc = acc + faded * old_acc[:, cols]
        acc_ref[:, cols] = acc
        ml_ref[0:1, cols] = largest
        ml_ref[1:2, cols] = total


def prompt_attention(info, query, cache, state, head, heads, offset=0):
    count = cache.shape[0]
    first = state is None
    wide = pl.BlockSpec((ROWS, GROUP), lambda k, s: (0, head + k))
    turned = pl.BlockSpec((HD, SHARED * ROWS), lambda k, s: (0, k))
    small = pl.BlockSpec((8, SHARED * ROWS), lambda k, s: (0, k))
    specs = [
        wide,
        pl.BlockSpec((count, HD), lambda k, s: (0, head + k)),
        pl.BlockSpec((count, HD), lambda k, s: (0, KVH + head + k)),
    ]
    operands = [query, cache, cache]
    if not first:
        specs += [
            pl.BlockSpec((HD, SHARED * ROWS), lambda k, s: (0, offset + k)),
            pl.BlockSpec((8, SHARED * ROWS), lambda k, s: (0, offset + k)),
        ]
        operands += list(state)
    return pl.pallas_call(
        functools.partial(prompt_kernel, first),
        grid_spec=pltpu.PrefetchScalarGridSpec(
            num_scalar_prefetch=1, grid=(heads,), in_specs=specs, out_specs=[turned, small]
        ),
        out_shape=[
            jax.ShapeDtypeStruct((HD, heads * SHARED * ROWS), jnp.float32),
            jax.ShapeDtypeStruct((8, heads * SHARED * ROWS), jnp.float32),
        ],
        compiler_params=pltpu.CompilerParams(vmem_limit_bytes=32 * 2**20),
        cost_estimate=pl.CostEstimate(
            flops=2**34 if first else 2**33, bytes_accessed=1024, transcendentals=0
        ),
        name="prompt_attention",
    )(info, *operands)


VMEM = pl.BlockSpec(memory_space=pltpu.VMEM)
SMEM = pl.BlockSpec(memory_space=pltpu.SMEM)
PARAMS = pltpu.CompilerParams(vmem_limit_bytes=32 * 2**20)


def on_chip(kernel, name, outs, scalars, *operands, scratch=()):
    return pl.pallas_call(
        kernel,
        in_specs=[SMEM] + [VMEM] * len(operands),
        out_specs=[VMEM] * len(outs),
        out_shape=outs,
        scratch_shapes=scratch,
        compiler_params=PARAMS,
        cost_estimate=HINT,
        name=name,
    )(scalars, *operands)


def pack_rows_kernel(where, own_ref, got_ref, keep, send):
    _, steps, _, part = keep.shape
    for z in range(steps):
        columns = [pl.ds(pl.multiple_of((2 * z + y) * part, 128), part) for y in (where[1], 1 - where[1])]
        keep[0, z] = own_ref[:, columns[0]]
        keep[1, z] = got_ref[:, columns[0]]
        send[z] = own_ref[:, columns[1]]


def pack_rows(where, own, got, y, steps):
    part = own.shape[1] // (2 * steps)
    if part % 128:
        halves = jnp.stack([own, got]).reshape(2, ROWS, steps, 2, part)
        halves = jnp.transpose(halves, (3, 0, 2, 1, 4))
        keep, send = [lax.dynamic_index_in_dim(halves, i, axis=0, keepdims=False) for i in (y, 1 - y)]
        return keep, send[0]
    shapes = [(2, steps, ROWS, part), (steps, ROWS, part)]
    outs = [jax.ShapeDtypeStruct(shape, own.dtype) for shape in shapes]
    return on_chip(pack_rows_kernel, "pack_rows", outs, where, own, got)


def row_split(rows, i):
    helped = rows * HELP[i] // 10
    return helped, rows - helped


def own_rows_kernel(where, weight_ref, *outs):
    rows = weight_ref.shape[0]
    for out, (head, heads) in zip(outs, CHUNKS):
        columns = pl.ds(pl.multiple_of((where[2] * KVH + head) * HD, 128), heads * HD)
        out[pl.ds(pl.multiple_of(where[2] * rows, 16), rows), :] = weight_ref[:, columns]


def own_rows(where, weight):
    outs = [jax.ShapeDtypeStruct((2 * weight.shape[0], heads * HD), weight.dtype) for _, heads in CHUNKS]
    return on_chip(own_rows_kernel, "own_rows", outs, where, weight)


def pack_weight_kernel(where, got_ref, *refs):
    count = len(CHUNKS)
    wholes, fars = refs[count : 2 * count], refs[2 * count :]
    rows = got_ref.shape[0]
    core, plane = where[2], where[3]
    for whole, far, (head, heads) in zip(wholes, fars, CHUNKS):
        columns = pl.ds(pl.multiple_of((core * KVH + head) * HD, 128), heads * HD)
        whole[pl.ds(pl.multiple_of((1 - core) * rows, 16), rows), :] = got_ref[:, columns]
        direct = far.shape[0]
        far[...] = whole[pl.ds(pl.multiple_of(plane * (2 * rows - direct), 16), direct), :]


def pack_weight(where, got, wholes):
    count = len(CHUNKS)
    outs = [jax.ShapeDtypeStruct(whole.shape, whole.dtype) for whole in wholes]
    for i, whole in enumerate(wholes):
        outs.append(jax.ShapeDtypeStruct((row_split(whole.shape[0], i)[1], whole.shape[1]), whole.dtype))
    outs = pl.pallas_call(
        pack_weight_kernel,
        in_specs=[SMEM] + [VMEM] * (1 + count),
        out_specs=[VMEM] * len(outs),
        out_shape=outs,
        input_output_aliases={2 + i: i for i in range(count)},
        compiler_params=PARAMS,
        cost_estimate=HINT,
        name="pack_weight",
    )(where, got, *wholes)
    return list(outs[:count]), list(outs[count:])


def project_kernel(where, keep, other, other_2, own, near, *refs):
    mine, theirs, whole = refs[-3:]
    far = whole.shape[0]
    direct, forwarded = refs[:far], refs[far:-3]
    plane = where[3]
    count, extra = direct[0].shape[0], whole.shape[1] - direct[0].shape[0]
    total = None
    for j in range(2 + far):
        if j == 0:
            weight = own[...]
        elif j == 1:
            weight = near[...]
        else:
            piece = whole.at[j - 2]
            piece[pl.ds(pl.multiple_of(plane * extra, 16), count), :] = direct[j - 2][...]
            rest = forwarded[0][j - 2] if len(forwarded) == 1 else forwarded[j - 2][...]
            piece[pl.ds(pl.multiple_of((1 - plane) * count, 16), extra), :] = rest
            weight = piece[...]
        place = where[0] ^ j
        left = jnp.concatenate([keep[0, place], keep[1, place], other[place], other_2[place]], axis=0)
        product = jnp.dot(left, weight, preferred_element_type=jnp.float32)
        total = product if total is None else total + product
    for i in range(2):
        mine[i] = total[i * ROWS : (i + 1) * ROWS]
        theirs[i] = total[(2 + i) * ROWS : (3 + i) * ROWS]


def project(where, rows_of_x, own, near, direct, forwarded):
    width = own.shape[1]
    out = jax.ShapeDtypeStruct((2, ROWS, width), jnp.float32)
    return on_chip(
        project_kernel,
        "project",
        [out, out],
        where,
        *rows_of_x,
        own,
        near,
        *direct,
        *forwarded,
        scratch=[pltpu.VMEM((len(direct), own.shape[0], width), jnp.bfloat16)],
    )


def final_kernel(chunk, offset, info, gain_ref, q_ref, acc_ref, ml_ref, mine, theirs, there, there_2, *refs):
    result, built, sem = refs[-3:]
    head, heads = chunk
    slot = lax.broadcasted_iota(jnp.int32, (ROWS, PAIR), 0)
    row = lax.broadcasted_iota(jnp.int32, (ROWS, PAIR), 1) % ROWS
    length = jnp.where(row < RLEN, info[0], info[1])
    base = jnp.where(row < RLEN, 0, RLEN)
    seen = (slot >= base) & (slot <= row) & (slot - base < length)
    live = jnp.where(row - base < length, 1.0, 0.0)[0:1]
    copies = []
    for k in range(heads):
        part = slice(k * HD, (k + 1) * HD)
        here = mine[0, :, part] + theirs[0, :, part]
        away = there[0, :, part] + there_2[0, :, part]
        first_core = jnp.full(here.shape, info[2]) == 0
        raw = jnp.where(first_core, here, away)
        mean = jnp.mean(raw * raw, axis=1, keepdims=True)
        keys = (raw * lax.rsqrt(mean + 1e-06) * gain_ref[...]).astype(jnp.bfloat16)
        values = jnp.where(first_core, away, here).T.astype(jnp.bfloat16)
        pairs = range(0, SHARED, 2)
        products = [scores_of(keys, pair_queries(q_ref, (head + k) * SHARED + g)) for g in pairs]
        for g, scores in zip(pairs, products):
            cols = slice(((offset + k) * SHARED + g) * HD, ((offset + k) * SHARED + g + 2) * HD)
            scores = jnp.where(seen, scores, HIDDEN)
            before = ml_ref[0:1, cols]
            largest = jnp.maximum(jnp.max(scores, axis=0, keepdims=True), before)
            faded = jnp.exp2((before - largest) * SCALE)
            weights = jnp.exp2((scores - largest) * SCALE)
            total = jnp.sum(weights, axis=0, keepdims=True) + faded * ml_ref[1:2, cols]
            acc = jnp.dot(values, weights.astype(jnp.bfloat16), preferred_element_type=jnp.float32)
            acc = (acc + faded * acc_ref[:, cols]) * (live / total)
            built[k, :, g * HD : (g + 1) * HD] = acc[:, :ROWS].T.astype(jnp.bfloat16)
            built[k, :, (g + 1) * HD : (g + 2) * HD] = acc[:, ROWS:].T.astype(jnp.bfloat16)
        place = result.at[:, pl.ds((head + k) * GROUP, GROUP)]
        copies.append(pltpu.make_async_copy(built.at[k], place, sem.at[k]))
        copies[-1].start()
    for copy in copies:
        copy.wait()


def final_attention(info, gain, query, state, offset, chunk, mine, theirs, there, result):
    heads = chunk[1]
    operands = [gain, query, *state, mine, theirs, *there]
    specs = [SMEM] + [VMEM] * len(operands)
    aliases = {}
    if result is not None:
        operands.append(result)
        specs.append(pl.BlockSpec(memory_space=pl.ANY))
        aliases = {len(operands): 0}
    return pl.pallas_call(
        functools.partial(final_kernel, chunk, offset),
        in_specs=specs,
        out_specs=pl.BlockSpec(memory_space=pl.ANY),
        out_shape=jax.ShapeDtypeStruct((ROWS, HQ * HD), jnp.bfloat16),
        scratch_shapes=[pltpu.VMEM((heads, ROWS, GROUP), jnp.bfloat16), pltpu.SemaphoreType.DMA((heads,))],
        input_output_aliases=aliases,
        compiler_params=PARAMS,
        cost_estimate=HINT,
        name="final_attention",
    )(info, *operands)


def xor_swap(array, axis, by):
    return lax.ppermute(array, axis, [(i, i ^ by) for i in range(lax.axis_size(axis))])


def per_device(
    x_resp, queries, prompt_cache, kv_weight, key_gain, prompt_lengths, block_table, resp_lengths
):
    x, query = x_resp[0], queries[0]
    steps = lax.axis_size("z")
    z, y, core = lax.axis_index("z"), lax.axis_index("y"), lax.axis_index("core")
    holder, cycle = lax.axis_index("blk"), lax.axis_size("blk")
    plane = holder % 2
    where = jnp.stack([z, y, core, plane]).astype(jnp.int32)

    tie = lax.optimization_barrier

    got_weight = xor_swap(kv_weight, "core", 1)
    got_x = xor_swap(x, "core", 1)
    caches = [prompt_cache[0]]
    for _ in range(cycle - 1):
        caches.append(lax.ppermute(caches[-1], "blk", [(i, (i + 1) % cycle) for i in range(cycle)]))

    wholes, got_weight = tie((own_rows(where, kv_weight), got_weight))
    whole, far = pack_weight(where, got_weight, wholes)

    def send(far):
        return [xor_swap(far, "z", j) for j in range(2, steps)]

    def forward(i, stacked):
        helped, direct = row_split(whole[0].shape[0], i)
        parts = [lax.dynamic_slice_in_dim(p, plane * (direct - helped), helped, axis=0) for p in sent[i]]
        return [xor_swap(part, "blk", 1) for part in ([jnp.stack(parts)] if stacked else parts)]

    sent = [send(far[0])]
    near = [xor_swap(whole[0], "z", 1)]
    got_x, whole[1] = tie((got_x, whole[1]))
    keep, given = pack_rows(where, x, got_x, y, steps)
    other = xor_swap(given, "y", 1)

    block_table, _ = tie((block_table, whole[0]))
    infos = []
    for stride in range(cycle):
        owner = lax.rem(holder + cycle - stride, cycle)
        place = owner * prompt_cache.shape[1]
        listed = lax.dynamic_index_in_dim(block_table[0], place // BLOCK, axis=1, keepdims=False)
        infos.append(jnp.concatenate([place[None], prompt_lengths, listed]).astype(jnp.int32))

    query, _, _ = tie((query, whole[0], given))
    state = prompt_attention(infos[0], query, caches[0], None, 0, KVH)

    sent[0], state, far[1], whole[1] = tie((sent[0], state, far[1], whole[1]))
    sent.append(send(far[1]))
    near.append(xor_swap(whole[1], "z", 1))
    sent[0], caches = tie((sent[0], caches))
    forwarded = [forward(0, True)]
    state, other = tie((state, other))
    rows_of_x = [keep, other, xor_swap(other, "core", 1)]
    for stride in range(1, cycle):
        state = prompt_attention(infos[stride], query, caches[stride], state, 0, KVH)

    def sums(i):
        return project(where, rows_of_x, whole[i], near[i], sent[i], forwarded[i])

    def owners(mine, theirs):
        there = [xor_swap(theirs[1:], ("y", "core"), 3), xor_swap(mine[1:], "core", 1)]
        return xor_swap(theirs[:1], "y", 1), there

    forwarded[0], state = tie((forwarded[0], state))
    mine_0, theirs_0 = sums(0)
    sent[1], mine_0 = tie((sent[1], mine_0))
    forwarded.append(forward(1, True))
    here_0, there_0 = owners(mine_0, theirs_0)
    forwarded[1], mine_0 = tie((forwarded[1], mine_0))
    mine_1, theirs_1 = sums(1)
    here_0, there_0, mine_1, theirs_1 = tie((here_0, there_0, mine_1, theirs_1))
    here_1, there_1 = owners(mine_1, theirs_1)
    info = jnp.concatenate([resp_lengths[0], core[None]]).astype(jnp.int32)
    gain = key_gain[None]
    result = final_attention(info, gain, query, state, 0, CHUNKS[0], mine_0, here_0, there_0, None)
    result = final_attention(info, gain, query, state, 2, CHUNKS[1], mine_1, here_1, there_1, result)
    return result[None]


def solution(mesh):
    groups, blocks = mesh.devices.shape
    split = Mesh(mesh.devices.reshape(groups // 4, 2, 2, blocks), ("z", "y", "core", "blk"))
    fsdp = ("z", "y", "core")
    return jax.shard_map(
        per_device,
        mesh=split,
        in_specs=(
            P(fsdp, "blk", None),
            P(fsdp, "blk", None),
            P(fsdp, "blk", None),
            P(fsdp, None),
            P(),
            P(fsdp),
            P(fsdp, "blk", None),
            P(fsdp, "blk"),
        ),
        out_specs=P(fsdp, "blk", None),
        check_vma=False,
    )
```

```python
import functools

import jax
import jax.numpy as jnp
from jax import lax
from jax.experimental import pallas as pl
from jax.experimental.pallas import tpu as pltpu
from jax.sharding import Mesh
from jax.sharding import PartitionSpec as P

HQ = 32
KVH = 4
HD = 128
SHARED = HQ // KVH
BLOCK = 512
RESP_DEV = 2
RLEN = 64
ROWS = RESP_DEV * RLEN
PAIR = 2 * ROWS
GROUP = SHARED * HD
SCALE = HD ** (-0.5) * 1.4426950408889634
HIDDEN = -1e30
NT = (((1,), (1,)), ((), ()))
HINT = pl.CostEstimate(flops=1024, bytes_accessed=1024, transcendentals=0)

CHUNKS = ((0, 2), (2, 2))
HELP = (5, 5)


def pair_queries(q_ref, g, extra=None):
    heads = [q_ref[:, i * HD : (i + 1) * HD] for i in (g, g + 1)]
    if extra is not None:
        heads = [jnp.concatenate([head, extra], axis=1) for head in heads]
    return jnp.concatenate(heads, axis=0)


def scores_of(keys, queries):
    return lax.dot_general(keys, queries, NT, preferred_element_type=jnp.float32)


def prompt_kernel(first, info, q_ref, k_ref, v_ref, *refs):
    if first:
        acc_ref, ml_ref = refs
    else:
        old_acc, old_ml, acc_ref, ml_ref = refs
    count = k_ref.shape[0]
    place = info[0] + lax.broadcasted_iota(jnp.int32, (count, HD), 0)
    column = lax.broadcasted_iota(jnp.int32, (count, HD), 1)
    listed = jnp.where(column == 0, info[2], info[3])
    hidden = (column < RESP_DEV) & ((place >= info[1]) | (listed != 1))
    keys = jnp.concatenate([k_ref[...], jnp.where(hidden, HIDDEN, 0.0).astype(jnp.bfloat16)], axis=1)
    owner = lax.broadcasted_iota(jnp.int32, (ROWS, HD), 0) // RLEN
    ours = jnp.where(owner == lax.broadcasted_iota(jnp.int32, (ROWS, HD), 1), 1.0, 0.0).astype(jnp.bfloat16)
    values = v_ref[...].T
    ahead = scores_of(keys, pair_queries(q_ref, 0, ours))
    for g in range(0, SHARED, 2):
        cols = slice(g * HD, (g + 2) * HD)
        scores = ahead
        if g + 2 < SHARED:
            ahead = scores_of(keys, pair_queries(q_ref, g + 2, ours))
        largest = jnp.max(scores, axis=0, keepdims=True)
        if not first:
            before = old_ml[0:1, cols]
            largest = jnp.maximum(largest, before)
            faded = jnp.exp2((before - largest) * SCALE)
        weights = jnp.exp2((scores - largest) * SCALE)
        total = jnp.sum(weights, axis=0, keepdims=True)
        acc = jnp.dot(values, weights.astype(jnp.bfloat16), preferred_element_type=jnp.float32)
        if not first:
            total = total + faded * old_ml[1:2, cols]
            acc = acc + faded * old_acc[:, cols]
        acc_ref[:, cols] = acc
        ml_ref[0:1, cols] = largest
        ml_ref[1:2, cols] = total


def prompt_attention(info, query, cache, state, head, heads, offset=0):
    count = cache.shape[0]
    first = state is None
    wide = pl.BlockSpec((ROWS, GROUP), lambda k, s: (0, head + k))
    turned = pl.BlockSpec((HD, SHARED * ROWS), lambda k, s: (0, k))
    small = pl.BlockSpec((8, SHARED * ROWS), lambda k, s: (0, k))
    specs = [
        wide,
        pl.BlockSpec((count, HD), lambda k, s: (0, head + k)),
        pl.BlockSpec((count, HD), lambda k, s: (0, KVH + head + k)),
    ]
    operands = [query, cache, cache]
    if not first:
        specs += [
            pl.BlockSpec((HD, SHARED * ROWS), lambda k, s: (0, offset + k)),
            pl.BlockSpec((8, SHARED * ROWS), lambda k, s: (0, offset + k)),
        ]
        operands += list(state)
    return pl.pallas_call(
        functools.partial(prompt_kernel, first),
        grid_spec=pltpu.PrefetchScalarGridSpec(
            num_scalar_prefetch=1, grid=(heads,), in_specs=specs, out_specs=[turned, small]
        ),
        out_shape=[
            jax.ShapeDtypeStruct((HD, heads * SHARED * ROWS), jnp.float32),
            jax.ShapeDtypeStruct((8, heads * SHARED * ROWS), jnp.float32),
        ],
        compiler_params=pltpu.CompilerParams(vmem_limit_bytes=32 * 2**20),
        cost_estimate=pl.CostEstimate(
            flops=2**34 if first else 2**33, bytes_accessed=1024, transcendentals=0
        ),
        name="prompt_attention",
    )(info, *operands)


VMEM = pl.BlockSpec(memory_space=pltpu.VMEM)
SMEM = pl.BlockSpec(memory_space=pltpu.SMEM)
PARAMS = pltpu.CompilerParams(vmem_limit_bytes=32 * 2**20)


def on_chip(kernel, name, outs, scalars, *operands, scratch=()):
    return pl.pallas_call(
        kernel,
        in_specs=[SMEM] + [VMEM] * len(operands),
        out_specs=[VMEM] * len(outs),
        out_shape=outs,
        scratch_shapes=scratch,
        compiler_params=PARAMS,
        cost_estimate=HINT,
        name=name,
    )(scalars, *operands)


def pack_rows_kernel(where, own_ref, got_ref, keep, send):
    _, steps, _, part = keep.shape
    for z in range(steps):
        columns = [pl.ds(pl.multiple_of((2 * z + y) * part, 128), part) for y in (where[1], 1 - where[1])]
        keep[0, z] = own_ref[:, columns[0]]
        keep[1, z] = got_ref[:, columns[0]]
        send[z] = own_ref[:, columns[1]]


def pack_rows(where, own, got, y, steps):
    part = own.shape[1] // (2 * steps)
    if part % 128:
        halves = jnp.stack([own, got]).reshape(2, ROWS, steps, 2, part)
        halves = jnp.transpose(halves, (3, 0, 2, 1, 4))
        keep, send = [lax.dynamic_index_in_dim(halves, i, axis=0, keepdims=False) for i in (y, 1 - y)]
        return keep, send[0]
    shapes = [(2, steps, ROWS, part), (steps, ROWS, part)]
    outs = [jax.ShapeDtypeStruct(shape, own.dtype) for shape in shapes]
    return on_chip(pack_rows_kernel, "pack_rows", outs, where, own, got)


def row_split(rows, i):
    helped = rows * HELP[i] // 10
    return helped, rows - helped


def weight_columns(core, chunk):
    head, heads = chunk
    return pl.ds(pl.multiple_of((core * KVH + head) * HD, 128), heads * HD)


def far_rows_kernel(chunk, where, own_ref, got_ref, far):
    rows, count = own_ref.shape[0], far.shape[0]
    core, place = where[2], where[3] * (2 * rows - count)
    columns = weight_columns(core, chunk)
    if count == rows:
        @pl.when(core == where[3])
        def _():
            far[...] = own_ref[:, columns]

        @pl.when(core != where[3])
        def _():
            far[...] = got_ref[:, columns]
    else:
        for z in range(0, count, 16):
            row = place + z
            from_own = row // rows == core
            inside = pl.ds(pl.multiple_of(lax.rem(row, rows), 16), 16)

            @pl.when(from_own)
            def _():
                far[z : z + 16, :] = own_ref[inside, columns]

            @pl.when(jnp.logical_not(from_own))
            def _():
                far[z : z + 16, :] = got_ref[inside, columns]


def far_rows(where, own, got, i):
    count = row_split(2 * own.shape[0], i)[1]
    out = jax.ShapeDtypeStruct((count, CHUNKS[i][1] * HD), own.dtype)
    return on_chip(functools.partial(far_rows_kernel, CHUNKS[i]), "far_rows", [out], where, own, got)[0]


def whole_rows_kernel(where, own_ref, got_ref, *outs):
    rows, core = own_ref.shape[0], where[2]
    for out, chunk in zip(outs, CHUNKS):
        columns = weight_columns(core, chunk)
        out[pl.ds(pl.multiple_of(core * rows, 16), rows), :] = own_ref[:, columns]
        out[pl.ds(pl.multiple_of((1 - core) * rows, 16), rows), :] = got_ref[:, columns]


def whole_rows(where, own, got):
    outs = [jax.ShapeDtypeStruct((2 * own.shape[0], heads * HD), own.dtype) for _, heads in CHUNKS]
    return list(on_chip(whole_rows_kernel, "whole_rows", outs, where, own, got))


def project_kernel(counts, where, keep, other, other_2, *refs):
    parts = []
    for count in counts:
        parts.append(refs[:count])
        refs = refs[count:]
    near, direct, forwarded, before = parts
    mine, theirs = refs[:2]
    plane = where[3]
    weights = list(enumerate(near))
    for i, piece in enumerate(direct):
        count, rows = piece.shape[0], refs[2].shape[1]
        whole = refs[2].at[i]
        whole[pl.ds(pl.multiple_of(plane * (rows - count), 16), count), :] = piece[...]
        whole[pl.ds(pl.multiple_of((1 - plane) * count, 16), rows - count), :] = forwarded[0][i]
        weights.append((2 + i, whole))
    total = None
    if before:
        total = jnp.concatenate([ref[i] for ref in before for i in range(2)], axis=0)
    for j, weight in weights:
        place = where[0] ^ j
        left = jnp.concatenate([keep[0, place], keep[1, place], other[place], other_2[place]], axis=0)
        product = jnp.dot(left, weight[...], preferred_element_type=jnp.float32)
        total = product if total is None else total + product
    for i in range(2):
        mine[i] = total[i * ROWS : (i + 1) * ROWS]
        theirs[i] = total[(2 + i) * ROWS : (3 + i) * ROWS]


def project(where, rows_of_x, near=(), direct=(), forwarded=(), before=()):
    width = (near or direct)[0].shape[1]
    out = jax.ShapeDtypeStruct((2, ROWS, width), jnp.float32)
    scratch = []
    if direct:
        rows = direct[0].shape[0] + forwarded[0].shape[1]
        scratch.append(pltpu.VMEM((len(direct), rows, width), jnp.bfloat16))
    operands = [near, direct, forwarded, before]
    return on_chip(
        functools.partial(project_kernel, [len(part) for part in operands]),
        "project",
        [out, out],
        where,
        *rows_of_x,
        *[array for part in operands for array in part],
        scratch=scratch,
    )


def final_kernel(chunk, offset, info, gain_ref, q_ref, acc_ref, ml_ref, mine, theirs, there, there_2, *refs):
    result, built, sem = refs[-3:]
    head, heads = chunk
    slot = lax.broadcasted_iota(jnp.int32, (ROWS, PAIR), 0)
    row = lax.broadcasted_iota(jnp.int32, (ROWS, PAIR), 1) % ROWS
    length = jnp.where(row < RLEN, info[0], info[1])
    base = jnp.where(row < RLEN, 0, RLEN)
    seen = (slot >= base) & (slot <= row) & (slot - base < length)
    live = jnp.where(row - base < length, 1.0, 0.0)[0:1]
    copies = []
    for k in range(heads):
        part = slice(k * HD, (k + 1) * HD)
        here = mine[0, :, part] + theirs[0, :, part]
        away = there[0, :, part] + there_2[0, :, part]
        first_core = jnp.full(here.shape, info[2]) == 0
        raw = jnp.where(first_core, here, away)
        mean = jnp.mean(raw * raw, axis=1, keepdims=True)
        keys = (raw * lax.rsqrt(mean + 1e-06) * gain_ref[...]).astype(jnp.bfloat16)
        values = jnp.where(first_core, away, here).astype(jnp.bfloat16).T
        pairs = range(0, SHARED, 2)
        products = [scores_of(keys, pair_queries(q_ref, (head + k) * SHARED + g)) for g in pairs]
        for g, scores in zip(pairs, products):
            cols = slice(((offset + k) * SHARED + g) * HD, ((offset + k) * SHARED + g + 2) * HD)
            scores = jnp.where(seen, scores, HIDDEN)
            before = ml_ref[0:1, cols]
            largest = jnp.maximum(jnp.max(scores, axis=0, keepdims=True), before)
            faded = jnp.exp2((before - largest) * SCALE)
            weights = jnp.exp2((scores - largest) * SCALE)
            total = jnp.sum(weights, axis=0, keepdims=True) + faded * ml_ref[1:2, cols]
            acc = jnp.dot(values, weights.astype(jnp.bfloat16), preferred_element_type=jnp.float32)
            acc = (acc + faded * acc_ref[:, cols]) * (live / total)
            acc = acc.astype(jnp.bfloat16)
            built[k, :, g * HD : (g + 1) * HD] = acc[:, :ROWS].T
            built[k, :, (g + 1) * HD : (g + 2) * HD] = acc[:, ROWS:].T
        place = result.at[:, pl.ds((head + k) * GROUP, GROUP)]
        copies.append(pltpu.make_async_copy(built.at[k], place, sem.at[k]))
        copies[-1].start()
    for copy in copies:
        copy.wait()


def final_attention(info, gain, query, state, offset, chunk, mine, theirs, there, result):
    heads = chunk[1]
    operands = [gain, query, *state, mine, theirs, *there]
    specs = [SMEM] + [VMEM] * len(operands)
    aliases = {}
    if result is not None:
        operands.append(result)
        specs.append(pl.BlockSpec(memory_space=pl.ANY))
        aliases = {len(operands): 0}
    return pl.pallas_call(
        functools.partial(final_kernel, chunk, offset),
        in_specs=specs,
        out_specs=pl.BlockSpec(memory_space=pl.ANY),
        out_shape=jax.ShapeDtypeStruct((ROWS, HQ * HD), jnp.bfloat16),
        scratch_shapes=[pltpu.VMEM((heads, ROWS, GROUP), jnp.bfloat16), pltpu.SemaphoreType.DMA((heads,))],
        input_output_aliases=aliases,
        compiler_params=PARAMS,
        cost_estimate=HINT,
        name="final_attention",
    )(info, *operands)


def xor_swap(array, axis, by):
    return lax.ppermute(array, axis, [(i, i ^ by) for i in range(lax.axis_size(axis))])


def per_device(
    x_resp, queries, prompt_cache, kv_weight, key_gain, prompt_lengths, block_table, resp_lengths
):
    x, query = x_resp[0], queries[0]
    steps = lax.axis_size("z")
    z, y, core = lax.axis_index("z"), lax.axis_index("y"), lax.axis_index("core")
    holder, cycle = lax.axis_index("blk"), lax.axis_size("blk")
    plane = holder % 2
    where = jnp.stack([z, y, core, plane]).astype(jnp.int32)

    tie = lax.optimization_barrier

    got_weight = xor_swap(kv_weight, "core", 1)
    got_x = xor_swap(x, "core", 1)
    caches = [prompt_cache[0]]
    for _ in range(cycle - 1):
        caches.append(lax.ppermute(caches[-1], "blk", [(i, (i + 1) % cycle) for i in range(cycle)]))

    far = [far_rows(where, kv_weight, got_weight, 0)]
    whole = whole_rows(where, kv_weight, got_weight)
    far.append(far_rows(where, kv_weight, got_weight, 1))

    def send(far):
        return [xor_swap(far, "z", j) for j in range(2, steps)]

    def forward(i):
        helped, direct = row_split(whole[0].shape[0], i)
        parts = [lax.dynamic_slice_in_dim(p, plane * (direct - helped), helped, axis=0) for p in sent[i]]
        return [xor_swap(jnp.stack(parts), "blk", 1)]

    sent = [send(far[0])]
    near = [xor_swap(whole[0], "z", 1)]
    got_x, whole[1] = tie((got_x, whole[1]))
    keep, given = pack_rows(where, x, got_x, y, steps)
    other = xor_swap(given, "y", 1)

    block_table, _ = tie((block_table, whole[0]))
    infos = []
    for stride in range(cycle):
        owner = lax.rem(holder + cycle - stride, cycle)
        place = owner * prompt_cache.shape[1]
        listed = lax.dynamic_index_in_dim(block_table[0], place // BLOCK, axis=1, keepdims=False)
        infos.append(jnp.concatenate([place[None], prompt_lengths, listed]).astype(jnp.int32))

    query, _, _ = tie((query, whole[0], given))
    state = prompt_attention(infos[0], query, caches[0], None, 0, KVH)

    sent.append([])
    for j, piece in enumerate(sent[0], 2):
        piece, far[1], state = tie((piece, far[1], state))
        sent[0][j - 2] = piece
        sent[1].append(xor_swap(far[1], "z", j))
    sent[0], caches, whole[1] = tie((sent[0], caches, whole[1]))
    near.append(xor_swap(whole[1], "z", 1))
    forwarded = [forward(0)]
    state, other = tie((state, other))
    rows_of_x = [keep, other, xor_swap(other, "core", 1)]
    for stride in range(1, cycle):
        state = prompt_attention(infos[stride], query, caches[stride], state, 0, KVH)

    def owners(mine, theirs):
        there = [xor_swap(theirs[1:], ("y", "core"), 3), xor_swap(mine[1:], "core", 1)]
        return xor_swap(theirs[:1], "y", 1), there

    forwarded[0], state = tie((forwarded[0], state))
    mine_0, theirs_0 = project(where, rows_of_x, [whole[0], near[0]], sent[0], forwarded[0])
    sent[1], mine_0, theirs_0 = tie((sent[1], mine_0, theirs_0))
    forwarded.append(forward(1))
    here_0, there_0 = owners(mine_0, theirs_0)
    early = project(where, rows_of_x, [whole[1], near[1]])
    forwarded[1], early = tie((forwarded[1], early))
    mine_1, theirs_1 = project(where, rows_of_x, (), sent[1], forwarded[1], early)
    here_0, there_0, mine_1, theirs_1 = tie((here_0, there_0, mine_1, theirs_1))
    here_1, there_1 = owners(mine_1, theirs_1)
    info = jnp.concatenate([resp_lengths[0], core[None]]).astype(jnp.int32)
    gain = key_gain[None]
    result = final_attention(info, gain, query, state, 0, CHUNKS[0], mine_0, here_0, there_0, None)
    result = final_attention(info, gain, query, state, 2, CHUNKS[1], mine_1, here_1, there_1, result)
    return result[None]


def solution(mesh):
    groups, blocks = mesh.devices.shape
    split = Mesh(mesh.devices.reshape(groups // 4, 2, 2, blocks), ("z", "y", "core", "blk"))
    fsdp = ("z", "y", "core")
    return jax.shard_map(
        per_device,
        mesh=split,
        in_specs=(
            P(fsdp, "blk", None),
            P(fsdp, "blk", None),
            P(fsdp, "blk", None),
            P(fsdp, None),
            P(),
            P(fsdp),
            P(fsdp, "blk", None),
            P(fsdp, "blk"),
        ),
        out_specs=P(fsdp, "blk", None),
        check_vma=False,
    )
```

```python
import functools

import jax
import jax.numpy as jnp
from jax import lax
from jax.experimental import pallas as pl
from jax.experimental.pallas import tpu as pltpu
from jax.sharding import Mesh
from jax.sharding import PartitionSpec as P

HQ = 32
KVH = 4
HD = 128
SHARED = HQ // KVH
BLOCK = 512
RESP_DEV = 2
RLEN = 64
ROWS = RESP_DEV * RLEN
PAIR = 2 * ROWS
GROUP = SHARED * HD
SCALE = HD ** (-0.5) * 1.4426950408889634
HIDDEN = -1e30
NT = (((1,), (1,)), ((), ()))
HINT = pl.CostEstimate(flops=1024, bytes_accessed=1024, transcendentals=0)

CHUNKS = ((0, 2), (2, 1), (3, 1))
HELP = (5, 5, 5)


def pair_queries(q_ref, g, extra=None):
    heads = [q_ref[:, i * HD : (i + 1) * HD] for i in (g, g + 1)]
    if extra is not None:
        heads = [jnp.concatenate([head, extra], axis=1) for head in heads]
    return jnp.concatenate(heads, axis=0)


def scores_of(keys, queries):
    return lax.dot_general(keys, queries, NT, preferred_element_type=jnp.float32)


def prompt_kernel(first, info, q_ref, k_ref, v_ref, *refs):
    if first:
        acc_ref, ml_ref = refs
    else:
        old_acc, old_ml, acc_ref, ml_ref = refs
    count = k_ref.shape[0]
    place = info[0] + lax.broadcasted_iota(jnp.int32, (count, HD), 0)
    column = lax.broadcasted_iota(jnp.int32, (count, HD), 1)
    listed = jnp.where(column == 0, info[2], info[3])
    hidden = (column < RESP_DEV) & ((place >= info[1]) | (listed != 1))
    keys = jnp.concatenate([k_ref[...], jnp.where(hidden, HIDDEN, 0.0).astype(jnp.bfloat16)], axis=1)
    owner = lax.broadcasted_iota(jnp.int32, (ROWS, HD), 0) // RLEN
    ours = jnp.where(owner == lax.broadcasted_iota(jnp.int32, (ROWS, HD), 1), 1.0, 0.0).astype(jnp.bfloat16)
    values = v_ref[...].T
    ahead = scores_of(keys, pair_queries(q_ref, 0, ours))
    for g in range(0, SHARED, 2):
        cols = slice(g * HD, (g + 2) * HD)
        scores = ahead
        if g + 2 < SHARED:
            ahead = scores_of(keys, pair_queries(q_ref, g + 2, ours))
        largest = jnp.max(scores, axis=0, keepdims=True)
        if not first:
            before = old_ml[0:1, cols]
            largest = jnp.maximum(largest, before)
            faded = jnp.exp2((before - largest) * SCALE)
        weights = jnp.exp2((scores - largest) * SCALE)
        total = jnp.sum(weights, axis=0, keepdims=True)
        acc = jnp.dot(values, weights.astype(jnp.bfloat16), preferred_element_type=jnp.float32)
        if not first:
            total = total + faded * old_ml[1:2, cols]
            acc = acc + faded * old_acc[:, cols]
        acc_ref[:, cols] = acc
        ml_ref[0:1, cols] = largest
        ml_ref[1:2, cols] = total


def prompt_attention(info, query, cache, state, head, heads, offset=0):
    count = cache.shape[0]
    first = state is None
    wide = pl.BlockSpec((ROWS, GROUP), lambda k, s: (0, head + k))
    turned = pl.BlockSpec((HD, SHARED * ROWS), lambda k, s: (0, k))
    small = pl.BlockSpec((8, SHARED * ROWS), lambda k, s: (0, k))
    specs = [
        wide,
        pl.BlockSpec((count, HD), lambda k, s: (0, head + k)),
        pl.BlockSpec((count, HD), lambda k, s: (0, KVH + head + k)),
    ]
    operands = [query, cache, cache]
    if not first:
        specs += [
            pl.BlockSpec((HD, SHARED * ROWS), lambda k, s: (0, offset + k)),
            pl.BlockSpec((8, SHARED * ROWS), lambda k, s: (0, offset + k)),
        ]
        operands += list(state)
    return pl.pallas_call(
        functools.partial(prompt_kernel, first),
        grid_spec=pltpu.PrefetchScalarGridSpec(
            num_scalar_prefetch=1, grid=(heads,), in_specs=specs, out_specs=[turned, small]
        ),
        out_shape=[
            jax.ShapeDtypeStruct((HD, heads * SHARED * ROWS), jnp.float32),
            jax.ShapeDtypeStruct((8, heads * SHARED * ROWS), jnp.float32),
        ],
        compiler_params=pltpu.CompilerParams(vmem_limit_bytes=32 * 2**20),
        cost_estimate=pl.CostEstimate(
            flops=2**34 if first else 2**33, bytes_accessed=1024, transcendentals=0
        ),
        name="prompt_attention",
    )(info, *operands)


VMEM = pl.BlockSpec(memory_space=pltpu.VMEM)
SMEM = pl.BlockSpec(memory_space=pltpu.SMEM)
PARAMS = pltpu.CompilerParams(vmem_limit_bytes=32 * 2**20)


def on_chip(kernel, name, outs, scalars, *operands, scratch=()):
    return pl.pallas_call(
        kernel,
        in_specs=[SMEM] + [VMEM] * len(operands),
        out_specs=[VMEM] * len(outs),
        out_shape=outs,
        scratch_shapes=scratch,
        compiler_params=PARAMS,
        cost_estimate=HINT,
        name=name,
    )(scalars, *operands)


def pack_rows_kernel(where, own_ref, got_ref, keep, send):
    _, steps, _, part = keep.shape
    for z in range(steps):
        columns = [pl.ds(pl.multiple_of((2 * z + y) * part, 128), part) for y in (where[1], 1 - where[1])]
        keep[0, z] = own_ref[:, columns[0]]
        keep[1, z] = got_ref[:, columns[0]]
        send[z] = own_ref[:, columns[1]]


def pack_rows(where, own, got, y, steps):
    part = own.shape[1] // (2 * steps)
    if part % 128:
        halves = jnp.stack([own, got]).reshape(2, ROWS, steps, 2, part)
        halves = jnp.transpose(halves, (3, 0, 2, 1, 4))
        keep, send = [lax.dynamic_index_in_dim(halves, i, axis=0, keepdims=False) for i in (y, 1 - y)]
        return keep, send[0]
    shapes = [(2, steps, ROWS, part), (steps, ROWS, part)]
    outs = [jax.ShapeDtypeStruct(shape, own.dtype) for shape in shapes]
    return on_chip(pack_rows_kernel, "pack_rows", outs, where, own, got)


def row_split(rows, i):
    helped = rows * HELP[i] // 10
    return helped, rows - helped


def own_rows_kernel(where, weight_ref, *outs):
    rows = weight_ref.shape[0]
    for out, (head, heads) in zip(outs, CHUNKS):
        columns = pl.ds(pl.multiple_of((where[2] * KVH + head) * HD, 128), heads * HD)
        out[pl.ds(pl.multiple_of(where[2] * rows, 16), rows), :] = weight_ref[:, columns]


def own_rows(where, weight):
    outs = [jax.ShapeDtypeStruct((2 * weight.shape[0], heads * HD), weight.dtype) for _, heads in CHUNKS]
    return on_chip(own_rows_kernel, "own_rows", outs, where, weight)


def pack_weight_kernel(where, got_ref, *refs):
    count = len(CHUNKS)
    wholes, fars = refs[count : 2 * count], refs[2 * count :]
    rows = got_ref.shape[0]
    core, plane = where[2], where[3]
    for whole, far, (head, heads) in zip(wholes, fars, CHUNKS):
        columns = pl.ds(pl.multiple_of((core * KVH + head) * HD, 128), heads * HD)
        whole[pl.ds(pl.multiple_of((1 - core) * rows, 16), rows), :] = got_ref[:, columns]
        direct = far.shape[0]
        far[...] = whole[pl.ds(pl.multiple_of(plane * (2 * rows - direct), 16), direct), :]


def pack_weight(where, got, wholes):
    count = len(CHUNKS)
    outs = [jax.ShapeDtypeStruct(whole.shape, whole.dtype) for whole in wholes]
    for i, whole in enumerate(wholes):
        outs.append(jax.ShapeDtypeStruct((row_split(whole.shape[0], i)[1], whole.shape[1]), whole.dtype))
    outs = pl.pallas_call(
        pack_weight_kernel,
        in_specs=[SMEM] + [VMEM] * (1 + count),
        out_specs=[VMEM] * len(outs),
        out_shape=outs,
        input_output_aliases={2 + i: i for i in range(count)},
        compiler_params=PARAMS,
        cost_estimate=HINT,
        name="pack_weight",
    )(where, got, *wholes)
    return list(outs[:count]), list(outs[count:])


def project_kernel(where, keep, other, other_2, own, near, *refs):
    mine, theirs, whole = refs[-3:]
    far = whole.shape[0]
    direct, forwarded = refs[:far], refs[far:-3]
    plane = where[3]
    count, extra = direct[0].shape[0], whole.shape[1] - direct[0].shape[0]
    total = None
    for j in range(2 + far):
        if j == 0:
            weight = own[...]
        elif j == 1:
            weight = near[...]
        else:
            piece = whole.at[j - 2]
            piece[pl.ds(pl.multiple_of(plane * extra, 16), count), :] = direct[j - 2][...]
            rest = forwarded[0][j - 2] if len(forwarded) == 1 else forwarded[j - 2][...]
            piece[pl.ds(pl.multiple_of((1 - plane) * count, 16), extra), :] = rest
            weight = piece[...]
        place = where[0] ^ j
        left = jnp.concatenate([keep[0, place], keep[1, place], other[place], other_2[place]], axis=0)
        product = jnp.dot(left, weight, preferred_element_type=jnp.float32)
        total = product if total is None else total + product
    for i in range(2):
        mine[i] = total[i * ROWS : (i + 1) * ROWS]
        theirs[i] = total[(2 + i) * ROWS : (3 + i) * ROWS]


def project(where, rows_of_x, own, near, direct, forwarded):
    width = own.shape[1]
    out = jax.ShapeDtypeStruct((2, ROWS, width), jnp.float32)
    return on_chip(
        project_kernel,
        "project",
        [out, out],
        where,
        *rows_of_x,
        own,
        near,
        *direct,
        *forwarded,
        scratch=[pltpu.VMEM((len(direct), own.shape[0], width), jnp.bfloat16)],
    )


def final_kernel(counts, head, info, gain_ref, q_ref, acc_ref, ml_ref, *refs):
    result, built, sem = refs[-3:]
    parts = []
    for count in counts:
        mine, here, *away = refs[:count]
        refs = refs[count:]
        for column in range(0, mine.shape[2], HD):
            parts.append((mine, here, away, slice(column, column + HD)))
    slot = lax.broadcasted_iota(jnp.int32, (ROWS, PAIR), 0)
    row = lax.broadcasted_iota(jnp.int32, (ROWS, PAIR), 1) % ROWS
    length = jnp.where(row < RLEN, info[0], info[1])
    base = jnp.where(row < RLEN, 0, RLEN)
    seen = (slot >= base) & (slot <= row) & (slot - base < length)
    live = jnp.where(row - base < length, 1.0, 0.0)[0:1]
    copies = []
    for k, (mine, here, away, part) in enumerate(parts):
        here = mine[0, :, part] + here[0, :, part]
        away = sum(ref[0, :, part] for ref in away)
        first_core = jnp.full(here.shape, info[2]) == 0
        raw = jnp.where(first_core, here, away)
        mean = jnp.mean(raw * raw, axis=1, keepdims=True)
        keys = (raw * lax.rsqrt(mean + 1e-06) * gain_ref[...]).astype(jnp.bfloat16)
        values = jnp.where(first_core, away, here).T.astype(jnp.bfloat16)
        pairs = range(0, SHARED, 2)
        products = [scores_of(keys, pair_queries(q_ref, (head + k) * SHARED + g)) for g in pairs]
        for g, scores in zip(pairs, products):
            cols = slice((k * SHARED + g) * HD, (k * SHARED + g + 2) * HD)
            scores = jnp.where(seen, scores, HIDDEN)
            before = ml_ref[0:1, cols]
            largest = jnp.maximum(jnp.max(scores, axis=0, keepdims=True), before)
            faded = jnp.exp2((before - largest) * SCALE)
            weights = jnp.exp2((scores - largest) * SCALE)
            total = jnp.sum(weights, axis=0, keepdims=True) + faded * ml_ref[1:2, cols]
            acc = jnp.dot(values, weights.astype(jnp.bfloat16), preferred_element_type=jnp.float32)
            acc = (acc + faded * acc_ref[:, cols]) * (live / total)
            built[k, :, g * HD : (g + 1) * HD] = acc[:, :ROWS].T.astype(jnp.bfloat16)
            built[k, :, (g + 1) * HD : (g + 2) * HD] = acc[:, ROWS:].T.astype(jnp.bfloat16)
        place = result.at[:, pl.ds((head + k) * GROUP, GROUP)]
        copies.append(pltpu.make_async_copy(built.at[k], place, sem.at[k]))
        copies[-1].start()
    for copy in copies:
        copy.wait()


def final_attention(info, gain, query, state, head, chunks, result):
    heads = sum(chunk[0].shape[2] for chunk in chunks) // HD
    operands = [gain, query, *state, *[array for chunk in chunks for array in chunk]]
    specs = [SMEM] + [VMEM] * len(operands)
    aliases = {}
    if result is not None:
        operands.append(result)
        specs.append(pl.BlockSpec(memory_space=pl.ANY))
        aliases = {len(operands): 0}
    return pl.pallas_call(
        functools.partial(final_kernel, [len(chunk) for chunk in chunks], head),
        in_specs=specs,
        out_specs=pl.BlockSpec(memory_space=pl.ANY),
        out_shape=jax.ShapeDtypeStruct((ROWS, HQ * HD), jnp.bfloat16),
        scratch_shapes=[pltpu.VMEM((heads, ROWS, GROUP), jnp.bfloat16), pltpu.SemaphoreType.DMA((heads,))],
        input_output_aliases=aliases,
        compiler_params=PARAMS,
        cost_estimate=HINT,
        name="final_attention",
    )(info, *operands)


def xor_swap(array, axis, by):
    return lax.ppermute(array, axis, [(i, i ^ by) for i in range(lax.axis_size(axis))])


def per_device(
    x_resp, queries, prompt_cache, kv_weight, key_gain, prompt_lengths, block_table, resp_lengths
):
    x, query = x_resp[0], queries[0]
    steps = lax.axis_size("z")
    z, y, core = lax.axis_index("z"), lax.axis_index("y"), lax.axis_index("core")
    holder, cycle = lax.axis_index("blk"), lax.axis_size("blk")
    plane = holder % 2
    where = jnp.stack([z, y, core, plane]).astype(jnp.int32)

    tie = lax.optimization_barrier

    got_weight = xor_swap(kv_weight, "core", 1)
    got_x = xor_swap(x, "core", 1)
    caches = [prompt_cache[0]]
    for _ in range(cycle - 1):
        caches.append(lax.ppermute(caches[-1], "blk", [(i, (i + 1) % cycle) for i in range(cycle)]))

    wholes, got_weight = tie((own_rows(where, kv_weight), got_weight))
    whole, far = pack_weight(where, got_weight, wholes)

    def send(far):
        return [xor_swap(far, "z", j) for j in range(2, steps)]

    def forward(i, stacked):
        helped, direct = row_split(whole[0].shape[0], i)
        parts = [lax.dynamic_slice_in_dim(p, plane * (direct - helped), helped, axis=0) for p in sent[i]]
        return [xor_swap(part, "blk", 1) for part in ([jnp.stack(parts)] if stacked else parts)]

    sent = [send(far[0])]
    near = [xor_swap(whole[0], "z", 1)]
    got_x, whole[1] = tie((got_x, whole[1]))
    keep, given = pack_rows(where, x, got_x, y, steps)
    other = xor_swap(given, "y", 1)

    block_table, _ = tie((block_table, whole[0]))
    infos = []
    for stride in range(cycle):
        owner = lax.rem(holder + cycle - stride, cycle)
        place = owner * prompt_cache.shape[1]
        listed = lax.dynamic_index_in_dim(block_table[0], place // BLOCK, axis=1, keepdims=False)
        infos.append(jnp.concatenate([place[None], prompt_lengths, listed]).astype(jnp.int32))

    query, _, _ = tie((query, whole[0], given))
    state = prompt_attention(infos[0], query, caches[0], None, 0, KVH)

    def rest(head, state):
        offset = head
        for stride in range(1, cycle):
            state = prompt_attention(infos[stride], query, caches[stride], state, head, 2, offset)
            offset = 0
        return state

    def sums(i):
        return project(where, rows_of_x, whole[i], near[i], sent[i], forwarded[i])

    sent[0], state, far[1], whole[1] = tie((sent[0], state, far[1], whole[1]))
    sent.append(send(far[1]))
    near.append(xor_swap(whole[1], "z", 1))
    sent[0], caches = tie((sent[0], caches))
    forwarded = [forward(0, True)]
    state, other = tie((state, other))
    rows_of_x = [keep, other, xor_swap(other, "core", 1)]
    halves = [rest(0, state)]
    sent[1], near[0], far[2], halves[0], state, rows_of_x[2] = tie((sent[1], near[0], far[2], halves[0], state, rows_of_x[2]))
    sent.append(send(far[2]))
    forwarded[0], sent[1], whole[2] = tie((forwarded[0], sent[1], whole[2]))
    forwarded.append(forward(1, True))
    near.append(xor_swap(whole[2], "z", 1))

    def owners(mine, theirs):
        there = [xor_swap(theirs[1:], ("y", "core"), 3), xor_swap(mine[1:], "core", 1)]
        return [mine, xor_swap(theirs[:1], "y", 1), *there]

    mine_0, theirs_0 = sums(0)
    state, mine_0 = tie((state, mine_0))
    halves.append(rest(2, state))
    sent[2], mine_0, halves[1] = tie((sent[2], mine_0, halves[1]))
    forwarded.append(forward(2, True))
    here_0 = xor_swap(theirs_0, "y", 1)
    forwarded[1], mine_0 = tie((forwarded[1], mine_0))
    mine_1, theirs_1 = sums(1)
    here_0, mine_1, theirs_1 = tie((here_0, mine_1, theirs_1))
    first = [mine_0, here_0, xor_swap(mine_0[1:] + here_0[1:], "core", 1)]
    here_1 = xor_swap(theirs_1, "y", 1)
    forwarded[2], mine_1 = tie((forwarded[2], mine_1))
    mine_2, theirs_2 = sums(2)
    third = owners(mine_2, theirs_2)
    second = [mine_1, here_1, xor_swap(mine_1[1:] + here_1[1:], "core", 1)]
    info = jnp.concatenate([resp_lengths[0], core[None]]).astype(jnp.int32)
    gain = key_gain[None]
    result = final_attention(info, gain, query, halves[0], 0, [first], None)
    return final_attention(info, gain, query, halves[1], 2, [second, third], result)[None]


def solution(mesh):
    groups, blocks = mesh.devices.shape
    split = Mesh(mesh.devices.reshape(groups // 4, 2, 2, blocks), ("z", "y", "core", "blk"))
    fsdp = ("z", "y", "core")
    return jax.shard_map(
        per_device,
        mesh=split,
        in_specs=(
            P(fsdp, "blk", None),
            P(fsdp, "blk", None),
            P(fsdp, "blk", None),
            P(fsdp, None),
            P(),
            P(fsdp),
            P(fsdp, "blk", None),
            P(fsdp, "blk"),
        ),
        out_specs=P(fsdp, "blk", None),
        check_vma=False,
    )
```

```python
import functools

import jax
import jax.numpy as jnp
from jax import lax
from jax.experimental import pallas as pl
from jax.experimental.pallas import tpu as pltpu
from jax.sharding import Mesh
from jax.sharding import PartitionSpec as P

HQ = 32
KVH = 4
HD = 128
SHARED = HQ // KVH
BLOCK = 512
RESP_DEV = 2
RLEN = 64
ROWS = RESP_DEV * RLEN
PAIR = 2 * ROWS
GROUP = SHARED * HD
SCALE = HD ** (-0.5) * 1.4426950408889634
HIDDEN = -1e30
NT = (((1,), (1,)), ((), ()))
HINT = pl.CostEstimate(flops=1024, bytes_accessed=1024, transcendentals=0)

CHUNKS = ((0, 2), (2, 1), (3, 1))
HELP = (5, 5, 5)


def pair_queries(q_ref, g, extra=None):
    heads = [q_ref[:, i * HD : (i + 1) * HD] for i in (g, g + 1)]
    if extra is not None:
        heads = [jnp.concatenate([head, extra], axis=1) for head in heads]
    return jnp.concatenate(heads, axis=0)


def scores_of(keys, queries):
    return lax.dot_general(keys, queries, NT, preferred_element_type=jnp.float32)


def prompt_kernel(first, info, q_ref, k_ref, v_ref, *refs):
    if first:
        acc_ref, ml_ref = refs
    else:
        old_acc, old_ml, acc_ref, ml_ref = refs
    count = k_ref.shape[0]
    place = info[0] + lax.broadcasted_iota(jnp.int32, (count, HD), 0)
    column = lax.broadcasted_iota(jnp.int32, (count, HD), 1)
    listed = jnp.where(column == 0, info[2], info[3])
    hidden = (column < RESP_DEV) & ((place >= info[1]) | (listed != 1))
    keys = jnp.concatenate([k_ref[...], jnp.where(hidden, HIDDEN, 0.0).astype(jnp.bfloat16)], axis=1)
    owner = lax.broadcasted_iota(jnp.int32, (ROWS, HD), 0) // RLEN
    ours = jnp.where(owner == lax.broadcasted_iota(jnp.int32, (ROWS, HD), 1), 1.0, 0.0).astype(jnp.bfloat16)
    values = v_ref[...].T
    ahead = scores_of(keys, pair_queries(q_ref, 0, ours))
    for g in range(0, SHARED, 2):
        cols = slice(g * HD, (g + 2) * HD)
        scores = ahead
        if g + 2 < SHARED:
            ahead = scores_of(keys, pair_queries(q_ref, g + 2, ours))
        largest = jnp.max(scores, axis=0, keepdims=True)
        if not first:
            before = old_ml[0:1, cols]
            largest = jnp.maximum(largest, before)
            faded = jnp.exp2((before - largest) * SCALE)
        weights = jnp.exp2((scores - largest) * SCALE)
        total = jnp.sum(weights, axis=0, keepdims=True)
        acc = jnp.dot(values, weights.astype(jnp.bfloat16), preferred_element_type=jnp.float32)
        if not first:
            total = total + faded * old_ml[1:2, cols]
            acc = acc + faded * old_acc[:, cols]
        acc_ref[:, cols] = acc
        ml_ref[0:1, cols] = largest
        ml_ref[1:2, cols] = total


def prompt_attention(info, query, cache, state, head, heads, offset=0):
    count = cache.shape[0]
    first = state is None
    wide = pl.BlockSpec((ROWS, GROUP), lambda k, s: (0, head + k))
    turned = pl.BlockSpec((HD, SHARED * ROWS), lambda k, s: (0, k))
    small = pl.BlockSpec((8, SHARED * ROWS), lambda k, s: (0, k))
    specs = [
        wide,
        pl.BlockSpec((count, HD), lambda k, s: (0, head + k)),
        pl.BlockSpec((count, HD), lambda k, s: (0, KVH + head + k)),
    ]
    operands = [query, cache, cache]
    if not first:
        specs += [
            pl.BlockSpec((HD, SHARED * ROWS), lambda k, s: (0, offset + k)),
            pl.BlockSpec((8, SHARED * ROWS), lambda k, s: (0, offset + k)),
        ]
        operands += list(state)
    return pl.pallas_call(
        functools.partial(prompt_kernel, first),
        grid_spec=pltpu.PrefetchScalarGridSpec(
            num_scalar_prefetch=1, grid=(heads,), in_specs=specs, out_specs=[turned, small]
        ),
        out_shape=[
            jax.ShapeDtypeStruct((HD, heads * SHARED * ROWS), jnp.float32),
            jax.ShapeDtypeStruct((8, heads * SHARED * ROWS), jnp.float32),
        ],
        compiler_params=pltpu.CompilerParams(vmem_limit_bytes=32 * 2**20),
        cost_estimate=pl.CostEstimate(
            flops=2**34 if first else 2**33, bytes_accessed=1024, transcendentals=0
        ),
        name="prompt_attention",
    )(info, *operands)


VMEM = pl.BlockSpec(memory_space=pltpu.VMEM)
SMEM = pl.BlockSpec(memory_space=pltpu.SMEM)
PARAMS = pltpu.CompilerParams(vmem_limit_bytes=32 * 2**20)


def on_chip(kernel, name, outs, scalars, *operands, scratch=()):
    return pl.pallas_call(
        kernel,
        in_specs=[SMEM] + [VMEM] * len(operands),
        out_specs=[VMEM] * len(outs),
        out_shape=outs,
        scratch_shapes=scratch,
        compiler_params=PARAMS,
        cost_estimate=HINT,
        name=name,
    )(scalars, *operands)


def pack_rows_kernel(where, own_ref, got_ref, keep, send):
    _, steps, _, part = keep.shape
    for z in range(steps):
        columns = [pl.ds(pl.multiple_of((2 * z + y) * part, 128), part) for y in (where[1], 1 - where[1])]
        keep[0, z] = own_ref[:, columns[0]]
        keep[1, z] = got_ref[:, columns[0]]
        send[z] = own_ref[:, columns[1]]


def pack_rows(where, own, got, y, steps):
    part = own.shape[1] // (2 * steps)
    if part % 128:
        halves = jnp.stack([own, got]).reshape(2, ROWS, steps, 2, part)
        halves = jnp.transpose(halves, (3, 0, 2, 1, 4))
        keep, send = [lax.dynamic_index_in_dim(halves, i, axis=0, keepdims=False) for i in (y, 1 - y)]
        return keep, send[0]
    shapes = [(2, steps, ROWS, part), (steps, ROWS, part)]
    outs = [jax.ShapeDtypeStruct(shape, own.dtype) for shape in shapes]
    return on_chip(pack_rows_kernel, "pack_rows", outs, where, own, got)


def row_split(rows, i):
    helped = rows * HELP[i] // 10
    return helped, rows - helped


def own_rows_kernel(where, weight_ref, *outs):
    rows = weight_ref.shape[0]
    for out, (head, heads) in zip(outs, CHUNKS):
        columns = pl.ds(pl.multiple_of((where[2] * KVH + head) * HD, 128), heads * HD)
        out[pl.ds(pl.multiple_of(where[2] * rows, 16), rows), :] = weight_ref[:, columns]


def own_rows(where, weight):
    outs = [jax.ShapeDtypeStruct((2 * weight.shape[0], heads * HD), weight.dtype) for _, heads in CHUNKS]
    return on_chip(own_rows_kernel, "own_rows", outs, where, weight)


def pack_weight_kernel(where, got_ref, *refs):
    count = len(CHUNKS)
    wholes, fars = refs[count : 2 * count], refs[2 * count :]
    rows = got_ref.shape[0]
    core, plane = where[2], where[3]
    for whole, far, (head, heads) in zip(wholes, fars, CHUNKS):
        columns = pl.ds(pl.multiple_of((core * KVH + head) * HD, 128), heads * HD)
        whole[pl.ds(pl.multiple_of((1 - core) * rows, 16), rows), :] = got_ref[:, columns]
        direct = far.shape[0]
        far[...] = whole[pl.ds(pl.multiple_of(plane * (2 * rows - direct), 16), direct), :]


def pack_weight(where, got, wholes):
    count = len(CHUNKS)
    outs = [jax.ShapeDtypeStruct(whole.shape, whole.dtype) for whole in wholes]
    for i, whole in enumerate(wholes):
        outs.append(jax.ShapeDtypeStruct((row_split(whole.shape[0], i)[1], whole.shape[1]), whole.dtype))
    outs = pl.pallas_call(
        pack_weight_kernel,
        in_specs=[SMEM] + [VMEM] * (1 + count),
        out_specs=[VMEM] * len(outs),
        out_shape=outs,
        input_output_aliases={2 + i: i for i in range(count)},
        compiler_params=PARAMS,
        cost_estimate=HINT,
        name="pack_weight",
    )(where, got, *wholes)
    return list(outs[:count]), list(outs[count:])


def project_kernel(where, keep, other, other_2, own, near, *refs):
    mine, theirs, whole = refs[-3:]
    far = whole.shape[0]
    direct, forwarded = refs[:far], refs[far:-3]
    plane = where[3]
    count, extra = direct[0].shape[0], whole.shape[1] - direct[0].shape[0]
    total = None
    for j in range(2 + far):
        if j == 0:
            weight = own[...]
        elif j == 1:
            weight = near[...]
        else:
            piece = whole.at[j - 2]
            piece[pl.ds(pl.multiple_of(plane * extra, 16), count), :] = direct[j - 2][...]
            rest = forwarded[0][j - 2] if len(forwarded) == 1 else forwarded[j - 2][...]
            piece[pl.ds(pl.multiple_of((1 - plane) * count, 16), extra), :] = rest
            weight = piece[...]
        place = where[0] ^ j
        left = jnp.concatenate([keep[0, place], keep[1, place], other[place], other_2[place]], axis=0)
        product = jnp.dot(left, weight, preferred_element_type=jnp.float32)
        total = product if total is None else total + product
    for i in range(2):
        mine[i] = total[i * ROWS : (i + 1) * ROWS]
        theirs[i] = total[(2 + i) * ROWS : (3 + i) * ROWS]


def project(where, rows_of_x, own, near, direct, forwarded):
    width = own.shape[1]
    out = jax.ShapeDtypeStruct((2, ROWS, width), jnp.float32)
    return on_chip(
        project_kernel,
        "project",
        [out, out],
        where,
        *rows_of_x,
        own,
        near,
        *direct,
        *forwarded,
        scratch=[pltpu.VMEM((len(direct), own.shape[0], width), jnp.bfloat16)],
    )


def final_kernel(counts, info, gain_ref, q_ref, *refs):
    result, built, sem = refs[-3:]
    states, refs = (refs[:2], refs[2:4]), refs[4:]
    parts = []
    for count in counts:
        mine, here, *away = refs[:count]
        refs = refs[count:]
        for column in range(0, mine.shape[2], HD):
            parts.append((mine, here, away, slice(column, column + HD)))
    slot = lax.broadcasted_iota(jnp.int32, (ROWS, PAIR), 0)
    row = lax.broadcasted_iota(jnp.int32, (ROWS, PAIR), 1) % ROWS
    length = jnp.where(row < RLEN, info[0], info[1])
    base = jnp.where(row < RLEN, 0, RLEN)
    seen = (slot >= base) & (slot <= row) & (slot - base < length)
    live = jnp.where(row - base < length, 1.0, 0.0)[0:1]
    copies = []
    for k, (mine, here, away, part) in enumerate(parts):
        acc_ref, ml_ref = states[k // 2]
        here = mine[0, :, part] + here[0, :, part]
        away = sum(ref[0, :, part] for ref in away)
        first_core = jnp.full(here.shape, info[2]) == 0
        raw = jnp.where(first_core, here, away)
        mean = jnp.mean(raw * raw, axis=1, keepdims=True)
        keys = (raw * lax.rsqrt(mean + 1e-06) * gain_ref[...]).astype(jnp.bfloat16)
        values = jnp.where(first_core, away, here).T.astype(jnp.bfloat16)
        pairs = range(0, SHARED, 2)
        products = [scores_of(keys, pair_queries(q_ref, k * SHARED + g)) for g in pairs]
        for g, scores in zip(pairs, products):
            cols = slice((k % 2 * SHARED + g) * HD, (k % 2 * SHARED + g + 2) * HD)
            scores = jnp.where(seen, scores, HIDDEN)
            before = ml_ref[0:1, cols]
            largest = jnp.maximum(jnp.max(scores, axis=0, keepdims=True), before)
            faded = jnp.exp2((before - largest) * SCALE)
            weights = jnp.exp2((scores - largest) * SCALE)
            total = jnp.sum(weights, axis=0, keepdims=True) + faded * ml_ref[1:2, cols]
            acc = jnp.dot(values, weights.astype(jnp.bfloat16), preferred_element_type=jnp.float32)
            acc = (acc + faded * acc_ref[:, cols]) * (live / total)
            built[k, :, g * HD : (g + 1) * HD] = acc[:, :ROWS].T.astype(jnp.bfloat16)
            built[k, :, (g + 1) * HD : (g + 2) * HD] = acc[:, ROWS:].T.astype(jnp.bfloat16)
        place = result.at[:, pl.ds(k * GROUP, GROUP)]
        copies.append(pltpu.make_async_copy(built.at[k], place, sem.at[k]))
        copies[-1].start()
    for copy in copies:
        copy.wait()


def final_attention(info, gain, query, states, chunks):
    operands = [gain, query]
    operands += [array for state in states for array in state]
    operands += [array for chunk in chunks for array in chunk]
    return pl.pallas_call(
        functools.partial(final_kernel, [len(chunk) for chunk in chunks]),
        in_specs=[SMEM] + [VMEM] * len(operands),
        out_specs=pl.BlockSpec(memory_space=pl.ANY),
        out_shape=jax.ShapeDtypeStruct((ROWS, HQ * HD), jnp.bfloat16),
        scratch_shapes=[pltpu.VMEM((KVH, ROWS, GROUP), jnp.bfloat16), pltpu.SemaphoreType.DMA((KVH,))],
        compiler_params=PARAMS,
        cost_estimate=HINT,
        name="final_attention",
    )(info, *operands)


def xor_swap(array, axis, by):
    return lax.ppermute(array, axis, [(i, i ^ by) for i in range(lax.axis_size(axis))])


def per_device(
    x_resp, queries, prompt_cache, kv_weight, key_gain, prompt_lengths, block_table, resp_lengths
):
    x, query = x_resp[0], queries[0]
    steps = lax.axis_size("z")
    z, y, core = lax.axis_index("z"), lax.axis_index("y"), lax.axis_index("core")
    holder, cycle = lax.axis_index("blk"), lax.axis_size("blk")
    plane = holder % 2
    where = jnp.stack([z, y, core, plane]).astype(jnp.int32)

    tie = lax.optimization_barrier

    got_weight = xor_swap(kv_weight, "core", 1)
    got_x = xor_swap(x, "core", 1)
    caches = [prompt_cache[0]]
    for _ in range(cycle - 1):
        caches.append(lax.ppermute(caches[-1], "blk", [(i, (i + 1) % cycle) for i in range(cycle)]))

    wholes, got_weight = tie((own_rows(where, kv_weight), got_weight))
    whole, far = pack_weight(where, got_weight, wholes)

    def send(far):
        return [xor_swap(far, "z", j) for j in range(2, steps)]

    def forward(i, stacked):
        helped, direct = row_split(whole[0].shape[0], i)
        parts = [lax.dynamic_slice_in_dim(p, plane * (direct - helped), helped, axis=0) for p in sent[i]]
        return [xor_swap(part, "blk", 1) for part in ([jnp.stack(parts)] if stacked else parts)]

    sent = [send(far[0])]
    near = [xor_swap(whole[0], "z", 1)]
    got_x, whole[1] = tie((got_x, whole[1]))
    keep, given = pack_rows(where, x, got_x, y, steps)
    other = xor_swap(given, "y", 1)

    block_table, _ = tie((block_table, whole[0]))
    infos = []
    for stride in range(cycle):
        owner = lax.rem(holder + cycle - stride, cycle)
        place = owner * prompt_cache.shape[1]
        listed = lax.dynamic_index_in_dim(block_table[0], place // BLOCK, axis=1, keepdims=False)
        infos.append(jnp.concatenate([place[None], prompt_lengths, listed]).astype(jnp.int32))

    query, _, _ = tie((query, whole[0], given))
    state = prompt_attention(infos[0], query, caches[0], None, 0, KVH)

    def rest(head, state):
        offset = head
        for stride in range(1, cycle):
            state = prompt_attention(infos[stride], query, caches[stride], state, head, 2, offset)
            offset = 0
        return state

    def sums(i):
        return project(where, rows_of_x, whole[i], near[i], sent[i], forwarded[i])

    sent[0], state, far[1], whole[1] = tie((sent[0], state, far[1], whole[1]))
    sent.append(send(far[1]))
    near.append(xor_swap(whole[1], "z", 1))
    sent[0], caches = tie((sent[0], caches))
    forwarded = [forward(0, True)]
    state, other = tie((state, other))
    rows_of_x = [keep, other, xor_swap(other, "core", 1)]
    halves = [rest(0, state)]
    sent[1], near[0], far[2], halves[0], state, rows_of_x[2] = tie((sent[1], near[0], far[2], halves[0], state, rows_of_x[2]))
    sent.append(send(far[2]))
    forwarded[0], sent[1], whole[2] = tie((forwarded[0], sent[1], whole[2]))
    forwarded.append(forward(1, True))
    near.append(xor_swap(whole[2], "z", 1))

    def owners(mine, theirs):
        there = [xor_swap(theirs[1:], ("y", "core"), 3), xor_swap(mine[1:], "core", 1)]
        return [mine, xor_swap(theirs[:1], "y", 1), *there]

    mine_0, theirs_0 = sums(0)
    sent[2], mine_0 = tie((sent[2], mine_0))
    forwarded.append(forward(2, True))
    here_0 = xor_swap(theirs_0, "y", 1)
    forwarded[1], mine_0 = tie((forwarded[1], mine_0))
    mine_1, theirs_1 = sums(1)
    here_1 = xor_swap(theirs_1, "y", 1)
    forwarded[2], mine_1, here_0, here_1 = tie((forwarded[2], mine_1, here_0, here_1))
    first = [mine_0, here_0, xor_swap(mine_0[1:] + here_0[1:], "core", 1)]
    mine_2, theirs_2 = sums(2)
    third = owners(mine_2, theirs_2)
    state, mine_2 = tie((state, mine_2))
    halves.append(rest(2, state))
    second = [mine_1, here_1, xor_swap(mine_1[1:] + here_1[1:], "core", 1)]
    info = jnp.concatenate([resp_lengths[0], core[None]]).astype(jnp.int32)
    gain = key_gain[None]
    return final_attention(info, gain, query, halves, [first, second, third])[None]


def solution(mesh):
    groups, blocks = mesh.devices.shape
    split = Mesh(mesh.devices.reshape(groups // 4, 2, 2, blocks), ("z", "y", "core", "blk"))
    fsdp = ("z", "y", "core")
    return jax.shard_map(
        per_device,
        mesh=split,
        in_specs=(
            P(fsdp, "blk", None),
            P(fsdp, "blk", None),
            P(fsdp, "blk", None),
            P(fsdp, None),
            P(),
            P(fsdp),
            P(fsdp, "blk", None),
            P(fsdp, "blk"),
        ),
        out_specs=P(fsdp, "blk", None),
        check_vma=False,
    )
```

```python
import functools

import jax
import jax.numpy as jnp
from jax import lax
from jax.experimental import pallas as pl
from jax.experimental.pallas import tpu as pltpu
from jax.sharding import Mesh
from jax.sharding import PartitionSpec as P

HQ = 32
KVH = 4
HD = 128
SHARED = HQ // KVH
BLOCK = 512
RESP_DEV = 2
RLEN = 64
ROWS = RESP_DEV * RLEN
PAIR = 2 * ROWS
GROUP = SHARED * HD
SCALE = HD ** (-0.5) * 1.4426950408889634
HIDDEN = -1e30
NT = (((1,), (1,)), ((), ()))
HINT = pl.CostEstimate(flops=1024, bytes_accessed=1024, transcendentals=0)

CHUNKS = ((0, 2), (2, 1), (3, 1))
HELP = (5, 5, 5)


def pair_queries(q_ref, g, extra=None):
    heads = [q_ref[:, i * HD : (i + 1) * HD] for i in (g, g + 1)]
    if extra is not None:
        heads = [jnp.concatenate([head, extra], axis=1) for head in heads]
    return jnp.concatenate(heads, axis=0)


def scores_of(keys, queries):
    return lax.dot_general(keys, queries, NT, preferred_element_type=jnp.float32)


def prompt_kernel(first, info, q_ref, k_ref, v_ref, *refs):
    if first:
        acc_ref, ml_ref = refs
    else:
        old_acc, old_ml, acc_ref, ml_ref = refs
    count = k_ref.shape[0]
    place = info[0] + lax.broadcasted_iota(jnp.int32, (count, HD), 0)
    column = lax.broadcasted_iota(jnp.int32, (count, HD), 1)
    listed = jnp.where(column == 0, info[2], info[3])
    hidden = (column < RESP_DEV) & ((place >= info[1]) | (listed != 1))
    keys = jnp.concatenate([k_ref[...], jnp.where(hidden, HIDDEN, 0.0).astype(jnp.bfloat16)], axis=1)
    owner = lax.broadcasted_iota(jnp.int32, (ROWS, HD), 0) // RLEN
    ours = jnp.where(owner == lax.broadcasted_iota(jnp.int32, (ROWS, HD), 1), 1.0, 0.0).astype(jnp.bfloat16)
    values = v_ref[...].T
    ahead = scores_of(keys, pair_queries(q_ref, 0, ours))
    for g in range(0, SHARED, 2):
        cols = slice(g * HD, (g + 2) * HD)
        scores = ahead
        if g + 2 < SHARED:
            ahead = scores_of(keys, pair_queries(q_ref, g + 2, ours))
        largest = jnp.max(scores, axis=0, keepdims=True)
        if not first:
            before = old_ml[0:1, cols]
            largest = jnp.maximum(largest, before)
            faded = jnp.exp2((before - largest) * SCALE)
        weights = jnp.exp2((scores - largest) * SCALE)
        total = jnp.sum(weights, axis=0, keepdims=True)
        acc = jnp.dot(values, weights.astype(jnp.bfloat16), preferred_element_type=jnp.float32)
        if not first:
            total = total + faded * old_ml[1:2, cols]
            acc = acc + faded * old_acc[:, cols]
        acc_ref[:, cols] = acc
        ml_ref[0:1, cols] = largest
        ml_ref[1:2, cols] = total


def prompt_attention(info, query, cache, state, head, heads, offset=0):
    count = cache.shape[0]
    first = state is None
    wide = pl.BlockSpec((ROWS, GROUP), lambda k, s: (0, head + k))
    turned = pl.BlockSpec((HD, SHARED * ROWS), lambda k, s: (0, k))
    small = pl.BlockSpec((8, SHARED * ROWS), lambda k, s: (0, k))
    specs = [
        wide,
        pl.BlockSpec((count, HD), lambda k, s: (0, head + k)),
        pl.BlockSpec((count, HD), lambda k, s: (0, KVH + head + k)),
    ]
    operands = [query, cache, cache]
    if not first:
        specs += [
            pl.BlockSpec((HD, SHARED * ROWS), lambda k, s: (0, offset + k)),
            pl.BlockSpec((8, SHARED * ROWS), lambda k, s: (0, offset + k)),
        ]
        operands += list(state)
    return pl.pallas_call(
        functools.partial(prompt_kernel, first),
        grid_spec=pltpu.PrefetchScalarGridSpec(
            num_scalar_prefetch=1, grid=(heads,), in_specs=specs, out_specs=[turned, small]
        ),
        out_shape=[
            jax.ShapeDtypeStruct((HD, heads * SHARED * ROWS), jnp.float32),
            jax.ShapeDtypeStruct((8, heads * SHARED * ROWS), jnp.float32),
        ],
        compiler_params=pltpu.CompilerParams(vmem_limit_bytes=32 * 2**20),
        cost_estimate=pl.CostEstimate(
            flops=2**34 if first else 2**33, bytes_accessed=1024, transcendentals=0
        ),
        name="prompt_attention",
    )(info, *operands)


VMEM = pl.BlockSpec(memory_space=pltpu.VMEM)
SMEM = pl.BlockSpec(memory_space=pltpu.SMEM)
PARAMS = pltpu.CompilerParams(vmem_limit_bytes=32 * 2**20)


def on_chip(kernel, name, outs, scalars, *operands, scratch=()):
    return pl.pallas_call(
        kernel,
        in_specs=[SMEM] + [VMEM] * len(operands),
        out_specs=[VMEM] * len(outs),
        out_shape=outs,
        scratch_shapes=scratch,
        compiler_params=PARAMS,
        cost_estimate=HINT,
        name=name,
    )(scalars, *operands)


def pack_rows_kernel(where, own_ref, got_ref, keep, send):
    _, steps, _, part = keep.shape
    for z in range(steps):
        columns = [pl.ds(pl.multiple_of((2 * z + y) * part, 128), part) for y in (where[1], 1 - where[1])]
        keep[0, z] = own_ref[:, columns[0]]
        keep[1, z] = got_ref[:, columns[0]]
        send[z] = own_ref[:, columns[1]]


def pack_rows(where, own, got, y, steps):
    part = own.shape[1] // (2 * steps)
    if part % 128:
        halves = jnp.stack([own, got]).reshape(2, ROWS, steps, 2, part)
        halves = jnp.transpose(halves, (3, 0, 2, 1, 4))
        keep, send = [lax.dynamic_index_in_dim(halves, i, axis=0, keepdims=False) for i in (y, 1 - y)]
        return keep, send[0]
    shapes = [(2, steps, ROWS, part), (steps, ROWS, part)]
    outs = [jax.ShapeDtypeStruct(shape, own.dtype) for shape in shapes]
    return on_chip(pack_rows_kernel, "pack_rows", outs, where, own, got)


def row_split(rows, i):
    helped = rows * HELP[i] // 10
    return helped, rows - helped


def own_rows_kernel(where, weight_ref, *outs):
    rows = weight_ref.shape[0]
    for out, (head, heads) in zip(outs, CHUNKS):
        columns = pl.ds(pl.multiple_of((where[2] * KVH + head) * HD, 128), heads * HD)
        out[pl.ds(pl.multiple_of(where[2] * rows, 16), rows), :] = weight_ref[:, columns]


def own_rows(where, weight):
    outs = [jax.ShapeDtypeStruct((2 * weight.shape[0], heads * HD), weight.dtype) for _, heads in CHUNKS]
    return on_chip(own_rows_kernel, "own_rows", outs, where, weight)


def pack_weight_kernel(where, got_ref, *refs):
    count = len(CHUNKS)
    wholes, fars = refs[count : 2 * count], refs[2 * count :]
    rows = got_ref.shape[0]
    core, plane = where[2], where[3]
    for whole, far, (head, heads) in zip(wholes, fars, CHUNKS):
        columns = pl.ds(pl.multiple_of((core * KVH + head) * HD, 128), heads * HD)
        whole[pl.ds(pl.multiple_of((1 - core) * rows, 16), rows), :] = got_ref[:, columns]
        direct = far.shape[0]
        far[...] = whole[pl.ds(pl.multiple_of(plane * (2 * rows - direct), 16), direct), :]


def pack_weight(where, got, wholes):
    count = len(CHUNKS)
    outs = [jax.ShapeDtypeStruct(whole.shape, whole.dtype) for whole in wholes]
    for i, whole in enumerate(wholes):
        outs.append(jax.ShapeDtypeStruct((row_split(whole.shape[0], i)[1], whole.shape[1]), whole.dtype))
    outs = pl.pallas_call(
        pack_weight_kernel,
        in_specs=[SMEM] + [VMEM] * (1 + count),
        out_specs=[VMEM] * len(outs),
        out_shape=outs,
        input_output_aliases={2 + i: i for i in range(count)},
        compiler_params=PARAMS,
        cost_estimate=HINT,
        name="pack_weight",
    )(where, got, *wholes)
    return list(outs[:count]), list(outs[count:])


def project_kernel(where, keep, other, other_2, own, near, *refs):
    mine, theirs, whole = refs[-3:]
    far = whole.shape[0]
    direct, forwarded, joined = refs[:far], refs[far], refs[far + 1 : -3]
    plane = where[3]
    count, extra = direct[0].shape[0], whole.shape[1] - direct[0].shape[0]
    total = None
    for j in range(2 + far):
        if j == 0:
            weight = own[...]
        elif j == 1:
            weight = near[...]
        else:
            piece = whole.at[j - 2]
            piece[pl.ds(pl.multiple_of(plane * extra, 16), count), :] = direct[j - 2][...]
            piece[pl.ds(pl.multiple_of((1 - plane) * count, 16), extra), :] = forwarded[j - 2]
            weight = piece[...]
        place = where[0] ^ j
        left = jnp.concatenate([keep[0, place], keep[1, place], other[place], other_2[place]], axis=0)
        product = jnp.dot(left, weight, preferred_element_type=jnp.float32)
        total = product if total is None else total + product
    begin = mine.shape[2] - total.shape[1]
    for out, old in zip((mine, theirs), joined):
        out[:, :, :begin] = old[...]
    for i in range(2):
        mine[i, :, begin:] = total[i * ROWS : (i + 1) * ROWS]
        theirs[i, :, begin:] = total[(2 + i) * ROWS : (3 + i) * ROWS]


def project(where, rows_of_x, own, near, direct, forwarded, joined=()):
    width = own.shape[1]
    begin = joined[0].shape[2] if joined else 0
    out = jax.ShapeDtypeStruct((2, ROWS, begin + width), jnp.float32)
    return on_chip(
        project_kernel,
        "project",
        [out, out],
        where,
        *rows_of_x,
        own,
        near,
        *direct,
        forwarded,
        *joined,
        scratch=[pltpu.VMEM((len(direct), own.shape[0], width), jnp.bfloat16)],
    )


def final_kernel(counts, info, gain_ref, q_ref, *refs):
    result, built, sem = refs[-3:]
    states, refs = (refs[:2], refs[2:4]), refs[4:]
    parts = []
    for count in counts:
        mine, here, *away = refs[:count]
        refs = refs[count:]
        for column in range(0, mine.shape[2], HD):
            parts.append((mine, here, away, slice(column, column + HD)))
    slot = lax.broadcasted_iota(jnp.int32, (ROWS, PAIR), 0)
    row = lax.broadcasted_iota(jnp.int32, (ROWS, PAIR), 1) % ROWS
    length = jnp.where(row < RLEN, info[0], info[1])
    base = jnp.where(row < RLEN, 0, RLEN)
    seen = (slot >= base) & (slot <= row) & (slot - base < length)
    live = jnp.where(row - base < length, 1.0, 0.0)[0:1]
    copies = []
    for k, (mine, here, away, part) in enumerate(parts):
        acc_ref, ml_ref = states[k // 2]
        here = mine[0, :, part] + here[0, :, part]
        away = sum(ref[0, :, part] for ref in away)
        first_core = jnp.full(here.shape, info[2]) == 0
        raw = jnp.where(first_core, here, away)
        mean = jnp.mean(raw * raw, axis=1, keepdims=True)
        keys = (raw * lax.rsqrt(mean + 1e-06) * gain_ref[...]).astype(jnp.bfloat16)
        values = jnp.where(first_core, away, here).T.astype(jnp.bfloat16)
        pairs = range(0, SHARED, 2)
        products = [scores_of(keys, pair_queries(q_ref, k * SHARED + g)) for g in pairs]
        for g, scores in zip(pairs, products):
            cols = slice((k % 2 * SHARED + g) * HD, (k % 2 * SHARED + g + 2) * HD)
            scores = jnp.where(seen, scores, HIDDEN)
            before = ml_ref[0:1, cols]
            largest = jnp.maximum(jnp.max(scores, axis=0, keepdims=True), before)
            faded = jnp.exp2((before - largest) * SCALE)
            weights = jnp.exp2((scores - largest) * SCALE)
            total = jnp.sum(weights, axis=0, keepdims=True) + faded * ml_ref[1:2, cols]
            acc = jnp.dot(values, weights.astype(jnp.bfloat16), preferred_element_type=jnp.float32)
            acc = (acc + faded * acc_ref[:, cols]) * (live / total)
            built[k, :, g * HD : (g + 1) * HD] = acc[:, :ROWS].T.astype(jnp.bfloat16)
            built[k, :, (g + 1) * HD : (g + 2) * HD] = acc[:, ROWS:].T.astype(jnp.bfloat16)
        place = result.at[:, pl.ds(k * GROUP, GROUP)]
        copies.append(pltpu.make_async_copy(built.at[k], place, sem.at[k]))
        copies[-1].start()
    for copy in copies:
        copy.wait()


def final_attention(info, gain, query, states, chunks):
    operands = [gain, query]
    operands += [array for state in states for array in state]
    operands += [array for chunk in chunks for array in chunk]
    return pl.pallas_call(
        functools.partial(final_kernel, [len(chunk) for chunk in chunks]),
        in_specs=[SMEM] + [VMEM] * len(operands),
        out_specs=pl.BlockSpec(memory_space=pl.ANY),
        out_shape=jax.ShapeDtypeStruct((ROWS, HQ * HD), jnp.bfloat16),
        scratch_shapes=[pltpu.VMEM((KVH, ROWS, GROUP), jnp.bfloat16), pltpu.SemaphoreType.DMA((KVH,))],
        compiler_params=PARAMS,
        cost_estimate=HINT,
        name="final_attention",
    )(info, *operands)


def xor_swap(array, axis, by):
    return lax.ppermute(array, axis, [(i, i ^ by) for i in range(lax.axis_size(axis))])


def per_device(
    x_resp, queries, prompt_cache, kv_weight, key_gain, prompt_lengths, block_table, resp_lengths
):
    x, query = x_resp[0], queries[0]
    steps = lax.axis_size("z")
    z, y, core = lax.axis_index("z"), lax.axis_index("y"), lax.axis_index("core")
    holder, cycle = lax.axis_index("blk"), lax.axis_size("blk")
    plane = holder % 2
    where = jnp.stack([z, y, core, plane]).astype(jnp.int32)

    tie = lax.optimization_barrier

    got_weight = xor_swap(kv_weight, "core", 1)
    got_x = xor_swap(x, "core", 1)
    caches = [prompt_cache[0]]
    for _ in range(cycle - 1):
        caches.append(lax.ppermute(caches[-1], "blk", [(i, (i + 1) % cycle) for i in range(cycle)]))

    wholes, got_weight = tie((own_rows(where, kv_weight), got_weight))
    whole, far = pack_weight(where, got_weight, wholes)

    def send(far):
        return [xor_swap(far, "z", j) for j in range(2, steps)]

    def forward(i):
        helped, direct = row_split(whole[0].shape[0], i)
        parts = [lax.dynamic_slice_in_dim(p, plane * (direct - helped), helped, axis=0) for p in sent[i]]
        return xor_swap(jnp.stack(parts), "blk", 1)

    sent = [send(far[0])]
    near = [xor_swap(whole[0], "z", 1)]
    got_x, whole[1] = tie((got_x, whole[1]))
    keep, given = pack_rows(where, x, got_x, y, steps)
    other = xor_swap(given, "y", 1)

    block_table, _ = tie((block_table, whole[0]))
    infos = []
    for stride in range(cycle):
        owner = lax.rem(holder + cycle - stride, cycle)
        place = owner * prompt_cache.shape[1]
        listed = lax.dynamic_index_in_dim(block_table[0], place // BLOCK, axis=1, keepdims=False)
        infos.append(jnp.concatenate([place[None], prompt_lengths, listed]).astype(jnp.int32))

    query, _, _ = tie((query, whole[0], given))
    state = prompt_attention(infos[0], query, caches[0], None, 0, KVH)

    def rest(head, state):
        offset = head
        for stride in range(1, cycle):
            state = prompt_attention(infos[stride], query, caches[stride], state, head, 2, offset)
            offset = 0
        return state

    def sums(i, joined=()):
        return project(where, rows_of_x, whole[i], near[i], sent[i], forwarded[i], joined)

    sent[0], state, far[1], whole[1] = tie((sent[0], state, far[1], whole[1]))
    sent.append(send(far[1]))
    near.append(xor_swap(whole[1], "z", 1))
    sent[0], caches = tie((sent[0], caches))
    forwarded = [forward(0)]
    state, other = tie((state, other))
    rows_of_x = [keep, other, xor_swap(other, "core", 1)]
    halves = [rest(0, state)]
    sent[1], near[0], far[2], halves[0], state, rows_of_x[2] = tie((sent[1], near[0], far[2], halves[0], state, rows_of_x[2]))
    sent.append(send(far[2]))
    forwarded[0], sent[1], whole[2] = tie((forwarded[0], sent[1], whole[2]))
    forwarded.append(forward(1))
    near.append(xor_swap(whole[2], "z", 1))

    def owners(mine, theirs):
        there = [xor_swap(theirs[1:], ("y", "core"), 3), xor_swap(mine[1:], "core", 1)]
        return [mine, xor_swap(theirs[:1], "y", 1), *there]

    mine_0, theirs_0 = sums(0)
    sent[2], mine_0 = tie((sent[2], mine_0))
    forwarded.append(forward(2))
    here_0 = xor_swap(theirs_0, "y", 1)
    forwarded[1], mine_0 = tie((forwarded[1], mine_0))
    mine_1, theirs_1 = sums(1)
    forwarded[2], mine_1, theirs_1, here_0 = tie((forwarded[2], mine_1, theirs_1, here_0))
    first = [mine_0, here_0, xor_swap(mine_0[1:] + here_0[1:], "core", 1)]
    mine_2, theirs_2 = sums(2, (mine_1, theirs_1))
    second = owners(mine_2, theirs_2)
    state, mine_2 = tie((state, mine_2))
    halves.append(rest(2, state))
    info = jnp.concatenate([resp_lengths[0], core[None]]).astype(jnp.int32)
    gain = key_gain[None]
    return final_attention(info, gain, query, halves, [first, second])[None]


def solution(mesh):
    groups, blocks = mesh.devices.shape
    split = Mesh(mesh.devices.reshape(groups // 4, 2, 2, blocks), ("z", "y", "core", "blk"))
    fsdp = ("z", "y", "core")
    return jax.shard_map(
        per_device,
        mesh=split,
        in_specs=(
            P(fsdp, "blk", None),
            P(fsdp, "blk", None),
            P(fsdp, "blk", None),
            P(fsdp, None),
            P(),
            P(fsdp),
            P(fsdp, "blk", None),
            P(fsdp, "blk"),
        ),
        out_specs=P(fsdp, "blk", None),
        check_vma=False,
    )
```

```python
import functools

import jax
import jax.numpy as jnp
from jax import lax
from jax.experimental import pallas as pl
from jax.experimental.pallas import tpu as pltpu
from jax.sharding import Mesh
from jax.sharding import PartitionSpec as P

HQ = 32
KVH = 4
HD = 128
SHARED = HQ // KVH
BLOCK = 512
RESP_DEV = 2
RLEN = 64
ROWS = RESP_DEV * RLEN
PAIR = 2 * ROWS
GROUP = SHARED * HD
SCALE = HD ** (-0.5) * 1.4426950408889634
HIDDEN = -1e30
NT = (((1,), (1,)), ((), ()))
HINT = pl.CostEstimate(flops=1024, bytes_accessed=1024, transcendentals=0)

CHUNKS = ((0, 2), (2, 2))


def pair_queries(q_ref, g, extra=None):
    heads = [q_ref[:, i * HD : (i + 1) * HD] for i in (g, g + 1)]
    if extra is not None:
        heads = [jnp.concatenate([head, extra], axis=1) for head in heads]
    return jnp.concatenate(heads, axis=0)


def scores_of(keys, queries):
    return lax.dot_general(keys, queries, NT, preferred_element_type=jnp.float32)


def prompt_kernel(first, info, q_ref, k_ref, v_ref, *refs):
    if first:
        acc_ref, ml_ref = refs
    else:
        old_acc, old_ml, acc_ref, ml_ref = refs
    count = k_ref.shape[0]
    place = info[0] + lax.broadcasted_iota(jnp.int32, (count, HD), 0)
    column = lax.broadcasted_iota(jnp.int32, (count, HD), 1)
    listed = jnp.where(column == 0, info[2], info[3])
    hidden = (column < RESP_DEV) & ((place >= info[1]) | (listed != 1))
    keys = jnp.concatenate([k_ref[...], jnp.where(hidden, HIDDEN, 0.0).astype(jnp.bfloat16)], axis=1)
    owner = lax.broadcasted_iota(jnp.int32, (ROWS, HD), 0) // RLEN
    ours = jnp.where(owner == lax.broadcasted_iota(jnp.int32, (ROWS, HD), 1), 1.0, 0.0).astype(jnp.bfloat16)
    values = v_ref[...].T
    ahead = scores_of(keys, pair_queries(q_ref, 0, ours))
    for g in range(0, SHARED, 2):
        cols = slice(g * HD, (g + 2) * HD)
        scores = ahead
        if g + 2 < SHARED:
            ahead = scores_of(keys, pair_queries(q_ref, g + 2, ours))
        largest = jnp.max(scores, axis=0, keepdims=True)
        if not first:
            before = old_ml[0:1, cols]
            largest = jnp.maximum(largest, before)
            faded = jnp.exp2((before - largest) * SCALE)
        weights = jnp.exp2((scores - largest) * SCALE)
        total = jnp.sum(weights, axis=0, keepdims=True)
        acc = jnp.dot(values, weights.astype(jnp.bfloat16), preferred_element_type=jnp.float32)
        if not first:
            total = total + faded * old_ml[1:2, cols]
            acc = acc + faded * old_acc[:, cols]
        acc_ref[:, cols] = acc
        ml_ref[0:1, cols] = largest
        ml_ref[1:2, cols] = total


def prompt_attention(info, query, cache, state, head, heads, offset=0):
    count = cache.shape[0]
    first = state is None
    wide = pl.BlockSpec((ROWS, GROUP), lambda k, s: (0, head + k))
    turned = pl.BlockSpec((HD, SHARED * ROWS), lambda k, s: (0, k))
    small = pl.BlockSpec((8, SHARED * ROWS), lambda k, s: (0, k))
    specs = [
        wide,
        pl.BlockSpec((count, HD), lambda k, s: (0, head + k)),
        pl.BlockSpec((count, HD), lambda k, s: (0, KVH + head + k)),
    ]
    operands = [query, cache, cache]
    if not first:
        specs += [
            pl.BlockSpec((HD, SHARED * ROWS), lambda k, s: (0, offset + k)),
            pl.BlockSpec((8, SHARED * ROWS), lambda k, s: (0, offset + k)),
        ]
        operands += list(state)
    return pl.pallas_call(
        functools.partial(prompt_kernel, first),
        grid_spec=pltpu.PrefetchScalarGridSpec(
            num_scalar_prefetch=1, grid=(heads,), in_specs=specs, out_specs=[turned, small]
        ),
        out_shape=[
            jax.ShapeDtypeStruct((HD, heads * SHARED * ROWS), jnp.float32),
            jax.ShapeDtypeStruct((8, heads * SHARED * ROWS), jnp.float32),
        ],
        compiler_params=pltpu.CompilerParams(vmem_limit_bytes=32 * 2**20),
        cost_estimate=pl.CostEstimate(
            flops=2**34 if first else 2**33, bytes_accessed=1024, transcendentals=0
        ),
        name="prompt_attention",
    )(info, *operands)


VMEM = pl.BlockSpec(memory_space=pltpu.VMEM)
SMEM = pl.BlockSpec(memory_space=pltpu.SMEM)
PARAMS = pltpu.CompilerParams(vmem_limit_bytes=32 * 2**20)


def on_chip(kernel, name, outs, scalars, *operands, scratch=()):
    return pl.pallas_call(
        kernel,
        in_specs=[SMEM] + [VMEM] * len(operands),
        out_specs=[VMEM] * len(outs),
        out_shape=outs,
        scratch_shapes=scratch,
        compiler_params=PARAMS,
        cost_estimate=HINT,
        name=name,
    )(scalars, *operands)


def pack_rows_kernel(where, own_ref, got_ref, keep, send):
    _, steps, _, part = keep.shape
    for z in range(steps):
        columns = [pl.ds(pl.multiple_of((2 * z + y) * part, 128), part) for y in (where[1], 1 - where[1])]
        keep[0, z] = own_ref[:, columns[0]]
        keep[1, z] = got_ref[:, columns[0]]
        send[z] = own_ref[:, columns[1]]


def pack_rows(where, own, got, y, steps):
    part = own.shape[1] // (2 * steps)
    if part % 128:
        halves = jnp.stack([own, got]).reshape(2, ROWS, steps, 2, part)
        halves = jnp.transpose(halves, (3, 0, 2, 1, 4))
        keep, send = [lax.dynamic_index_in_dim(halves, i, axis=0, keepdims=False) for i in (y, 1 - y)]
        return keep, send[0]
    shapes = [(2, steps, ROWS, part), (steps, ROWS, part)]
    outs = [jax.ShapeDtypeStruct(shape, own.dtype) for shape in shapes]
    return on_chip(pack_rows_kernel, "pack_rows", outs, where, own, got)


def own_rows_kernel(where, weight_ref, *outs):
    rows = weight_ref.shape[0]
    for out, (head, heads) in zip(outs, CHUNKS):
        columns = pl.ds(pl.multiple_of((where[2] * KVH + head) * HD, 128), heads * HD)
        out[pl.ds(pl.multiple_of(where[2] * rows, 16), rows), :] = weight_ref[:, columns]


def own_rows(where, weight):
    outs = [jax.ShapeDtypeStruct((2 * weight.shape[0], heads * HD), weight.dtype) for _, heads in CHUNKS]
    return on_chip(own_rows_kernel, "own_rows", outs, where, weight)


def far_first_kernel(where, whole_ref, got_ref, far):
    rows, core, plane = got_ref.shape[0], where[2], where[3]
    head, heads = CHUNKS[0]

    @pl.when(core == plane)
    def _():
        far[...] = whole_ref[pl.ds(pl.multiple_of(core * rows, 16), rows), :]

    @pl.when(core != plane)
    def _():
        far[...] = got_ref[:, pl.ds(pl.multiple_of((core * KVH + head) * HD, 128), heads * HD)]


def far_first(where, whole, got):
    out = jax.ShapeDtypeStruct((got.shape[0], whole.shape[1]), whole.dtype)
    return on_chip(far_first_kernel, "far_first", [out], where, whole, got)[0]


def pack_weight_kernel(where, got_ref, *refs):
    count = len(CHUNKS)
    wholes, fars = refs[count : 2 * count], refs[2 * count :]
    rows = got_ref.shape[0]
    core, plane = where[2], where[3]
    for whole, (head, heads) in zip(wholes, CHUNKS):
        columns = pl.ds(pl.multiple_of((core * KVH + head) * HD, 128), heads * HD)
        whole[pl.ds(pl.multiple_of((1 - core) * rows, 16), rows), :] = got_ref[:, columns]
    for whole, far in zip(wholes[1:], fars):
        far[...] = whole[pl.ds(pl.multiple_of(plane * rows, 16), rows), :]


def pack_weight(where, got, wholes):
    count = len(CHUNKS)
    outs = [jax.ShapeDtypeStruct(whole.shape, whole.dtype) for whole in wholes]
    outs += [jax.ShapeDtypeStruct((got.shape[0], whole.shape[1]), whole.dtype) for whole in wholes[1:]]
    outs = pl.pallas_call(
        pack_weight_kernel,
        in_specs=[SMEM] + [VMEM] * (1 + count),
        out_specs=[VMEM] * len(outs),
        out_shape=outs,
        input_output_aliases={2 + i: i for i in range(count)},
        compiler_params=PARAMS,
        cost_estimate=HINT,
        name="pack_weight",
    )(where, got, *wholes)
    return list(outs[:count]), list(outs[count:])


def project_kernel(where, keep, other, other_2, own, near, *refs):
    mine, theirs, whole = refs[-3:]
    far = whole.shape[0]
    direct, forwarded = refs[:far], refs[far:-3]
    plane = where[3]
    count, extra = direct[0].shape[0], whole.shape[1] - direct[0].shape[0]
    total = None
    for j in range(2 + far):
        if j == 0:
            weight = own[...]
        elif j == 1:
            weight = near[...]
        else:
            piece = whole.at[j - 2]
            piece[pl.ds(pl.multiple_of(plane * extra, 16), count), :] = direct[j - 2][...]
            rest = forwarded[0][j - 2] if len(forwarded) == 1 else forwarded[j - 2][...]
            piece[pl.ds(pl.multiple_of((1 - plane) * count, 16), extra), :] = rest
            weight = piece[...]
        place = where[0] ^ j
        left = jnp.concatenate([keep[0, place], keep[1, place], other[place], other_2[place]], axis=0)
        product = jnp.dot(left, weight, preferred_element_type=jnp.float32)
        total = product if total is None else total + product
    for i in range(2):
        mine[i] = total[i * ROWS : (i + 1) * ROWS]
        theirs[i] = total[(2 + i) * ROWS : (3 + i) * ROWS]


def project(where, rows_of_x, own, near, direct, forwarded):
    width = own.shape[1]
    out = jax.ShapeDtypeStruct((2, ROWS, width), jnp.float32)
    return on_chip(
        project_kernel,
        "project",
        [out, out],
        where,
        *rows_of_x,
        own,
        near,
        *direct,
        *forwarded,
        scratch=[pltpu.VMEM((len(direct), own.shape[0], width), jnp.bfloat16)],
    )


def final_kernel(chunk, offset, info, gain_ref, q_ref, acc_ref, ml_ref, mine, theirs, there, there_2, *refs):
    result, built, sem = refs[-3:]
    head, heads = chunk
    slot = lax.broadcasted_iota(jnp.int32, (ROWS, PAIR), 0)
    row = lax.broadcasted_iota(jnp.int32, (ROWS, PAIR), 1) % ROWS
    length = jnp.where(row < RLEN, info[0], info[1])
    base = jnp.where(row < RLEN, 0, RLEN)
    seen = (slot >= base) & (slot <= row) & (slot - base < length)
    live = jnp.where(row - base < length, 1.0, 0.0)[0:1]
    copies = []
    for k in range(heads):
        part = slice(k * HD, (k + 1) * HD)
        here = mine[0, :, part] + theirs[0, :, part]
        away = there[0, :, part] + there_2[0, :, part]
        first_core = jnp.full(here.shape, info[2]) == 0
        raw = jnp.where(first_core, here, away)
        mean = jnp.mean(raw * raw, axis=1, keepdims=True)
        keys = (raw * lax.rsqrt(mean + 1e-06) * gain_ref[...]).astype(jnp.bfloat16)
        values = jnp.where(first_core, away, here).T.astype(jnp.bfloat16)
        pairs = range(0, SHARED, 2)
        products = [scores_of(keys, pair_queries(q_ref, (head + k) * SHARED + g)) for g in pairs]
        for g, scores in zip(pairs, products):
            cols = slice(((offset + k) * SHARED + g) * HD, ((offset + k) * SHARED + g + 2) * HD)
            scores = jnp.where(seen, scores, HIDDEN)
            before = ml_ref[0:1, cols]
            largest = jnp.maximum(jnp.max(scores, axis=0, keepdims=True), before)
            faded = jnp.exp2((before - largest) * SCALE)
            weights = jnp.exp2((scores - largest) * SCALE)
            total = jnp.sum(weights, axis=0, keepdims=True) + faded * ml_ref[1:2, cols]
            acc = jnp.dot(values, weights.astype(jnp.bfloat16), preferred_element_type=jnp.float32)
            acc = (acc + faded * acc_ref[:, cols]) * (live / total)
            built[k, :, g * HD : (g + 1) * HD] = acc[:, :ROWS].T.astype(jnp.bfloat16)
            built[k, :, (g + 1) * HD : (g + 2) * HD] = acc[:, ROWS:].T.astype(jnp.bfloat16)
        place = result.at[:, pl.ds((head + k) * GROUP, GROUP)]
        copies.append(pltpu.make_async_copy(built.at[k], place, sem.at[k]))
        copies[-1].start()
    for copy in copies:
        copy.wait()


def final_attention(info, gain, query, state, offset, chunk, mine, theirs, there, result):
    heads = chunk[1]
    operands = [gain, query, *state, mine, theirs, *there]
    specs = [SMEM] + [VMEM] * len(operands)
    aliases = {}
    if result is not None:
        operands.append(result)
        specs.append(pl.BlockSpec(memory_space=pl.ANY))
        aliases = {len(operands): 0}
    return pl.pallas_call(
        functools.partial(final_kernel, chunk, offset),
        in_specs=specs,
        out_specs=pl.BlockSpec(memory_space=pl.ANY),
        out_shape=jax.ShapeDtypeStruct((ROWS, HQ * HD), jnp.bfloat16),
        scratch_shapes=[pltpu.VMEM((heads, ROWS, GROUP), jnp.bfloat16), pltpu.SemaphoreType.DMA((heads,))],
        input_output_aliases=aliases,
        compiler_params=PARAMS,
        cost_estimate=HINT,
        name="final_attention",
    )(info, *operands)


def xor_swap(array, axis, by):
    return lax.ppermute(array, axis, [(i, i ^ by) for i in range(lax.axis_size(axis))])


def per_device(
    x_resp, queries, prompt_cache, kv_weight, key_gain, prompt_lengths, block_table, resp_lengths
):
    x, query = x_resp[0], queries[0]
    steps = lax.axis_size("z")
    z, y, core = lax.axis_index("z"), lax.axis_index("y"), lax.axis_index("core")
    holder, cycle = lax.axis_index("blk"), lax.axis_size("blk")
    plane = holder % 2
    where = jnp.stack([z, y, core, plane]).astype(jnp.int32)

    tie = lax.optimization_barrier

    got_weight = xor_swap(kv_weight, "core", 1)
    got_x = xor_swap(x, "core", 1)
    caches = [prompt_cache[0]]
    for _ in range(cycle - 1):
        caches.append(lax.ppermute(caches[-1], "blk", [(i, (i + 1) % cycle) for i in range(cycle)]))

    wholes, got_weight = tie((own_rows(where, kv_weight), got_weight))
    far = far_first(where, wholes[0], got_weight)
    got_weight, far = tie((got_weight, far))
    whole, rest = pack_weight(where, got_weight, wholes)
    far = [far, *rest]

    def send(far):
        return [xor_swap(far, "z", j) for j in range(2, steps)]

    def forward(i):
        return [xor_swap(jnp.stack(sent[i]), "blk", 1)]

    sent = [send(far[0])]
    near = [xor_swap(whole[0], "z", 1)]
    got_x, whole[1] = tie((got_x, whole[1]))
    keep, given = pack_rows(where, x, got_x, y, steps)
    other = xor_swap(given, "y", 1)

    block_table, _ = tie((block_table, whole[0]))
    infos = []
    for stride in range(cycle):
        owner = lax.rem(holder + cycle - stride, cycle)
        place = owner * prompt_cache.shape[1]
        listed = lax.dynamic_index_in_dim(block_table[0], place // BLOCK, axis=1, keepdims=False)
        infos.append(jnp.concatenate([place[None], prompt_lengths, listed]).astype(jnp.int32))

    query, _, _ = tie((query, whole[0], given))
    state = prompt_attention(infos[0], query, caches[0], None, 0, KVH)

    sent[0], state, far[1], whole[1] = tie((sent[0], state, far[1], whole[1]))
    sent.append(send(far[1]))
    near.append(xor_swap(whole[1], "z", 1))
    sent[0], caches = tie((sent[0], caches))
    forwarded = [forward(0)]
    state, other = tie((state, other))
    rows_of_x = [keep, other, xor_swap(other, "core", 1)]
    for stride in range(1, cycle):
        state = prompt_attention(infos[stride], query, caches[stride], state, 0, KVH)

    def sums(i):
        return project(where, rows_of_x, whole[i], near[i], sent[i], forwarded[i])

    def owners(mine, theirs):
        there = [xor_swap(theirs[1:], ("y", "core"), 3), xor_swap(mine[1:], "core", 1)]
        return xor_swap(theirs[:1], "y", 1), there

    forwarded[0], state = tie((forwarded[0], state))
    mine_0, theirs_0 = sums(0)
    sent[1], mine_0 = tie((sent[1], mine_0))
    forwarded.append(forward(1))
    here_0, there_0 = owners(mine_0, theirs_0)
    forwarded[1], mine_0 = tie((forwarded[1], mine_0))
    mine_1, theirs_1 = sums(1)
    here_0, there_0, mine_1, theirs_1 = tie((here_0, there_0, mine_1, theirs_1))
    here_1, there_1 = owners(mine_1, theirs_1)
    info = jnp.concatenate([resp_lengths[0], core[None]]).astype(jnp.int32)
    gain = key_gain[None]
    result = final_attention(info, gain, query, state, 0, CHUNKS[0], mine_0, here_0, there_0, None)
    result = final_attention(info, gain, query, state, 2, CHUNKS[1], mine_1, here_1, there_1, result)
    return result[None]


def solution(mesh):
    groups, blocks = mesh.devices.shape
    split = Mesh(mesh.devices.reshape(groups // 4, 2, 2, blocks), ("z", "y", "core", "blk"))
    fsdp = ("z", "y", "core")
    return jax.shard_map(
        per_device,
        mesh=split,
        in_specs=(
            P(fsdp, "blk", None),
            P(fsdp, "blk", None),
            P(fsdp, "blk", None),
            P(fsdp, None),
            P(),
            P(fsdp),
            P(fsdp, "blk", None),
            P(fsdp, "blk"),
        ),
        out_specs=P(fsdp, "blk", None),
        check_vma=False,
    )
```

```python
import functools

import jax
import jax.numpy as jnp
from jax import lax
from jax.experimental import pallas as pl
from jax.experimental.pallas import tpu as pltpu
from jax.sharding import Mesh
from jax.sharding import PartitionSpec as P

HQ = 32
KVH = 4
HD = 128
SHARED = HQ // KVH
BLOCK = 512
RESP_DEV = 2
RLEN = 64
ROWS = RESP_DEV * RLEN
PAIR = 2 * ROWS
GROUP = SHARED * HD
SCALE = HD ** (-0.5) * 1.4426950408889634
HIDDEN = -1e30
NT = (((1,), (1,)), ((), ()))
HINT = pl.CostEstimate(flops=1024, bytes_accessed=1024, transcendentals=0)

CHUNKS = ((0, 2), (2, 2))


def pair_queries(q_ref, g, extra=None):
    heads = [q_ref[:, i * HD : (i + 1) * HD] for i in (g, g + 1)]
    if extra is not None:
        heads = [jnp.concatenate([head, extra], axis=1) for head in heads]
    return jnp.concatenate(heads, axis=0)


def scores_of(keys, queries):
    return lax.dot_general(keys, queries, NT, preferred_element_type=jnp.float32)


def prompt_kernel(first, info, q_ref, k_ref, v_ref, *refs):
    if first:
        acc_ref, ml_ref = refs
    else:
        old_acc, old_ml, acc_ref, ml_ref = refs
    count = k_ref.shape[0]
    place = info[0] + lax.broadcasted_iota(jnp.int32, (count, HD), 0)
    column = lax.broadcasted_iota(jnp.int32, (count, HD), 1)
    listed = jnp.where(column == 0, info[2], info[3])
    hidden = (column < RESP_DEV) & ((place >= info[1]) | (listed != 1))
    keys = jnp.concatenate([k_ref[...], jnp.where(hidden, HIDDEN, 0.0).astype(jnp.bfloat16)], axis=1)
    owner = lax.broadcasted_iota(jnp.int32, (ROWS, HD), 0) // RLEN
    ours = jnp.where(owner == lax.broadcasted_iota(jnp.int32, (ROWS, HD), 1), 1.0, 0.0).astype(jnp.bfloat16)
    values = v_ref[...].T
    ahead = scores_of(keys, pair_queries(q_ref, 0, ours))
    for g in range(0, SHARED, 2):
        cols = slice(g * HD, (g + 2) * HD)
        scores = ahead
        if g + 2 < SHARED:
            ahead = scores_of(keys, pair_queries(q_ref, g + 2, ours))
        largest = jnp.max(scores, axis=0, keepdims=True)
        if not first:
            before = old_ml[0:1, cols]
            largest = jnp.maximum(largest, before)
            faded = jnp.exp2((before - largest) * SCALE)
        weights = jnp.exp2((scores - largest) * SCALE)
        total = jnp.sum(weights, axis=0, keepdims=True)
        acc = jnp.dot(values, weights.astype(jnp.bfloat16), preferred_element_type=jnp.float32)
        if not first:
            total = total + faded * old_ml[1:2, cols]
            acc = acc + faded * old_acc[:, cols]
        acc_ref[:, cols] = acc
        ml_ref[0:1, cols] = largest
        ml_ref[1:2, cols] = total


def prompt_attention(info, query, cache, state, head, heads, offset=0):
    count = cache.shape[0]
    first = state is None
    wide = pl.BlockSpec((ROWS, GROUP), lambda k, s: (0, head + k))
    turned = pl.BlockSpec((HD, SHARED * ROWS), lambda k, s: (0, k))
    small = pl.BlockSpec((8, SHARED * ROWS), lambda k, s: (0, k))
    specs = [
        wide,
        pl.BlockSpec((count, HD), lambda k, s: (0, head + k)),
        pl.BlockSpec((count, HD), lambda k, s: (0, KVH + head + k)),
    ]
    operands = [query, cache, cache]
    if not first:
        specs += [
            pl.BlockSpec((HD, SHARED * ROWS), lambda k, s: (0, offset + k)),
            pl.BlockSpec((8, SHARED * ROWS), lambda k, s: (0, offset + k)),
        ]
        operands += list(state)
    return pl.pallas_call(
        functools.partial(prompt_kernel, first),
        grid_spec=pltpu.PrefetchScalarGridSpec(
            num_scalar_prefetch=1, grid=(heads,), in_specs=specs, out_specs=[turned, small]
        ),
        out_shape=[
            jax.ShapeDtypeStruct((HD, heads * SHARED * ROWS), jnp.float32),
            jax.ShapeDtypeStruct((8, heads * SHARED * ROWS), jnp.float32),
        ],
        compiler_params=pltpu.CompilerParams(vmem_limit_bytes=32 * 2**20),
        cost_estimate=pl.CostEstimate(
            flops=2**34 if first else 2**33, bytes_accessed=1024, transcendentals=0
        ),
        name="prompt_attention",
    )(info, *operands)


VMEM = pl.BlockSpec(memory_space=pltpu.VMEM)
SMEM = pl.BlockSpec(memory_space=pltpu.SMEM)
PARAMS = pltpu.CompilerParams(vmem_limit_bytes=32 * 2**20)


def on_chip(kernel, name, outs, scalars, *operands, scratch=()):
    return pl.pallas_call(
        kernel,
        in_specs=[SMEM] + [VMEM] * len(operands),
        out_specs=[VMEM] * len(outs),
        out_shape=outs,
        scratch_shapes=scratch,
        compiler_params=PARAMS,
        cost_estimate=HINT,
        name=name,
    )(scalars, *operands)


def pack_rows_kernel(where, own_ref, got_ref, keep, send):
    _, steps, _, part = keep.shape
    for z in range(steps):
        columns = [pl.ds(pl.multiple_of((2 * z + y) * part, 128), part) for y in (where[1], 1 - where[1])]
        keep[0, z] = own_ref[:, columns[0]]
        keep[1, z] = got_ref[:, columns[0]]
        send[z] = own_ref[:, columns[1]]


def pack_rows(where, own, got, y, steps):
    part = own.shape[1] // (2 * steps)
    if part % 128:
        halves = jnp.stack([own, got]).reshape(2, ROWS, steps, 2, part)
        halves = jnp.transpose(halves, (3, 0, 2, 1, 4))
        keep, send = [lax.dynamic_index_in_dim(halves, i, axis=0, keepdims=False) for i in (y, 1 - y)]
        return keep, send[0]
    shapes = [(2, steps, ROWS, part), (steps, ROWS, part)]
    outs = [jax.ShapeDtypeStruct(shape, own.dtype) for shape in shapes]
    return on_chip(pack_rows_kernel, "pack_rows", outs, where, own, got)


def own_rows_kernel(where, weight_ref, *outs):
    rows = weight_ref.shape[0]
    for out, (head, heads) in zip(outs, CHUNKS):
        columns = pl.ds(pl.multiple_of((where[2] * KVH + head) * HD, 128), heads * HD)
        out[pl.ds(pl.multiple_of(where[2] * rows, 16), rows), :] = weight_ref[:, columns]


def own_rows(where, weight):
    outs = [jax.ShapeDtypeStruct((2 * weight.shape[0], heads * HD), weight.dtype) for _, heads in CHUNKS]
    return on_chip(own_rows_kernel, "own_rows", outs, where, weight)


def far_first_kernel(where, whole_ref, got_ref, far):
    rows, core, plane = got_ref.shape[0], where[2], where[3]
    head, heads = CHUNKS[0]

    @pl.when(core == plane)
    def _():
        far[...] = whole_ref[pl.ds(pl.multiple_of(core * rows, 16), rows), :]

    @pl.when(core != plane)
    def _():
        far[...] = got_ref[:, pl.ds(pl.multiple_of((core * KVH + head) * HD, 128), heads * HD)]


def far_first(where, whole, got):
    out = jax.ShapeDtypeStruct((got.shape[0], whole.shape[1]), whole.dtype)
    return on_chip(far_first_kernel, "far_first", [out], where, whole, got)[0]


def pack_weight_kernel(where, got_ref, *refs):
    count = len(CHUNKS)
    wholes, fars = refs[count : 2 * count], refs[2 * count :]
    rows = got_ref.shape[0]
    core, plane = where[2], where[3]
    for whole, (head, heads) in zip(wholes, CHUNKS):
        columns = pl.ds(pl.multiple_of((core * KVH + head) * HD, 128), heads * HD)
        whole[pl.ds(pl.multiple_of((1 - core) * rows, 16), rows), :] = got_ref[:, columns]
    for whole, far in zip(wholes[1:], fars):
        far[...] = whole[pl.ds(pl.multiple_of(plane * rows, 16), rows), :]


def pack_weight(where, got, wholes):
    count = len(CHUNKS)
    outs = [jax.ShapeDtypeStruct(whole.shape, whole.dtype) for whole in wholes]
    outs += [jax.ShapeDtypeStruct((got.shape[0], whole.shape[1]), whole.dtype) for whole in wholes[1:]]
    outs = pl.pallas_call(
        pack_weight_kernel,
        in_specs=[SMEM] + [VMEM] * (1 + count),
        out_specs=[VMEM] * len(outs),
        out_shape=outs,
        input_output_aliases={2 + i: i for i in range(count)},
        compiler_params=PARAMS,
        cost_estimate=HINT,
        name="pack_weight",
    )(where, got, *wholes)
    return list(outs[:count]), list(outs[count:])


def project_kernel(where, keep, other, other_2, own, near, *refs):
    mine, theirs, whole = refs[-3:]
    far = whole.shape[0]
    direct, forwarded = refs[:far], refs[far:-3]
    plane = where[3]
    count, extra = direct[0].shape[0], whole.shape[1] - direct[0].shape[0]
    total = None
    for j in range(2 + far):
        if j == 0:
            weight = own[...]
        elif j == 1:
            weight = near[...]
        else:
            piece = whole.at[j - 2]
            piece[pl.ds(pl.multiple_of(plane * extra, 16), count), :] = direct[j - 2][...]
            rest = forwarded[0][j - 2] if len(forwarded) == 1 else forwarded[j - 2][...]
            piece[pl.ds(pl.multiple_of((1 - plane) * count, 16), extra), :] = rest
            weight = piece[...]
        place = where[0] ^ j
        left = jnp.concatenate([keep[0, place], keep[1, place], other[place], other_2[place]], axis=0)
        product = jnp.dot(left, weight, preferred_element_type=jnp.float32)
        total = product if total is None else total + product
    for i in range(2):
        mine[i] = total[i * ROWS : (i + 1) * ROWS]
        theirs[i] = total[(2 + i) * ROWS : (3 + i) * ROWS]


def project(where, rows_of_x, own, near, direct, forwarded):
    width = own.shape[1]
    out = jax.ShapeDtypeStruct((2, ROWS, width), jnp.float32)
    return on_chip(
        project_kernel,
        "project",
        [out, out],
        where,
        *rows_of_x,
        own,
        near,
        *direct,
        *forwarded,
        scratch=[pltpu.VMEM((len(direct), own.shape[0], width), jnp.bfloat16)],
    )


def final_kernel(chunk, offset, info, gain_ref, q_ref, acc_ref, ml_ref, mine, theirs, there, there_2, *refs):
    result, built, sem = refs[-3:]
    head, heads = chunk
    slot = lax.broadcasted_iota(jnp.int32, (ROWS, PAIR), 0)
    row = lax.broadcasted_iota(jnp.int32, (ROWS, PAIR), 1) % ROWS
    length = jnp.where(row < RLEN, info[0], info[1])
    base = jnp.where(row < RLEN, 0, RLEN)
    seen = (slot >= base) & (slot <= row) & (slot - base < length)
    live = jnp.where(row - base < length, 1.0, 0.0)[0:1]
    pairs = range(0, SHARED, 2)
    values, products = [], []
    for k in range(heads):
        part = slice(k * HD, (k + 1) * HD)
        here = mine[0, :, part] + theirs[0, :, part]
        away = there[0, :, part] + there_2[0, :, part]
        first_core = jnp.full(here.shape, info[2]) == 0
        raw = jnp.where(first_core, here, away)
        mean = jnp.mean(raw * raw, axis=1, keepdims=True)
        keys = (raw * lax.rsqrt(mean + 1e-06) * gain_ref[...]).astype(jnp.bfloat16)
        values.append(jnp.where(first_core, away, here).T.astype(jnp.bfloat16))
        products.append([scores_of(keys, pair_queries(q_ref, (head + k) * SHARED + g)) for g in pairs])
    copies = []
    for k in range(heads):
        for g, scores in zip(pairs, products[k]):
            cols = slice(((offset + k) * SHARED + g) * HD, ((offset + k) * SHARED + g + 2) * HD)
            scores = jnp.where(seen, scores, HIDDEN)
            before = ml_ref[0:1, cols]
            largest = jnp.maximum(jnp.max(scores, axis=0, keepdims=True), before)
            faded = jnp.exp2((before - largest) * SCALE)
            weights = jnp.exp2((scores - largest) * SCALE)
            total = jnp.sum(weights, axis=0, keepdims=True) + faded * ml_ref[1:2, cols]
            acc = jnp.dot(values[k], weights.astype(jnp.bfloat16), preferred_element_type=jnp.float32)
            acc = (acc + faded * acc_ref[:, cols]) * (live / total)
            built[k, :, g * HD : (g + 1) * HD] = acc[:, :ROWS].T.astype(jnp.bfloat16)
            built[k, :, (g + 1) * HD : (g + 2) * HD] = acc[:, ROWS:].T.astype(jnp.bfloat16)
        place = result.at[:, pl.ds((head + k) * GROUP, GROUP)]
        copies.append(pltpu.make_async_copy(built.at[k], place, sem.at[k]))
        copies[-1].start()
    for copy in copies:
        copy.wait()


def final_attention(info, gain, query, state, offset, chunk, mine, theirs, there, result):
    heads = chunk[1]
    operands = [gain, query, *state, mine, theirs, *there]
    specs = [SMEM] + [VMEM] * len(operands)
    aliases = {}
    if result is not None:
        operands.append(result)
        specs.append(pl.BlockSpec(memory_space=pl.ANY))
        aliases = {len(operands): 0}
    return pl.pallas_call(
        functools.partial(final_kernel, chunk, offset),
        in_specs=specs,
        out_specs=pl.BlockSpec(memory_space=pl.ANY),
        out_shape=jax.ShapeDtypeStruct((ROWS, HQ * HD), jnp.bfloat16),
        scratch_shapes=[pltpu.VMEM((heads, ROWS, GROUP), jnp.bfloat16), pltpu.SemaphoreType.DMA((heads,))],
        input_output_aliases=aliases,
        compiler_params=PARAMS,
        cost_estimate=HINT,
        name="final_attention",
    )(info, *operands)


def xor_swap(array, axis, by):
    return lax.ppermute(array, axis, [(i, i ^ by) for i in range(lax.axis_size(axis))])


def per_device(
    x_resp, queries, prompt_cache, kv_weight, key_gain, prompt_lengths, block_table, resp_lengths
):
    x, query = x_resp[0], queries[0]
    steps = lax.axis_size("z")
    z, y, core = lax.axis_index("z"), lax.axis_index("y"), lax.axis_index("core")
    holder, cycle = lax.axis_index("blk"), lax.axis_size("blk")
    plane = holder % 2
    where = jnp.stack([z, y, core, plane]).astype(jnp.int32)

    tie = lax.optimization_barrier

    got_weight = xor_swap(kv_weight, "core", 1)
    got_x = xor_swap(x, "core", 1)
    caches = [prompt_cache[0]]
    for _ in range(cycle - 1):
        caches.append(lax.ppermute(caches[-1], "blk", [(i, (i + 1) % cycle) for i in range(cycle)]))

    wholes, got_weight = tie((own_rows(where, kv_weight), got_weight))
    far = far_first(where, wholes[0], got_weight)
    got_weight, far = tie((got_weight, far))
    whole, rest = pack_weight(where, got_weight, wholes)
    far = [far, *rest]

    def send(far):
        return [xor_swap(far, "z", j) for j in range(2, steps)]

    def forward(i):
        return [xor_swap(jnp.stack(sent[i]), "blk", 1)]

    sent = [send(far[0])]
    near = [xor_swap(whole[0], "z", 1)]
    got_x, whole[1] = tie((got_x, whole[1]))
    keep, given = pack_rows(where, x, got_x, y, steps)
    other = xor_swap(given, "y", 1)

    block_table, _ = tie((block_table, whole[0]))
    infos = []
    for stride in range(cycle):
        owner = lax.rem(holder + cycle - stride, cycle)
        place = owner * prompt_cache.shape[1]
        listed = lax.dynamic_index_in_dim(block_table[0], place // BLOCK, axis=1, keepdims=False)
        infos.append(jnp.concatenate([place[None], prompt_lengths, listed]).astype(jnp.int32))

    query, _, _ = tie((query, whole[0], given))
    state = prompt_attention(infos[0], query, caches[0], None, 0, KVH)

    sent[0], state, far[1], whole[1] = tie((sent[0], state, far[1], whole[1]))
    sent.append(send(far[1]))
    near.append(xor_swap(whole[1], "z", 1))
    sent[0], caches = tie((sent[0], caches))
    forwarded = [forward(0)]
    state, other = tie((state, other))
    rows_of_x = [keep, other, xor_swap(other, "core", 1)]
    for stride in range(1, cycle):
        state = prompt_attention(infos[stride], query, caches[stride], state, 0, KVH)

    def sums(i):
        return project(where, rows_of_x, whole[i], near[i], sent[i], forwarded[i])

    def owners(mine, theirs):
        there = [xor_swap(theirs[1:], ("y", "core"), 3), xor_swap(mine[1:], "core", 1)]
        return xor_swap(theirs[:1], "y", 1), there

    forwarded[0], state = tie((forwarded[0], state))
    mine_0, theirs_0 = sums(0)
    sent[1], mine_0 = tie((sent[1], mine_0))
    forwarded.append(forward(1))
    here_0, there_0 = owners(mine_0, theirs_0)
    forwarded[1], mine_0 = tie((forwarded[1], mine_0))
    mine_1, theirs_1 = sums(1)
    here_0, there_0, mine_1, theirs_1 = tie((here_0, there_0, mine_1, theirs_1))
    here_1, there_1 = owners(mine_1, theirs_1)
    info = jnp.concatenate([resp_lengths[0], core[None]]).astype(jnp.int32)
    gain = key_gain[None]
    result = final_attention(info, gain, query, state, 0, CHUNKS[0], mine_0, here_0, there_0, None)
    result = final_attention(info, gain, query, state, 2, CHUNKS[1], mine_1, here_1, there_1, result)
    return result[None]


def solution(mesh):
    groups, blocks = mesh.devices.shape
    split = Mesh(mesh.devices.reshape(groups // 4, 2, 2, blocks), ("z", "y", "core", "blk"))
    fsdp = ("z", "y", "core")
    return jax.shard_map(
        per_device,
        mesh=split,
        in_specs=(
            P(fsdp, "blk", None),
            P(fsdp, "blk", None),
            P(fsdp, "blk", None),
            P(fsdp, None),
            P(),
            P(fsdp),
            P(fsdp, "blk", None),
            P(fsdp, "blk"),
        ),
        out_specs=P(fsdp, "blk", None),
        check_vma=False,
    )
```

```python
import functools

import jax
import jax.numpy as jnp
from jax import lax
from jax.experimental import pallas as pl
from jax.experimental.pallas import tpu as pltpu
from jax.sharding import Mesh
from jax.sharding import PartitionSpec as P

HQ = 32
KVH = 4
HD = 128
SHARED = HQ // KVH
BLOCK = 512
RESP_DEV = 2
RLEN = 64
ROWS = RESP_DEV * RLEN
PAIR = 2 * ROWS
GROUP = SHARED * HD
SCALE = HD ** (-0.5) * 1.4426950408889634
HIDDEN = -1e30
NT = (((1,), (1,)), ((), ()))
HINT = pl.CostEstimate(flops=1024, bytes_accessed=1024, transcendentals=0)

CHUNKS = ((0, 2), (2, 2))


def pair_queries(q_ref, g, extra=None):
    heads = [q_ref[:, i * HD : (i + 1) * HD] for i in (g, g + 1)]
    if extra is not None:
        heads = [jnp.concatenate([head, extra], axis=1) for head in heads]
    return jnp.concatenate(heads, axis=0)


def scores_of(keys, queries):
    return lax.dot_general(keys, queries, NT, preferred_element_type=jnp.float32)


def prompt_kernel(first, info, q_ref, k_ref, v_ref, *refs):
    if first:
        acc_ref, ml_ref = refs
    else:
        old_acc, old_ml, acc_ref, ml_ref = refs
    count = k_ref.shape[0]
    place = info[0] + lax.broadcasted_iota(jnp.int32, (count, HD), 0)
    column = lax.broadcasted_iota(jnp.int32, (count, HD), 1)
    listed = jnp.where(column == 0, info[2], info[3])
    hidden = (column < RESP_DEV) & ((place >= info[1]) | (listed != 1))
    keys = jnp.concatenate([k_ref[...], jnp.where(hidden, HIDDEN, 0.0).astype(jnp.bfloat16)], axis=1)
    owner = lax.broadcasted_iota(jnp.int32, (ROWS, HD), 0) // RLEN
    ours = jnp.where(owner == lax.broadcasted_iota(jnp.int32, (ROWS, HD), 1), 1.0, 0.0).astype(jnp.bfloat16)
    values = v_ref[...].T
    ahead = scores_of(keys, pair_queries(q_ref, 0, ours))
    for g in range(0, SHARED, 2):
        cols = slice(g * HD, (g + 2) * HD)
        scores = ahead
        if g + 2 < SHARED:
            ahead = scores_of(keys, pair_queries(q_ref, g + 2, ours))
        largest = jnp.max(scores, axis=0, keepdims=True)
        if not first:
            before = old_ml[0:1, cols]
            largest = jnp.maximum(largest, before)
            faded = jnp.exp2((before - largest) * SCALE)
        weights = jnp.exp2((scores - largest) * SCALE)
        total = jnp.sum(weights, axis=0, keepdims=True)
        acc = jnp.dot(values, weights.astype(jnp.bfloat16), preferred_element_type=jnp.float32)
        if not first:
            total = total + faded * old_ml[1:2, cols]
            acc = acc + faded * old_acc[:, cols]
        acc_ref[:, cols] = acc
        ml_ref[0:1, cols] = largest
        ml_ref[1:2, cols] = total


def prompt_attention(info, query, cache, state, head, heads, offset=0):
    count = cache.shape[0]
    first = state is None
    wide = pl.BlockSpec((ROWS, GROUP), lambda k, s: (0, head + k))
    turned = pl.BlockSpec((HD, SHARED * ROWS), lambda k, s: (0, k))
    small = pl.BlockSpec((8, SHARED * ROWS), lambda k, s: (0, k))
    specs = [
        wide,
        pl.BlockSpec((count, HD), lambda k, s: (0, head + k)),
        pl.BlockSpec((count, HD), lambda k, s: (0, KVH + head + k)),
    ]
    operands = [query, cache, cache]
    if not first:
        specs += [
            pl.BlockSpec((HD, SHARED * ROWS), lambda k, s: (0, offset + k)),
            pl.BlockSpec((8, SHARED * ROWS), lambda k, s: (0, offset + k)),
        ]
        operands += list(state)
    return pl.pallas_call(
        functools.partial(prompt_kernel, first),
        grid_spec=pltpu.PrefetchScalarGridSpec(
            num_scalar_prefetch=1, grid=(heads,), in_specs=specs, out_specs=[turned, small]
        ),
        out_shape=[
            jax.ShapeDtypeStruct((HD, heads * SHARED * ROWS), jnp.float32),
            jax.ShapeDtypeStruct((8, heads * SHARED * ROWS), jnp.float32),
        ],
        compiler_params=pltpu.CompilerParams(vmem_limit_bytes=32 * 2**20),
        cost_estimate=pl.CostEstimate(
            flops=2**34 if first else 2**33, bytes_accessed=1024, transcendentals=0
        ),
        name="prompt_attention",
    )(info, *operands)


VMEM = pl.BlockSpec(memory_space=pltpu.VMEM)
SMEM = pl.BlockSpec(memory_space=pltpu.SMEM)
PARAMS = pltpu.CompilerParams(vmem_limit_bytes=32 * 2**20)


def on_chip(kernel, name, outs, scalars, *operands, scratch=()):
    return pl.pallas_call(
        kernel,
        in_specs=[SMEM] + [VMEM] * len(operands),
        out_specs=[VMEM] * len(outs),
        out_shape=outs,
        scratch_shapes=scratch,
        compiler_params=PARAMS,
        cost_estimate=HINT,
        name=name,
    )(scalars, *operands)


def pack_rows_kernel(where, own_ref, got_ref, keep, send):
    _, steps, _, part = keep.shape
    for z in range(steps):
        columns = [pl.ds(pl.multiple_of((2 * z + y) * part, 128), part) for y in (where[1], 1 - where[1])]
        keep[0, z] = own_ref[:, columns[0]]
        keep[1, z] = got_ref[:, columns[0]]
        send[z] = own_ref[:, columns[1]]


def pack_rows(where, own, got, y, steps):
    part = own.shape[1] // (2 * steps)
    if part % 128:
        halves = jnp.stack([own, got]).reshape(2, ROWS, steps, 2, part)
        halves = jnp.transpose(halves, (3, 0, 2, 1, 4))
        keep, send = [lax.dynamic_index_in_dim(halves, i, axis=0, keepdims=False) for i in (y, 1 - y)]
        return keep, send[0]
    shapes = [(2, steps, ROWS, part), (steps, ROWS, part)]
    outs = [jax.ShapeDtypeStruct(shape, own.dtype) for shape in shapes]
    return on_chip(pack_rows_kernel, "pack_rows", outs, where, own, got)


def own_rows_kernel(where, weight_ref, *outs):
    rows = weight_ref.shape[0]
    for out, (head, heads) in zip(outs, CHUNKS):
        columns = pl.ds(pl.multiple_of((where[2] * KVH + head) * HD, 128), heads * HD)
        out[pl.ds(pl.multiple_of(where[2] * rows, 16), rows), :] = weight_ref[:, columns]


def own_rows(where, weight):
    outs = [jax.ShapeDtypeStruct((2 * weight.shape[0], heads * HD), weight.dtype) for _, heads in CHUNKS]
    return on_chip(own_rows_kernel, "own_rows", outs, where, weight)


def far_first_kernel(where, whole_ref, got_ref, far):
    rows, core, plane = got_ref.shape[0], where[2], where[3]
    head, heads = CHUNKS[0]

    @pl.when(core == plane)
    def _():
        far[...] = whole_ref[pl.ds(pl.multiple_of(core * rows, 16), rows), :]

    @pl.when(core != plane)
    def _():
        far[...] = got_ref[:, pl.ds(pl.multiple_of((core * KVH + head) * HD, 128), heads * HD)]


def far_first(where, whole, got):
    out = jax.ShapeDtypeStruct((got.shape[0], whole.shape[1]), whole.dtype)
    return on_chip(far_first_kernel, "far_first", [out], where, whole, got)[0]


def pack_weight_kernel(where, got_ref, *refs):
    count = len(CHUNKS)
    wholes, fars = refs[count : 2 * count], refs[2 * count :]
    rows = got_ref.shape[0]
    core, plane = where[2], where[3]
    for whole, (head, heads) in zip(wholes, CHUNKS):
        columns = pl.ds(pl.multiple_of((core * KVH + head) * HD, 128), heads * HD)
        whole[pl.ds(pl.multiple_of((1 - core) * rows, 16), rows), :] = got_ref[:, columns]
    for whole, far in zip(wholes[1:], fars):
        far[...] = whole[pl.ds(pl.multiple_of(plane * rows, 16), rows), :]


def pack_weight(where, got, wholes):
    count = len(CHUNKS)
    outs = [jax.ShapeDtypeStruct(whole.shape, whole.dtype) for whole in wholes]
    outs += [jax.ShapeDtypeStruct((got.shape[0], whole.shape[1]), whole.dtype) for whole in wholes[1:]]
    outs = pl.pallas_call(
        pack_weight_kernel,
        in_specs=[SMEM] + [VMEM] * (1 + count),
        out_specs=[VMEM] * len(outs),
        out_shape=outs,
        input_output_aliases={2 + i: i for i in range(count)},
        compiler_params=PARAMS,
        cost_estimate=HINT,
        name="pack_weight",
    )(where, got, *wholes)
    return list(outs[:count]), list(outs[count:])


def project_kernel(where, keep, other, other_2, own, near, *refs):
    mine, theirs, whole = refs[-3:]
    far = whole.shape[0]
    direct, forwarded = refs[:far], refs[far:-3]
    plane = where[3]
    count, extra = direct[0].shape[0], whole.shape[1] - direct[0].shape[0]
    total = None
    for j in range(2 + far):
        if j == 0:
            weight = own[...]
        elif j == 1:
            weight = near[...]
        else:
            piece = whole.at[j - 2]
            piece[pl.ds(pl.multiple_of(plane * extra, 16), count), :] = direct[j - 2][...]
            rest = forwarded[0][j - 2] if len(forwarded) == 1 else forwarded[j - 2][...]
            piece[pl.ds(pl.multiple_of((1 - plane) * count, 16), extra), :] = rest
            weight = piece[...]
        place = where[0] ^ j
        left = jnp.concatenate([keep[0, place], keep[1, place], other[place], other_2[place]], axis=0)
        product = jnp.dot(left, weight, preferred_element_type=jnp.float32)
        total = product if total is None else total + product
    for i in range(2):
        mine[i] = total[i * ROWS : (i + 1) * ROWS]
        theirs[i] = total[(2 + i) * ROWS : (3 + i) * ROWS]


def project(where, rows_of_x, own, near, direct, forwarded):
    width = own.shape[1]
    out = jax.ShapeDtypeStruct((2, ROWS, width), jnp.float32)
    return on_chip(
        project_kernel,
        "project",
        [out, out],
        where,
        *rows_of_x,
        own,
        near,
        *direct,
        *forwarded,
        scratch=[pltpu.VMEM((len(direct), own.shape[0], width), jnp.bfloat16)],
    )


def final_kernel(chunk, offset, info, gain_ref, q_ref, acc_ref, ml_ref, mine, theirs, there, there_2, *refs):
    result, built, sem = refs[-3:]
    head, heads = chunk
    slot = lax.broadcasted_iota(jnp.int32, (ROWS, PAIR), 0)
    row = lax.broadcasted_iota(jnp.int32, (ROWS, PAIR), 1) % ROWS
    length = jnp.where(row < RLEN, info[0], info[1])
    base = jnp.where(row < RLEN, 0, RLEN)
    seen = (slot >= base) & (slot <= row) & (slot - base < length)
    live = jnp.where(row - base < length, 1.0, 0.0)[0:1]
    pairs = range(0, SHARED, 2)
    values, products = [], []
    for k in range(heads):
        part = slice(k * HD, (k + 1) * HD)
        here = mine[0, :, part] + theirs[0, :, part]
        away = there[0, :, part] + there_2[0, :, part]
        first_core = jnp.full(here.shape, info[2]) == 0
        raw = jnp.where(first_core, here, away)
        mean = jnp.mean(raw * raw, axis=1, keepdims=True)
        keys = (raw * lax.rsqrt(mean + 1e-06) * gain_ref[...]).astype(jnp.bfloat16)
        values.append(jnp.where(first_core, away, here).T.astype(jnp.bfloat16))
        products.append([scores_of(keys, pair_queries(q_ref, (head + k) * SHARED + g)) for g in pairs])
    copies = []
    for k in range(heads):
        for g, scores in zip(pairs, products[k]):
            cols = slice(((offset + k) * SHARED + g) * HD, ((offset + k) * SHARED + g + 2) * HD)
            scores = jnp.where(seen, scores, HIDDEN)
            before = ml_ref[0:1, cols]
            largest = jnp.maximum(jnp.max(scores, axis=0, keepdims=True), before)
            faded = jnp.exp2((before - largest) * SCALE)
            weights = jnp.exp2((scores - largest) * SCALE)
            total = jnp.sum(weights, axis=0, keepdims=True) + faded * ml_ref[1:2, cols]
            acc = jnp.dot(values[k], weights.astype(jnp.bfloat16), preferred_element_type=jnp.float32)
            acc = (acc + faded * acc_ref[:, cols]) * (live / total)
            built[k, :, g * HD : (g + 1) * HD] = acc[:, :ROWS].T.astype(jnp.bfloat16)
            built[k, :, (g + 1) * HD : (g + 2) * HD] = acc[:, ROWS:].T.astype(jnp.bfloat16)
        place = result.at[:, pl.ds((head + k) * GROUP, GROUP)]
        copies.append(pltpu.make_async_copy(built.at[k], place, sem.at[k]))
        copies[-1].start()
    for copy in copies:
        copy.wait()


def final_attention(info, gain, query, state, offset, chunk, mine, theirs, there, result):
    heads = chunk[1]
    operands = [gain, query, *state, mine, theirs, *there]
    specs = [SMEM] + [VMEM] * len(operands)
    aliases = {}
    if result is not None:
        operands.append(result)
        specs.append(pl.BlockSpec(memory_space=pl.ANY))
        aliases = {len(operands): 0}
    return pl.pallas_call(
        functools.partial(final_kernel, chunk, offset),
        in_specs=specs,
        out_specs=pl.BlockSpec(memory_space=pl.ANY),
        out_shape=jax.ShapeDtypeStruct((ROWS, HQ * HD), jnp.bfloat16),
        scratch_shapes=[pltpu.VMEM((heads, ROWS, GROUP), jnp.bfloat16), pltpu.SemaphoreType.DMA((heads,))],
        input_output_aliases=aliases,
        compiler_params=PARAMS,
        cost_estimate=HINT,
        name="final_attention",
    )(info, *operands)


def xor_swap(array, axis, by):
    return lax.ppermute(array, axis, [(i, i ^ by) for i in range(lax.axis_size(axis))])


def per_device(
    x_resp, queries, prompt_cache, kv_weight, key_gain, prompt_lengths, block_table, resp_lengths
):
    x, query = x_resp[0], queries[0]
    steps = lax.axis_size("z")
    z, y, core = lax.axis_index("z"), lax.axis_index("y"), lax.axis_index("core")
    holder, cycle = lax.axis_index("blk"), lax.axis_size("blk")
    plane = holder % 2
    where = jnp.stack([z, y, core, plane]).astype(jnp.int32)

    tie = lax.optimization_barrier

    got_weight = xor_swap(kv_weight, "core", 1)
    caches = [prompt_cache[0]]
    for _ in range(cycle - 1):
        caches.append(lax.ppermute(caches[-1], "blk", [(i, (i + 1) % cycle) for i in range(cycle)]))

    wholes, got_weight = tie((own_rows(where, kv_weight), got_weight))
    far = far_first(where, wholes[0], got_weight)
    got_weight, far, own_x = tie((got_weight, far, x))
    got_x = xor_swap(own_x, "core", 1)
    whole, rest = pack_weight(where, got_weight, wholes)
    far = [far, *rest]

    def send(far):
        return [xor_swap(far, "z", j) for j in range(2, steps)]

    def forward(i):
        return [xor_swap(jnp.stack(sent[i]), "blk", 1)]

    sent = [send(far[0])]
    near = [xor_swap(whole[0], "z", 1)]
    got_x, whole[1] = tie((got_x, whole[1]))
    keep, given = pack_rows(where, x, got_x, y, steps)
    other = xor_swap(given, "y", 1)

    block_table, _ = tie((block_table, whole[0]))
    infos = []
    for stride in range(cycle):
        owner = lax.rem(holder + cycle - stride, cycle)
        place = owner * prompt_cache.shape[1]
        listed = lax.dynamic_index_in_dim(block_table[0], place // BLOCK, axis=1, keepdims=False)
        infos.append(jnp.concatenate([place[None], prompt_lengths, listed]).astype(jnp.int32))

    query, _, _ = tie((query, whole[0], given))
    state = prompt_attention(infos[0], query, caches[0], None, 0, KVH)

    sent[0], state, far[1], whole[1] = tie((sent[0], state, far[1], whole[1]))
    sent.append(send(far[1]))
    near.append(xor_swap(whole[1], "z", 1))
    sent[0], caches = tie((sent[0], caches))
    forwarded = [forward(0)]
    state, other = tie((state, other))
    rows_of_x = [keep, other, xor_swap(other, "core", 1)]
    for stride in range(1, cycle):
        state = prompt_attention(infos[stride], query, caches[stride], state, 0, KVH)

    def sums(i):
        return project(where, rows_of_x, whole[i], near[i], sent[i], forwarded[i])

    def owners(mine, theirs):
        there = [xor_swap(theirs[1:], ("y", "core"), 3), xor_swap(mine[1:], "core", 1)]
        return xor_swap(theirs[:1], "y", 1), there

    forwarded[0], state = tie((forwarded[0], state))
    mine_0, theirs_0 = sums(0)
    sent[1], mine_0 = tie((sent[1], mine_0))
    forwarded.append(forward(1))
    here_0, there_0 = owners(mine_0, theirs_0)
    forwarded[1], mine_0 = tie((forwarded[1], mine_0))
    mine_1, theirs_1 = sums(1)
    here_0, there_0, mine_1, theirs_1 = tie((here_0, there_0, mine_1, theirs_1))
    here_1, there_1 = owners(mine_1, theirs_1)
    info = jnp.concatenate([resp_lengths[0], core[None]]).astype(jnp.int32)
    gain = key_gain[None]
    result = final_attention(info, gain, query, state, 0, CHUNKS[0], mine_0, here_0, there_0, None)
    result = final_attention(info, gain, query, state, 2, CHUNKS[1], mine_1, here_1, there_1, result)
    return result[None]


def solution(mesh):
    groups, blocks = mesh.devices.shape
    split = Mesh(mesh.devices.reshape(groups // 4, 2, 2, blocks), ("z", "y", "core", "blk"))
    fsdp = ("z", "y", "core")
    return jax.shard_map(
        per_device,
        mesh=split,
        in_specs=(
            P(fsdp, "blk", None),
            P(fsdp, "blk", None),
            P(fsdp, "blk", None),
            P(fsdp, None),
            P(),
            P(fsdp),
            P(fsdp, "blk", None),
            P(fsdp, "blk"),
        ),
        out_specs=P(fsdp, "blk", None),
        check_vma=False,
    )
```

```python
import functools

import jax
import jax.numpy as jnp
from jax import lax
from jax.experimental import pallas as pl
from jax.experimental.pallas import tpu as pltpu
from jax.sharding import Mesh
from jax.sharding import PartitionSpec as P

HQ = 32
KVH = 4
HD = 128
SHARED = HQ // KVH
BLOCK = 512
RESP_DEV = 2
RLEN = 64
ROWS = RESP_DEV * RLEN
PAIR = 2 * ROWS
GROUP = SHARED * HD
SCALE = HD ** (-0.5) * 1.4426950408889634
HIDDEN = -1e30
NT = (((1,), (1,)), ((), ()))
HINT = pl.CostEstimate(flops=1024, bytes_accessed=1024, transcendentals=0)

CHUNKS = ((0, 2), (2, 2))


def pair_queries(q_ref, g, extra=None):
    heads = [q_ref[:, i * HD : (i + 1) * HD] for i in (g, g + 1)]
    if extra is not None:
        heads = [jnp.concatenate([head, extra], axis=1) for head in heads]
    return jnp.concatenate(heads, axis=0)


def scores_of(keys, queries):
    return lax.dot_general(keys, queries, NT, preferred_element_type=jnp.float32)


def prompt_kernel(first, info, q_ref, k_ref, v_ref, *refs):
    if first:
        acc_ref, ml_ref = refs
    else:
        old_acc, old_ml, acc_ref, ml_ref = refs
    count = k_ref.shape[0]
    place = info[0] + lax.broadcasted_iota(jnp.int32, (count, HD), 0)
    column = lax.broadcasted_iota(jnp.int32, (count, HD), 1)
    listed = jnp.where(column == 0, info[2], info[3])
    hidden = (column < RESP_DEV) & ((place >= info[1]) | (listed != 1))
    keys = jnp.concatenate([k_ref[...], jnp.where(hidden, HIDDEN, 0.0).astype(jnp.bfloat16)], axis=1)
    owner = lax.broadcasted_iota(jnp.int32, (ROWS, HD), 0) // RLEN
    ours = jnp.where(owner == lax.broadcasted_iota(jnp.int32, (ROWS, HD), 1), 1.0, 0.0).astype(jnp.bfloat16)
    values = v_ref[...].T
    ahead = scores_of(keys, pair_queries(q_ref, 0, ours))
    for g in range(0, SHARED, 2):
        cols = slice(g * HD, (g + 2) * HD)
        scores = ahead
        if g + 2 < SHARED:
            ahead = scores_of(keys, pair_queries(q_ref, g + 2, ours))
        largest = jnp.max(scores, axis=0, keepdims=True)
        if not first:
            before = old_ml[0:1, cols]
            largest = jnp.maximum(largest, before)
            faded = jnp.exp2((before - largest) * SCALE)
        weights = jnp.exp2((scores - largest) * SCALE)
        total = jnp.sum(weights, axis=0, keepdims=True)
        acc = jnp.dot(values, weights.astype(jnp.bfloat16), preferred_element_type=jnp.float32)
        if not first:
            total = total + faded * old_ml[1:2, cols]
            acc = acc + faded * old_acc[:, cols]
        acc_ref[:, cols] = acc
        ml_ref[0:1, cols] = largest
        ml_ref[1:2, cols] = total


def prompt_attention(info, query, cache, state, head, heads, offset=0):
    count = cache.shape[0]
    first = state is None
    wide = pl.BlockSpec((ROWS, GROUP), lambda k, s: (0, head + k))
    turned = pl.BlockSpec((HD, SHARED * ROWS), lambda k, s: (0, k))
    small = pl.BlockSpec((8, SHARED * ROWS), lambda k, s: (0, k))
    specs = [
        wide,
        pl.BlockSpec((count, HD), lambda k, s: (0, head + k)),
        pl.BlockSpec((count, HD), lambda k, s: (0, KVH + head + k)),
    ]
    operands = [query, cache, cache]
    if not first:
        specs += [
            pl.BlockSpec((HD, SHARED * ROWS), lambda k, s: (0, offset + k)),
            pl.BlockSpec((8, SHARED * ROWS), lambda k, s: (0, offset + k)),
        ]
        operands += list(state)
    return pl.pallas_call(
        functools.partial(prompt_kernel, first),
        grid_spec=pltpu.PrefetchScalarGridSpec(
            num_scalar_prefetch=1, grid=(heads,), in_specs=specs, out_specs=[turned, small]
        ),
        out_shape=[
            jax.ShapeDtypeStruct((HD, heads * SHARED * ROWS), jnp.float32),
            jax.ShapeDtypeStruct((8, heads * SHARED * ROWS), jnp.float32),
        ],
        compiler_params=pltpu.CompilerParams(vmem_limit_bytes=32 * 2**20),
        cost_estimate=pl.CostEstimate(
            flops=2**34 if first else 2**33, bytes_accessed=1024, transcendentals=0
        ),
        name="prompt_attention",
    )(info, *operands)


VMEM = pl.BlockSpec(memory_space=pltpu.VMEM)
SMEM = pl.BlockSpec(memory_space=pltpu.SMEM)
PARAMS = pltpu.CompilerParams(vmem_limit_bytes=32 * 2**20)


def on_chip(kernel, name, outs, scalars, *operands, scratch=()):
    return pl.pallas_call(
        kernel,
        in_specs=[SMEM] + [VMEM] * len(operands),
        out_specs=[VMEM] * len(outs),
        out_shape=outs,
        scratch_shapes=scratch,
        compiler_params=PARAMS,
        cost_estimate=HINT,
        name=name,
    )(scalars, *operands)


def pack_rows_kernel(where, own_ref, got_ref, keep, send):
    _, steps, _, part = keep.shape
    for z in range(steps):
        columns = [pl.ds(pl.multiple_of((2 * z + y) * part, 128), part) for y in (where[1], 1 - where[1])]
        keep[0, z] = own_ref[:, columns[0]]
        keep[1, z] = got_ref[:, columns[0]]
        send[z] = own_ref[:, columns[1]]


def pack_rows(where, own, got, y, steps):
    part = own.shape[1] // (2 * steps)
    if part % 128:
        halves = jnp.stack([own, got]).reshape(2, ROWS, steps, 2, part)
        halves = jnp.transpose(halves, (3, 0, 2, 1, 4))
        keep, send = [lax.dynamic_index_in_dim(halves, i, axis=0, keepdims=False) for i in (y, 1 - y)]
        return keep, send[0]
    shapes = [(2, steps, ROWS, part), (steps, ROWS, part)]
    outs = [jax.ShapeDtypeStruct(shape, own.dtype) for shape in shapes]
    return on_chip(pack_rows_kernel, "pack_rows", outs, where, own, got)


def own_rows_kernel(where, weight_ref, *outs):
    rows = weight_ref.shape[0]
    for out, (head, heads) in zip(outs, CHUNKS):
        columns = pl.ds(pl.multiple_of((where[2] * KVH + head) * HD, 128), heads * HD)
        out[pl.ds(pl.multiple_of(where[2] * rows, 16), rows), :] = weight_ref[:, columns]


def own_rows(where, weight):
    outs = [jax.ShapeDtypeStruct((2 * weight.shape[0], heads * HD), weight.dtype) for _, heads in CHUNKS]
    return on_chip(own_rows_kernel, "own_rows", outs, where, weight)


def far_first_kernel(where, whole_ref, got_ref, far):
    rows, core, plane = got_ref.shape[0], where[2], where[3]
    head, heads = CHUNKS[0]

    @pl.when(core == plane)
    def _():
        far[...] = whole_ref[pl.ds(pl.multiple_of(core * rows, 16), rows), :]

    @pl.when(core != plane)
    def _():
        far[...] = got_ref[:, pl.ds(pl.multiple_of((core * KVH + head) * HD, 128), heads * HD)]


def far_first(where, whole, got):
    out = jax.ShapeDtypeStruct((got.shape[0], whole.shape[1]), whole.dtype)
    return on_chip(far_first_kernel, "far_first", [out], where, whole, got)[0]


def pack_weight_kernel(where, got_ref, *refs):
    count = len(CHUNKS)
    wholes, fars = refs[count : 2 * count], refs[2 * count :]
    rows = got_ref.shape[0]
    core, plane = where[2], where[3]
    for whole, (head, heads) in zip(wholes, CHUNKS):
        columns = pl.ds(pl.multiple_of((core * KVH + head) * HD, 128), heads * HD)
        whole[pl.ds(pl.multiple_of((1 - core) * rows, 16), rows), :] = got_ref[:, columns]
    for whole, far in zip(wholes[1:], fars):
        far[...] = whole[pl.ds(pl.multiple_of(plane * rows, 16), rows), :]


def pack_weight(where, got, wholes):
    count = len(CHUNKS)
    outs = [jax.ShapeDtypeStruct(whole.shape, whole.dtype) for whole in wholes]
    outs += [jax.ShapeDtypeStruct((got.shape[0], whole.shape[1]), whole.dtype) for whole in wholes[1:]]
    outs = pl.pallas_call(
        pack_weight_kernel,
        in_specs=[SMEM] + [VMEM] * (1 + count),
        out_specs=[VMEM] * len(outs),
        out_shape=outs,
        input_output_aliases={2 + i: i for i in range(count)},
        compiler_params=PARAMS,
        cost_estimate=HINT,
        name="pack_weight",
    )(where, got, *wholes)
    return list(outs[:count]), list(outs[count:])


def project_kernel(counts, where, keep, other, other_2, *refs):
    parts = []
    for count in counts:
        parts.append(refs[:count])
        refs = refs[count:]
    near, direct, forwarded, before = parts
    mine, theirs = refs[:2]
    plane = where[3]
    weights = list(enumerate(near))
    for i, piece in enumerate(direct):
        count, rows = piece.shape[0], refs[2].shape[1]
        whole = refs[2].at[i]
        whole[pl.ds(pl.multiple_of(plane * (rows - count), 16), count), :] = piece[...]
        whole[pl.ds(pl.multiple_of((1 - plane) * count, 16), rows - count), :] = forwarded[0][i]
        weights.append((2 + i, whole))
    total = None
    if before:
        total = jnp.concatenate([ref[i] for ref in before for i in range(2)], axis=0)
    for j, weight in weights:
        place = where[0] ^ j
        left = jnp.concatenate([keep[0, place], keep[1, place], other[place], other_2[place]], axis=0)
        product = jnp.dot(left, weight[...], preferred_element_type=jnp.float32)
        total = product if total is None else total + product
    for i in range(2):
        mine[i] = total[i * ROWS : (i + 1) * ROWS]
        theirs[i] = total[(2 + i) * ROWS : (3 + i) * ROWS]


def project(where, rows_of_x, near=(), direct=(), forwarded=(), before=()):
    width = (near or direct)[0].shape[1]
    out = jax.ShapeDtypeStruct((2, ROWS, width), jnp.float32)
    scratch = []
    if direct:
        rows = direct[0].shape[0] + forwarded[0].shape[1]
        scratch.append(pltpu.VMEM((len(direct), rows, width), jnp.bfloat16))
    operands = [near, direct, forwarded, before]
    return on_chip(
        functools.partial(project_kernel, [len(part) for part in operands]),
        "project",
        [out, out],
        where,
        *rows_of_x,
        *[array for part in operands for array in part],
        scratch=scratch,
    )


def final_kernel(chunk, offset, info, gain_ref, q_ref, acc_ref, ml_ref, mine, theirs, there, there_2, *refs):
    result, built, sem = refs[-3:]
    head, heads = chunk
    slot = lax.broadcasted_iota(jnp.int32, (ROWS, PAIR), 0)
    row = lax.broadcasted_iota(jnp.int32, (ROWS, PAIR), 1) % ROWS
    length = jnp.where(row < RLEN, info[0], info[1])
    base = jnp.where(row < RLEN, 0, RLEN)
    seen = (slot >= base) & (slot <= row) & (slot - base < length)
    live = jnp.where(row - base < length, 1.0, 0.0)[0:1]
    copies = []
    for k in range(heads):
        part = slice(k * HD, (k + 1) * HD)
        here = mine[0, :, part] + theirs[0, :, part]
        away = there[0, :, part] + there_2[0, :, part]
        first_core = jnp.full(here.shape, info[2]) == 0
        raw = jnp.where(first_core, here, away)
        mean = jnp.mean(raw * raw, axis=1, keepdims=True)
        keys = (raw * lax.rsqrt(mean + 1e-06) * gain_ref[...]).astype(jnp.bfloat16)
        values = jnp.where(first_core, away, here).T.astype(jnp.bfloat16)
        pairs = range(0, SHARED, 2)
        products = [scores_of(keys, pair_queries(q_ref, (head + k) * SHARED + g)) for g in pairs]
        for g, scores in zip(pairs, products):
            cols = slice(((offset + k) * SHARED + g) * HD, ((offset + k) * SHARED + g + 2) * HD)
            scores = jnp.where(seen, scores, HIDDEN)
            before = ml_ref[0:1, cols]
            largest = jnp.maximum(jnp.max(scores, axis=0, keepdims=True), before)
            faded = jnp.exp2((before - largest) * SCALE)
            weights = jnp.exp2((scores - largest) * SCALE)
            total = jnp.sum(weights, axis=0, keepdims=True) + faded * ml_ref[1:2, cols]
            acc = jnp.dot(values, weights.astype(jnp.bfloat16), preferred_element_type=jnp.float32)
            acc = (acc + faded * acc_ref[:, cols]) * (live / total)
            built[k, :, g * HD : (g + 1) * HD] = acc[:, :ROWS].T.astype(jnp.bfloat16)
            built[k, :, (g + 1) * HD : (g + 2) * HD] = acc[:, ROWS:].T.astype(jnp.bfloat16)
        place = result.at[:, pl.ds((head + k) * GROUP, GROUP)]
        copies.append(pltpu.make_async_copy(built.at[k], place, sem.at[k]))
        copies[-1].start()
    for copy in copies:
        copy.wait()


def final_attention(info, gain, query, state, offset, chunk, mine, theirs, there, result):
    heads = chunk[1]
    operands = [gain, query, *state, mine, theirs, *there]
    specs = [SMEM] + [VMEM] * len(operands)
    aliases = {}
    if result is not None:
        operands.append(result)
        specs.append(pl.BlockSpec(memory_space=pl.ANY))
        aliases = {len(operands): 0}
    return pl.pallas_call(
        functools.partial(final_kernel, chunk, offset),
        in_specs=specs,
        out_specs=pl.BlockSpec(memory_space=pl.ANY),
        out_shape=jax.ShapeDtypeStruct((ROWS, HQ * HD), jnp.bfloat16),
        scratch_shapes=[pltpu.VMEM((heads, ROWS, GROUP), jnp.bfloat16), pltpu.SemaphoreType.DMA((heads,))],
        input_output_aliases=aliases,
        compiler_params=PARAMS,
        cost_estimate=HINT,
        name="final_attention",
    )(info, *operands)


def xor_swap(array, axis, by):
    return lax.ppermute(array, axis, [(i, i ^ by) for i in range(lax.axis_size(axis))])


def per_device(
    x_resp, queries, prompt_cache, kv_weight, key_gain, prompt_lengths, block_table, resp_lengths
):
    x, query = x_resp[0], queries[0]
    steps = lax.axis_size("z")
    z, y, core = lax.axis_index("z"), lax.axis_index("y"), lax.axis_index("core")
    holder, cycle = lax.axis_index("blk"), lax.axis_size("blk")
    plane = holder % 2
    where = jnp.stack([z, y, core, plane]).astype(jnp.int32)

    tie = lax.optimization_barrier

    got_weight = xor_swap(kv_weight, "core", 1)
    got_x = xor_swap(x, "core", 1)
    caches = [prompt_cache[0]]
    for _ in range(cycle - 1):
        caches.append(lax.ppermute(caches[-1], "blk", [(i, (i + 1) % cycle) for i in range(cycle)]))

    wholes, got_weight = tie((own_rows(where, kv_weight), got_weight))
    far = far_first(where, wholes[0], got_weight)
    got_weight, far = tie((got_weight, far))
    whole, rest = pack_weight(where, got_weight, wholes)
    far = [far, *rest]

    def send(far):
        return [xor_swap(far, "z", j) for j in range(2, steps)]

    def forward(stacked):
        return [xor_swap(stacked, "blk", 1)]

    sent = [send(far[0])]
    near = [xor_swap(whole[0], "z", 1)]
    got_x, whole[1] = tie((got_x, whole[1]))
    keep, given = pack_rows(where, x, got_x, y, steps)
    other = xor_swap(given, "y", 1)

    block_table, _ = tie((block_table, whole[0]))
    infos = []
    for stride in range(cycle):
        owner = lax.rem(holder + cycle - stride, cycle)
        place = owner * prompt_cache.shape[1]
        listed = lax.dynamic_index_in_dim(block_table[0], place // BLOCK, axis=1, keepdims=False)
        infos.append(jnp.concatenate([place[None], prompt_lengths, listed]).astype(jnp.int32))

    query, _, _ = tie((query, whole[0], given))
    state = prompt_attention(infos[0], query, caches[0], None, 0, KVH)

    sent[0], state, far[1], whole[1] = tie((sent[0], state, far[1], whole[1]))
    sent.append(send(far[1]))
    near.append(xor_swap(whole[1], "z", 1))
    sent[0], caches = tie((sent[0], caches))
    forwarded = [forward(jnp.stack(sent[0]))]
    state, other = tie((state, other))
    rows_of_x = [keep, other, xor_swap(other, "core", 1)]
    for stride in range(1, cycle):
        state = prompt_attention(infos[stride], query, caches[stride], state, 0, KVH)

    def owners(mine, theirs):
        there = [xor_swap(theirs[1:], ("y", "core"), 3), xor_swap(mine[1:], "core", 1)]
        return xor_swap(theirs[:1], "y", 1), there

    forwarded[0], state = tie((forwarded[0], state))
    mine_0, theirs_0 = project(where, rows_of_x, [whole[0], near[0]], sent[0], forwarded[0])
    sent[1], mine_0 = tie((sent[1], mine_0))
    stacked, mine_0, theirs_0 = tie((jnp.stack(sent[1]), mine_0, theirs_0))
    forwarded.append(forward(stacked))
    here_0, there_0 = owners(mine_0, theirs_0)
    early = project(where, rows_of_x, [whole[1], near[1]])
    forwarded[1], early = tie((forwarded[1], early))
    mine_1, theirs_1 = project(where, rows_of_x, (), sent[1], forwarded[1], early)
    here_0, there_0, mine_1, theirs_1 = tie((here_0, there_0, mine_1, theirs_1))
    here_1, there_1 = owners(mine_1, theirs_1)
    info = jnp.concatenate([resp_lengths[0], core[None]]).astype(jnp.int32)
    gain = key_gain[None]
    result = final_attention(info, gain, query, state, 0, CHUNKS[0], mine_0, here_0, there_0, None)
    result = final_attention(info, gain, query, state, 2, CHUNKS[1], mine_1, here_1, there_1, result)
    return result[None]


def solution(mesh):
    groups, blocks = mesh.devices.shape
    split = Mesh(mesh.devices.reshape(groups // 4, 2, 2, blocks), ("z", "y", "core", "blk"))
    fsdp = ("z", "y", "core")
    return jax.shard_map(
        per_device,
        mesh=split,
        in_specs=(
            P(fsdp, "blk", None),
            P(fsdp, "blk", None),
            P(fsdp, "blk", None),
            P(fsdp, None),
            P(),
            P(fsdp),
            P(fsdp, "blk", None),
            P(fsdp, "blk"),
        ),
        out_specs=P(fsdp, "blk", None),
        check_vma=False,
    )
```
